256 devices in a mesh: req: 8 (over y, z_hi), tp: 32 (over z_lo, x, core).
Axes of the slice: x: 4, y: 4, z: 8 (z_hi: 2, z_lo: 4; z = z_hi * 4 + z_lo), core: 2. Of those that a mesh axis runs over, the one named last changes fastest.
Arguments:
- tokens: bfloat16 [2048, 4096], P('req', 'tp'), parts along dimension 0, may hold values from -6 to 6
- gate_codes: int32 [1024, 28672], P(None, 'tp'), may hold values from -32768 to 32767, as said below
- gate_scales: bfloat16 [32, 28672], P(None, 'tp'), as said below
- up_codes: int32 [1024, 28672], P(None, 'tp'), may hold values from -32768 to 32767, as said below
- up_scales: bfloat16 [32, 28672], P(None, 'tp'), as said below
- local_factor: bfloat16 [896, 896], replicated, may hold values from -0.1875 to 0.1875
- down_codes: int32 [7168, 4096], P('tp'), may hold values from -32768 to 32767, as said below
- down_scales: bfloat16 [224, 4096], P('tp'), as said below
Outputs:
- mixed: bfloat16 [2048, 4096], P('req', 'tp'), parts along dimension 0
The draws below stay inside these ranges and needn't reach their ends.
There are 8 independent parts, one for each index of `req`. The reference program is written for one: setup_inputs(seed, part) draws one part's arguments, and reference() takes and returns one part's arrays. A program takes and returns all parts, laid end to end along the dimension named above; an argument that names none is the same for every part. Nothing has to cross between parts.
Inputs may be any that keep to these rules, and one draw needn't show every extreme that they name: `gate_codes`: each word plus 32768 holds four 4-bit codes; field k (bits 4k to 4k+3, read as 0 to 15) of word r belongs to weight row 4r+k. `up_codes`: each word plus 32768 holds four 4-bit codes; field k of word r belongs to weight row 4r+k. `down_codes`: each word plus 32768 holds four 4-bit codes; field k of word r belongs to hidden unit 4r+k. `gate_scales`: Positive. `up_scales`: Positive. `down_scales`: Positive.
All inputs are finite; a program needn't handle non-finite values.
Results may differ from the reference program's by a relative error of at most 0.034.
Values may be sent and summed in bfloat16 or wider, within the bound.
A program may use at most 128 MiB of HBM per device.

```python
import math
import jax
import jax.numpy as jnp
from jax import lax

D = 4096
FF = 28672
TOK = 256
GROUP = 128
LOCAL = 896
N_TP = 32


def code_words(key, row_count, col_count):
    words = jax.random.randint(key, (row_count, col_count), -32768, 32768, dtype=jnp.int32)
    words = words.at[0, 0].set(-32768)
    return words.at[row_count - 1, col_count - 1].set(32767)


def group_scales(key, row_count, col_count, fan_in, lowest, highest):
    spread = jax.random.uniform(key, (row_count, col_count), jnp.float32, jnp.log(lowest), jnp.log(highest))
    return (jnp.exp(spread) * 0.22 / jnp.sqrt(jnp.float32(fan_in))).astype(jnp.bfloat16)


def draw_gate_codes(key, part):
    key = jax.random.fold_in(key, 3)
    return code_words(key, D // 4, FF)


def draw_up_codes(key, part):
    key = jax.random.fold_in(key, 5)
    return code_words(key, D // 4, FF)


def draw_down_codes(key, part):
    key = jax.random.fold_in(key, 7)
    return code_words(key, FF // 4, D)


def draw_gate_scales(key, part):
    key = jax.random.fold_in(key, 11)
    return group_scales(key, D // GROUP, FF, D, 0.5, 2.0)


def draw_up_scales(key, part):
    key = jax.random.fold_in(key, 13)
    return group_scales(key, D // GROUP, FF, D, 0.5, 2.0)


def draw_down_scales(key, part):
    key = jax.random.fold_in(key, 17)
    return group_scales(key, FF // GROUP, D, FF, 0.5, 2.0)


def steps_of(key, shape, shards, smallest, top_value):
    factor_of, own = 1.0, jax.random.fold_in(key, 6)
    for position, blocks in shards:
        steps = jnp.exp(jax.random.uniform(jax.random.fold_in(own, position), (blocks,), jnp.float32, smallest / len(shards), top_value / len(shards)))
        factor_of = factor_of * jnp.repeat(steps, shape[position] // blocks).reshape([-1 if axis == position else 1 for axis in range(len(shape))])
    return factor_of


def noise(own_key, dims, scale, reach, shards=(), held_as=jnp.bfloat16):
    gain = steps_of(own_key, dims, shards, -0.22, 0.18) if shards else 1.0
    drawn = jax.random.normal(own_key, dims, jnp.float32) * scale * gain
    return jnp.minimum(jnp.maximum(drawn, -reach), reach).astype(held_as)


def setup_inputs(seed: int = 0, part: int = 0) -> dict:
    key_list = jax.random.split(jax.random.key(seed), 9)
    own_keys = jax.random.split(jax.random.fold_in(key_list[8], part), 9)
    return {
        "tokens": noise(own_keys[0], (TOK, D), 1.0, 6.0, ((1, 32),)),
        "gate_codes": draw_gate_codes(jax.random.fold_in(key_list[8], 71), part),
        "gate_scales": draw_gate_scales(jax.random.fold_in(key_list[8], 71), part),
        "up_codes": draw_up_codes(jax.random.fold_in(key_list[8], 71), part),
        "up_scales": draw_up_scales(jax.random.fold_in(key_list[8], 71), part),
        "local_factor": noise(key_list[5], (LOCAL, LOCAL), LOCAL ** -0.5, 0.1875),
        "down_codes": draw_down_codes(jax.random.fold_in(key_list[8], 71), part),
        "down_scales": draw_down_scales(jax.random.fold_in(key_list[8], 71), part),
    }


def unpack(packed, scales):
    row_count = packed.shape[0] * 4
    col_count = packed.shape[1]
    groups = scales.shape[0]
    shifts = (4 * jnp.arange(4, dtype=jnp.int32))[None, :, None]
    lifted = packed + 32768
    nibble = jnp.bitwise_and(jnp.right_shift(lifted[:, None, :], shifts), 15)
    values = (nibble - 8).astype(jnp.float32).reshape(groups, row_count // groups, col_count)
    values = values * scales.astype(jnp.float32)[:, None, :]
    return values.reshape(row_count, col_count).astype(jnp.bfloat16)

def sylvester(devices):
    ordinal = jnp.arange(devices, dtype=jnp.int32)
    anded = jnp.bitwise_and(ordinal[:, None], ordinal[None, :])
    parity = jnp.zeros((devices, devices), jnp.int32)
    for section in range(devices.bit_length() - 1):
        parity = parity + jnp.bitwise_and(jnp.right_shift(anded, section), 1)
    return (1 - 2 * (parity % 2)).astype(jnp.float32)

def reference(tokens, gate_codes, gate_scales, up_codes, up_scales, local_factor, down_codes, down_scales):
    devices = N_TP
    unit_count = FF // devices
    scale_rows = unit_count // GROUP

    def first_pass(block):
        offset = block * unit_count
        w_gate = unpack(lax.dynamic_slice_in_dim(gate_codes, offset, unit_count, 1), lax.dynamic_slice_in_dim(gate_scales, offset, unit_count, 1))
        w_up = unpack(lax.dynamic_slice_in_dim(up_codes, offset, unit_count, 1), lax.dynamic_slice_in_dim(up_scales, offset, unit_count, 1))
        gate = jnp.dot(tokens, w_gate, preferred_element_type=jnp.float32)
        upward = jnp.dot(tokens, w_up, preferred_element_type=jnp.float32)
        hidden = (jax.nn.silu(gate) * upward).astype(jnp.bfloat16)
        return jnp.dot(hidden, local_factor, preferred_element_type=jnp.float32).astype(jnp.bfloat16)
    blocked = lax.map(first_pass, jnp.arange(devices, dtype=jnp.int32))
    sign_table = sylvester(devices)
    rotated = jnp.einsum('bc,ctj->btj', sign_table, blocked.astype(jnp.float32), precision=lax.Precision.HIGHEST)
    rotated = (rotated * (1.0 / math.sqrt(devices))).astype(jnp.bfloat16)

    def down_pass(summed, block):
        w_down = unpack(lax.dynamic_slice_in_dim(down_codes, block * (unit_count // 4), unit_count // 4, 0), lax.dynamic_slice_in_dim(down_scales, block * scale_rows, scale_rows, 0))
        partial_value = jnp.dot(rotated[block], w_down, preferred_element_type=jnp.float32).astype(jnp.bfloat16)
        partial_value = lax.optimization_barrier(partial_value)
        return (summed + partial_value.astype(jnp.float32), None)
    summed, _ = lax.scan(down_pass, jnp.zeros((tokens.shape[0], D), jnp.float32), jnp.arange(devices, dtype=jnp.int32))
    return summed.astype(jnp.bfloat16)
```

```python
import functools
import math

import jax
import jax.numpy as jnp
from jax import lax
from jax.experimental import pallas as pl
from jax.experimental.pallas import tpu as pltpu
from jax.sharding import PartitionSpec as P

MESH = pl.DeviceIdType.MESH
TP = 32
ROWS = 256
UNITS = 896
TILES = 7
CHUNKS = 2
CR = ROWS // CHUNKS
HALF = CR // 2
F32 = jnp.float32
BF16 = jnp.bfloat16


def field_order():
    source = lax.broadcasted_iota(jnp.int32, (128, 128), 0)
    target = lax.broadcasted_iota(jnp.int32, (128, 128), 1)
    return jnp.where(target == (source % 4) * 32 + source // 4, 1.0, 0.0).astype(BF16)


def decode(words, scale):
    flipped = jnp.bitwise_xor(words, 0x0888)
    planes = []
    for field in range(4):
        if field == 3:
            value = jnp.right_shift(words, 12)
        else:
            value = jnp.right_shift(jnp.left_shift(flipped, 28 - 4 * field), 28)
        scaled = value.astype(F32).reshape(4, 8, 128) * scale
        planes.append(scaled.reshape(32, 128).astype(BF16))
    return planes


def kernel(
    tok_in, gate_scales, up_scales, down_scales, gate_hbm, up_hbm, factor_hbm, down_hbm, out_ref,
    gate_codes, up_codes, down_codes, factor, tok, w_both, w_down, ordered, gate_f32, up_f32, down_f32,
    hidden, blocked, had_in, had_out, rotated, part, core_in, sums, first_in, second_in, mixed, z_in,
    load_sem, tok_send, tok_recv, a_send, a_recv, b_send, b_recv, c_send, c_recv, x_send, x_recv,
    y_send, y_recv, z_send, z_recv,
):
    me = lax.axis_index("tp")
    z, x, c = me // 8, (me // 2) % 4, me % 2
    other = me + 1 - 2 * c
    right = z * 8 + ((x + 1) % 4) * 2 + c
    left = z * 8 + ((x + 3) % 4) * 2 + c
    z_of = [z, z + 1 - 2 * (z % 2), (z + 2) % 4, 3 - z]

    barrier = pltpu.get_barrier_semaphore()

    @pl.loop(1, TP)
    def _(step):
        pl.semaphore_signal(barrier, inc=1, device_id={"tp": (me + step) % TP}, device_id_type=MESH)

    loads = []
    for piece in range(4):
        rows = pl.ds(256 * piece, 256)
        loads.append([
            pltpu.make_async_copy(gate_hbm.at[rows], gate_codes.at[rows], load_sem.at[piece]),
            pltpu.make_async_copy(up_hbm.at[rows], up_codes.at[rows], load_sem.at[4 + piece]),
        ])
        for copy in loads[-1]:
            copy.start()
    factor_load = pltpu.make_async_copy(factor_hbm, factor, load_sem.at[8])
    factor_load.start()
    down_load = pltpu.make_async_copy(down_hbm, down_codes, load_sem.at[9])
    down_load.start()

    order = field_order()

    def columns(block):
        return pl.ds(pl.multiple_of(block * 128, 128), 128)

    tok[:, columns(me)] = jnp.dot(tok_in[...], order, preferred_element_type=F32).astype(BF16)
    for source, spread, groups in ((gate_scales, gate_f32, 32), (up_scales, up_f32, 32), (down_scales, down_f32, 7)):
        scales = source[...].astype(F32)
        for group in range(groups):
            spread[group] = jnp.broadcast_to(scales[group : group + 1], spread.shape[1:])

    pl.semaphore_wait(barrier, TP - 1)

    waiting = []

    def pass_on(block, device, row=0, count=ROWS):
        where = tok.at[pl.ds(row, count), columns(block)]
        copy = pltpu.make_async_remote_copy(
            src_ref=where, dst_ref=where, send_sem=tok_send.at[len(waiting)],
            recv_sem=tok_recv.at[block, 1 if row else 0],
            device_id={"tp": device}, device_id_type=MESH,
        )
        copy.start()
        waiting.append(copy)

    def arrived(block, row=0, count=ROWS):
        where = tok.at[pl.ds(row, count), columns(block)]
        pltpu.make_async_copy(where, where, tok_recv.at[block, 1 if row else 0]).wait()

    def at(near, shift):
        return z_of[near] * 8 + ((x + shift) % 4) * 2 + c

    def from_z(near):
        if near:
            arrived(at(near, 0))
        else:
            for peer in (1, 2, 3):
                pass_on(me, at(peer, 0))
        pass_on(at(near, 0), right)
        pass_on(at(near, 0), left)
        pass_on(at(near, 0), other)

    def from_x(near):
        block = at(near, 3)
        arrived(block)
        pass_on(block, right, 0, ROWS // 2)
        pass_on(block, other)
        block = at(near, 1)
        arrived(block)
        pass_on(block, left, ROWS // 2, ROWS // 2)
        pass_on(block, other)

    def from_far(near):
        block = at(near, 2)
        arrived(block, 0, ROWS // 2)
        arrived(block, ROWS // 2, ROWS // 2)
        pass_on(block, other)

    def decode_piece(piece):
        for copy in loads[piece]:
            copy.wait()

        @pl.loop(8 * piece, 8 * piece + 8)
        def _(group):
            rows = pl.ds(pl.multiple_of(group * 32, 32), 32)
            for tile in range(TILES):
                cols = pl.ds(128 * tile, 128)
                for place, codes, scales in ((0, gate_codes, gate_f32), (128, up_codes, up_f32)):
                    planes = decode(codes[rows, cols], scales[group, :, cols])
                    for field, plane in enumerate(planes):
                        to = pl.ds(pl.multiple_of(group * 128 + 32 * field, 32), 32)
                        w_both[tile, to, pl.ds(place, 128)] = plane

    from_z(0)
    decode_piece(0)
    from_z(1)
    from_x(0)
    decode_piece(1)
    from_z(2)
    from_x(1)
    decode_piece(2)
    from_z(3)
    from_x(2)
    from_far(0)
    decode_piece(3)
    factor_load.wait()
    for tile in range(TILES):
        cols = pl.ds(128 * tile, 128)
        ordered[:, cols] = jnp.dot(factor[:, cols], order, preferred_element_type=F32).astype(BF16)
    from_x(3)
    from_far(1)
    from_far(2)
    from_far(3)

    @pl.loop(0, TP // 2)
    def _(chip):
        arrived(chip * 2 + 1 - c)

    @pl.loop(0, TILES)
    def _(tile):
        both = jnp.dot(tok[...], w_both[tile], preferred_element_type=F32)
        gate, up = both[:, :128], both[:, 128:]
        value = gate / (1.0 + jnp.exp(-gate)) * up
        hidden[:, pl.ds(pl.multiple_of(tile * 128, 128), 128)] = value.astype(BF16)

    def share(device):
        dz, dx, dc = device // 8, (device // 2) % 4, device % 2
        return dz * 2 + dx // 2, (dx % 2) * 2 + dc

    row_tile, quarter = share(me)
    wide = quarter < 3
    narrow = quarter == 3

    def two(start):
        return pl.ds(pl.multiple_of(start * 256, 256), 256)

    last = pl.ds(768, 128)

    def scatter(chunk):
        value = jnp.dot(hidden[pl.ds(chunk * CR, CR), :], ordered[...], preferred_element_type=F32)
        blocked[chunk] = value.astype(BF16).reshape(CR // 16, 16, UNITS)

        @pl.loop(1, TP)
        def _(step):
            device = (me + step) % TP
            tile, part_of = share(device)

            @pl.when(part_of < 3)
            def _():
                pltpu.make_async_remote_copy(
                    src_ref=blocked.at[chunk, tile, :, two(part_of)], dst_ref=had_in.at[chunk, me],
                    send_sem=a_send.at[chunk], recv_sem=a_recv.at[chunk],
                    device_id={"tp": device}, device_id_type=MESH,
                ).start()

            @pl.when(part_of == 3)
            def _():
                pltpu.make_async_remote_copy(
                    src_ref=blocked.at[chunk, tile, :, last], dst_ref=had_in.at[chunk, me, :, pl.ds(0, 128)],
                    send_sem=a_send.at[chunk], recv_sem=a_recv.at[chunk],
                    device_id={"tp": device}, device_id_type=MESH,
                ).start()

        @pl.when(wide)
        def _():
            pltpu.make_async_copy(
                blocked.at[chunk, row_tile, :, two(quarter)], had_in.at[chunk, me], a_recv.at[chunk]
            ).start()

        @pl.when(narrow)
        def _():
            pltpu.make_async_copy(
                blocked.at[chunk, row_tile, :, last], had_in.at[chunk, me, :, pl.ds(0, 128)], a_recv.at[chunk]
            ).start()

    def rotate(chunk):
        def combine(tile):
            cols = pl.ds(128 * tile, 128)
            held = [had_in[chunk, source, :, cols].astype(F32) for source in range(TP)]
            apart = 1
            while apart < TP:
                held = [
                    held[i - apart] - held[i] if i & apart else held[i] + held[i + apart]
                    for i in range(TP)
                ]
                apart *= 2
            for target in range(TP):
                had_out[chunk, target, :, cols] = (held[target] * (1.0 / math.sqrt(TP))).astype(BF16)

        def give(out_cols, to_cols):
            @pl.loop(1, TP)
            def _(step):
                device = (me + step) % TP
                pltpu.make_async_remote_copy(
                    src_ref=had_out.at[chunk, device, :, out_cols], dst_ref=rotated.at[chunk, row_tile, :, to_cols],
                    send_sem=b_send.at[chunk], recv_sem=b_recv.at[chunk],
                    device_id={"tp": device}, device_id_type=MESH,
                ).start()

            pltpu.make_async_copy(
                had_out.at[chunk, me, :, out_cols], rotated.at[chunk, row_tile, :, to_cols], b_recv.at[chunk]
            ).start()

        @pl.when(wide)
        def _():
            everything = had_in.at[chunk]
            pltpu.make_async_copy(everything, everything, a_recv.at[chunk]).wait()
            combine(0)
            combine(1)
            give(pl.ds(0, 256), two(quarter))

        @pl.when(narrow)
        def _():
            everything = had_in.at[chunk, :, :, pl.ds(0, 128)]
            pltpu.make_async_copy(everything, everything, a_recv.at[chunk]).wait()
            combine(0)
            give(pl.ds(0, 128), last)

    def remote(src, dst, send, recv, device):
        copy = pltpu.make_async_remote_copy(
            src_ref=src, dst_ref=dst, send_sem=send, recv_sem=recv,
            device_id={"tp": device}, device_id_type=MESH,
        )
        copy.start()
        waiting.append(copy)
        return copy

    x_of = [x, (x + 1) % 4, (x + 2) % 4, (x + 3) % 4]
    from_core = {}

    def down(chunk):
        everything = rotated.at[chunk]
        pltpu.make_async_copy(everything, everything, b_recv.at[chunk]).wait()
        for shift in (2, 1, 3, 0):
            place = x_of[shift]

            @pl.loop(0, 4)
            def _(z_to):
                both = jnp.dot(
                    rotated[chunk].reshape(CR, UNITS), w_down[z_to * 4 + place], preferred_element_type=F32
                ).astype(BF16)
                part[chunk, 0, place, z_to] = both[:, :128]
                part[chunk, 1, place, z_to] = both[:, 128:]

            from_core[chunk, shift] = remote(
                part.at[chunk, 1 - c, place], core_in.at[chunk, shift],
                c_send.at[chunk, shift], c_recv.at[chunk, shift], other,
            )

    top, bottom = pl.ds(0, HALF), pl.ds(HALF, HALF)

    def join(chunk, shift, rows):
        return part[chunk, c, x_of[shift], :, rows].astype(F32) + core_in[chunk, shift, :, rows].astype(F32)

    x_copies = {}

    def x_first(chunk):
        from_core[chunk, 2].wait_recv()
        sums[chunk, 2] = join(chunk, 2, pl.ds(0, CR)).astype(BF16)
        x_copies[chunk, "r1"] = remote(
            sums.at[chunk, 2, :, top], first_in.at[chunk, 0], x_send.at[chunk, 0], x_recv.at[chunk, 0], right
        )
        x_copies[chunk, "l1"] = remote(
            sums.at[chunk, 2, :, bottom], first_in.at[chunk, 1], x_send.at[chunk, 1], x_recv.at[chunk, 1], left
        )
        from_core[chunk, 1].wait_recv()
        sums[chunk, 1, :, bottom] = join(chunk, 1, bottom).astype(BF16)
        from_core[chunk, 3].wait_recv()
        sums[chunk, 3, :, top] = join(chunk, 3, top).astype(BF16)

    def x_second(chunk):
        x_copies[chunk, "r1"].wait_recv()
        sums[chunk, 1, :, top] = (join(chunk, 1, top) + first_in[chunk, 0].astype(F32)).astype(BF16)
        x_copies[chunk, "r2"] = remote(
            sums.at[chunk, 1], second_in.at[chunk, 0], y_send.at[chunk, 0], y_recv.at[chunk, 0], right
        )
        x_copies[chunk, "l1"].wait_recv()
        sums[chunk, 3, :, bottom] = (join(chunk, 3, bottom) + first_in[chunk, 1].astype(F32)).astype(BF16)
        x_copies[chunk, "l2"] = remote(
            sums.at[chunk, 3], second_in.at[chunk, 1], y_send.at[chunk, 1], y_recv.at[chunk, 1], left
        )
        from_core[chunk, 0].wait_recv()

    z_copies = {}

    def z_first(chunk):
        x_copies[chunk, "r2"].wait_recv()
        x_copies[chunk, "l2"].wait_recv()
        for near in (3, 2, 1, 0):
            to = z_of[near]
            value = (
                part[chunk, c, x, to].astype(F32) + core_in[chunk, 0, to].astype(F32)
                + second_in[chunk, 0, to].astype(F32) + second_in[chunk, 1, to].astype(F32)
            )
            mixed[chunk, near] = value.astype(BF16)
            if near:
                z_copies[chunk, near] = remote(
                    mixed.at[chunk, near], z_in.at[chunk, near], z_send.at[chunk, near], z_recv.at[chunk, near],
                    to * 8 + x * 2 + c,
                )

    def z_last(chunk):
        total = mixed[chunk, 0].astype(F32)
        for near in (1, 2, 3):
            z_copies[chunk, near].wait_recv()
            total = total + z_in[chunk, near].astype(F32)
        out_ref[pl.ds(chunk * CR, CR), :] = total.astype(BF16)

    scatter(0)
    scatter(1)

    down_load.wait()

    @pl.loop(0, 16)
    def _(chip):
        for group in range(TILES):
            for side in range(2):
                cols = pl.ds(pl.multiple_of(chip * 256 + 128 * side, 128), 128)
                planes = decode(down_codes[pl.ds(32 * group, 32), cols], down_f32[group, :, cols])
                for field, plane in enumerate(planes):
                    w_down[chip, pl.ds(128 * group + 32 * field, 32), pl.ds(128 * side, 128)] = plane

    rotate(0)
    rotate(1)
    down(0)
    x_first(0)
    down(1)
    x_second(0)
    x_first(1)
    z_first(0)
    x_second(1)
    z_last(0)
    z_first(1)
    z_last(1)

    for copy in waiting:
        copy.wait_send()
    for chunk in range(CHUNKS):
        for mine, tiles_sent, slot in ((wide, 54, 256), (narrow, 55, 128)):
            @pl.when(mine)
            def _():
                sent = w_both.at[0, pl.ds(0, 16 * tiles_sent), pl.ds(0, 128)]
                pltpu.make_async_copy(sent, sent, a_send.at[chunk]).wait()
                sent = had_out.at[chunk, pl.ds(0, TP - 1), :, pl.ds(0, slot)]
                pltpu.make_async_copy(sent, sent, b_send.at[chunk]).wait()


def shards(tokens, gate_codes, gate_scales, up_codes, up_scales, local_factor, down_codes, down_scales):
    vmem, hbm, dma = pl.BlockSpec(memory_space=pltpu.VMEM), pl.BlockSpec(memory_space=pl.ANY), pltpu.SemaphoreType.DMA
    return pl.pallas_call(
        kernel,
        out_shape=jax.ShapeDtypeStruct((ROWS, 128), BF16),
        in_specs=[vmem] * 4 + [hbm] * 4,
        out_specs=vmem,
        scratch_shapes=[
            pltpu.VMEM((1024, UNITS), jnp.int32),
            pltpu.VMEM((1024, UNITS), jnp.int32),
            pltpu.VMEM((224, 4096), jnp.int32),
            pltpu.VMEM((UNITS, UNITS), BF16),
            pltpu.VMEM((ROWS, 4096), BF16),
            pltpu.VMEM((TILES, 4096, 256), BF16),
            pltpu.VMEM((16, UNITS, 256), BF16),
            pltpu.VMEM((UNITS, UNITS), BF16),
            pltpu.VMEM((32, 8, UNITS), F32),
            pltpu.VMEM((32, 8, UNITS), F32),
            pltpu.VMEM((7, 8, 4096), F32),
            pltpu.VMEM((ROWS, UNITS), BF16),
            pltpu.VMEM((CHUNKS, CR // 16, 16, UNITS), BF16),
            pltpu.VMEM((CHUNKS, TP, 16, 256), BF16),
            pltpu.VMEM((CHUNKS, TP, 16, 256), BF16),
            pltpu.VMEM((CHUNKS, CR // 16, 16, UNITS), BF16),
            pltpu.VMEM((CHUNKS, 2, 4, 4, CR, 128), BF16),
            pltpu.VMEM((CHUNKS, 4, 4, CR, 128), BF16),
            pltpu.VMEM((CHUNKS, 4, 4, CR, 128), BF16),
            pltpu.VMEM((CHUNKS, 2, 4, HALF, 128), BF16),
            pltpu.VMEM((CHUNKS, 2, 4, CR, 128), BF16),
            pltpu.VMEM((CHUNKS, 4, CR, 128), BF16),
            pltpu.VMEM((CHUNKS, 4, CR, 128), BF16),
            dma((10,)),
            dma((48,)),
            dma((TP, 2)),
            dma((CHUNKS,)),
            dma((CHUNKS,)),
            dma((CHUNKS,)),
            dma((CHUNKS,)),
            dma((CHUNKS, 4)),
            dma((CHUNKS, 4)),
            dma((CHUNKS, 2)),
            dma((CHUNKS, 2)),
            dma((CHUNKS, 2)),
            dma((CHUNKS, 2)),
            dma((CHUNKS, 4)),
            dma((CHUNKS, 4)),
        ],
        compiler_params=pltpu.CompilerParams(
            collective_id=0, has_side_effects=True, vmem_limit_bytes=58 * 1024 * 1024
        ),
        name="feed_forward",
    )(tokens, gate_scales, up_scales, down_scales, gate_codes, up_codes, local_factor, down_codes)


def solution(mesh):
    return jax.shard_map(
        shards,
        mesh=mesh,
        in_specs=(
            P("req", "tp"),
            P(None, "tp"),
            P(None, "tp"),
            P(None, "tp"),
            P(None, "tp"),
            P(),
            P("tp", None),
            P("tp", None),
        ),
        out_specs=P("req", "tp"),
        check_vma=False,
    )
```

```python
import functools
import math

import jax
import jax.numpy as jnp
from jax import lax
from jax.experimental import pallas as pl
from jax.experimental.pallas import tpu as pltpu
from jax.sharding import PartitionSpec as P

MESH = pl.DeviceIdType.MESH
TP = 32
ROWS = 256
UNITS = 896
TILES = 7
CHUNKS = 2
CR = ROWS // CHUNKS
HALF = CR // 2
F32 = jnp.float32
BF16 = jnp.bfloat16


def field_order():
    source = lax.broadcasted_iota(jnp.int32, (128, 128), 0)
    target = lax.broadcasted_iota(jnp.int32, (128, 128), 1)
    return jnp.where(target == (source % 4) * 32 + source // 4, 1.0, 0.0).astype(BF16)


def decode(words, scale):
    flipped = jnp.bitwise_xor(words, 0x0888)
    planes = []
    for field in range(4):
        if field == 3:
            value = jnp.right_shift(words, 12)
        else:
            value = jnp.right_shift(jnp.left_shift(flipped, 28 - 4 * field), 28)
        scaled = value.astype(F32).reshape(4, 8, 128) * scale
        planes.append(scaled.reshape(32, 128).astype(BF16))
    return planes


def kernel(
    tok_in, gate_scales, up_scales, down_scales, gate_hbm, up_hbm, factor_hbm, down_hbm, out_ref,
    staged, gate_codes, up_codes, down_codes, factor, tok, w_both, w_down, ordered, gate_f32, up_f32, down_f32,
    hidden, blocked, had_in, had_out, rotated, part, core_in, sums, first_in, second_in, mixed, z_in,
    load_sem, tok_send, tok_recv, a_send, a_recv, b_send, b_recv, c_send, c_recv, x_send, x_recv,
    y_send, y_recv, z_send, z_recv,
):
    me, mine = lax.axis_index("tp"), lax.axis_index("req")
    z, x, c = me // 8, (me // 2) % 4, me % 2
    upper, plane = mine % 2, mine - mine % 2
    low = z < 2
    other = me + 1 - 2 * c
    right = z * 8 + ((x + 1) % 4) * 2 + c
    left = z * 8 + ((x + 3) % 4) * 2 + c
    z_of = [z, z + 1 - 2 * (z % 2), (z + 2) % 4, 3 - z]

    served = jnp.where(low, 1 - upper, upper)

    def window(request, device_z):
        return plane + jnp.where(device_z < 2, 1 - request, request)

    def member(chunk, device):
        return {"req": window(served, device // 8) if chunk else mine, "tp": device}

    def worker(chunk, device):
        return {"req": window(upper, device // 8) if chunk else mine, "tp": device}

    def owner(chunk, device):
        return {"req": plane + served if chunk else mine, "tp": device}

    def here(device):
        return {"req": mine, "tp": device}

    barrier = pltpu.get_barrier_semaphore()

    def greet(device):
        pl.semaphore_signal(barrier, inc=1, device_id=device, device_id_type=MESH)

    @pl.loop(1, TP)
    def _(step):
        greet(here((me + step) % TP))

    far_side = jnp.where(low, 16, 0)

    @pl.loop(0, 16)
    def _(step):
        greet({"req": plane + 1 - upper, "tp": far_side + step})

    @pl.when(low)
    def _():
        for near in range(2):
            greet({"req": plane + 1 - upper, "tp": near * 8 + x * 2 + c})

    loads = []
    for piece in range(4):
        rows = pl.ds(256 * piece, 256)
        loads.append([
            pltpu.make_async_copy(gate_hbm.at[rows], gate_codes.at[rows], load_sem.at[piece]),
            pltpu.make_async_copy(up_hbm.at[rows], up_codes.at[rows], load_sem.at[4 + piece]),
        ])
        for copy in loads[-1]:
            copy.start()
    factor_load = pltpu.make_async_copy(factor_hbm, factor, load_sem.at[8])
    factor_load.start()
    down_load = pltpu.make_async_copy(down_hbm, down_codes, load_sem.at[9])
    down_load.start()

    order = field_order()

    def columns(block):
        return pl.ds(pl.multiple_of(block * 128, 128), 128)

    staged[...] = jnp.dot(tok_in[...], order, preferred_element_type=F32).astype(BF16)
    tok[pl.ds(0, CR), columns(me)] = staged[pl.ds(0, CR), :]

    @pl.when(jnp.logical_not(low))
    def _():
        tok[pl.ds(CR, CR), columns(me)] = staged[pl.ds(CR, CR), :]

    for source, spread, groups in ((gate_scales, gate_f32, 32), (up_scales, up_f32, 32), (down_scales, down_f32, 7)):
        scales = source[...].astype(F32)
        for group in range(groups):
            spread[group] = jnp.broadcast_to(scales[group : group + 1], spread.shape[1:])

    pl.semaphore_wait(barrier, TP + 15 + jnp.where(low, 2, 0))

    waiting = []

    def remote(src, dst, send, recv, device):
        copy = pltpu.make_async_remote_copy(
            src_ref=src, dst_ref=dst, send_sem=send, recv_sem=recv, device_id=device, device_id_type=MESH,
        )
        copy.start()
        waiting.append(copy)
        return copy

    def rows_of(chunk, part):
        if part is None:
            return pl.ds(chunk * CR, CR)
        return pl.ds(chunk * CR + part * HALF, HALF)

    def slot(chunk, block, part):
        return tok_recv.at[chunk, block, part or 0]

    def pass_on(chunk, block, device, part=None):
        where = tok.at[rows_of(chunk, part), columns(block)]
        remote(where, where, tok_send.at[len(waiting)], slot(chunk, block, part), here(device))

    def arrived(chunk, block, part=None):
        where = tok.at[rows_of(chunk, part), columns(block)]
        pltpu.make_async_copy(where, where, slot(chunk, block, part)).wait()

    def at(near, shift):
        return z_of[near] * 8 + ((x + shift) % 4) * 2 + c

    def send_own(chunk):
        for near in (3, 2, 1):
            remote(
                staged.at[rows_of(chunk, None)], tok.at[rows_of(chunk, None), columns(me)],
                tok_send.at[len(waiting)], slot(chunk, me, None), worker(chunk, at(near, 0)),
            )
        if chunk:
            @pl.when(low)
            def _():
                own_copy().start()

    def own_copy():
        return pltpu.make_async_remote_copy(
            src_ref=staged.at[rows_of(1, None)], dst_ref=tok.at[rows_of(1, None), columns(me)],
            send_sem=tok_send.at[95], recv_sem=slot(1, me, None), device_id=worker(1, me), device_id_type=MESH,
        )

    def from_z(chunk, near):
        block = at(near, 0)
        if near:
            arrived(chunk, block)
        elif chunk:
            @pl.when(low)
            def _():
                arrived(chunk, block)
        pass_on(chunk, block, right)
        pass_on(chunk, block, left)
        pass_on(chunk, block, other)

    def from_x(chunk, near):
        block = at(near, 3)
        arrived(chunk, block)
        pass_on(chunk, block, right, 0)
        pass_on(chunk, block, other)
        block = at(near, 1)
        arrived(chunk, block)
        pass_on(chunk, block, left, 1)
        pass_on(chunk, block, other)

    def from_far(chunk, near):
        block = at(near, 2)
        arrived(chunk, block, 0)
        arrived(chunk, block, 1)
        pass_on(chunk, block, other)

    def from_core(chunk):
        @pl.loop(0, TP // 2)
        def _(chip):
            arrived(chunk, chip * 2 + 1 - c)

    def decode_piece(piece):
        if piece % 2 == 0:
            for copy in loads[piece // 2]:
                copy.wait()

        @pl.loop(4 * piece, 4 * piece + 4)
        def _(group):
            rows = pl.ds(pl.multiple_of(group * 32, 32), 32)
            for tile in range(TILES):
                cols = pl.ds(128 * tile, 128)
                for place, codes, scales in ((0, gate_codes, gate_f32), (128, up_codes, up_f32)):
                    planes = decode(codes[rows, cols], scales[group, :, cols])
                    for field, plane_of in enumerate(planes):
                        to = pl.ds(pl.multiple_of(group * 128 + 32 * field, 32), 32)
                        w_both[tile, to, pl.ds(place, 128)] = plane_of

    def gate_up(chunk, first, stop):
        @pl.loop(first, stop)
        def _(tile):
            rows = rows_of(chunk, None)
            both = jnp.dot(tok[rows, :], w_both[tile], preferred_element_type=F32)
            gate, up = both[:, :128], both[:, 128:]
            value = gate / (1.0 + jnp.exp(-gate)) * up
            hidden[rows, pl.ds(pl.multiple_of(tile * 128, 128), 128)] = value.astype(BF16)

    def share(device):
        dz, dx, dc = device // 8, (device // 2) % 4, device % 2
        return dz * 2 + dx // 2, (dx % 2) * 2 + dc

    row_tile, quarter = share(me)
    wide = quarter < 3
    narrow = quarter == 3

    def two(start):
        return pl.ds(pl.multiple_of(start * 256, 256), 256)

    last = pl.ds(768, 128)

    def scatter(chunk):
        value = jnp.dot(hidden[pl.ds(chunk * CR, CR), :], ordered[...], preferred_element_type=F32)
        blocked[chunk] = value.astype(BF16).reshape(CR // 16, 16, UNITS)

        @pl.loop(1, TP)
        def _(step):
            device = (me + 1 + (step + 6) % (TP - 1)) % TP
            tile, part_of = share(device)

            @pl.when(part_of < 3)
            def _():
                pltpu.make_async_remote_copy(
                    src_ref=blocked.at[chunk, tile, :, two(part_of)], dst_ref=had_in.at[chunk, me],
                    send_sem=a_send.at[chunk], recv_sem=a_recv.at[chunk],
                    device_id=member(chunk, device), device_id_type=MESH,
                ).start()

            @pl.when(part_of == 3)
            def _():
                pltpu.make_async_remote_copy(
                    src_ref=blocked.at[chunk, tile, :, last], dst_ref=had_in.at[chunk, me, :, pl.ds(0, 128)],
                    send_sem=a_send.at[chunk], recv_sem=a_recv.at[chunk],
                    device_id=member(chunk, device), device_id_type=MESH,
                ).start()

        @pl.when(wide)
        def _():
            pltpu.make_async_copy(
                blocked.at[chunk, row_tile, :, two(quarter)], had_in.at[chunk, me], a_recv.at[chunk]
            ).start()

        @pl.when(narrow)
        def _():
            pltpu.make_async_copy(
                blocked.at[chunk, row_tile, :, last], had_in.at[chunk, me, :, pl.ds(0, 128)], a_recv.at[chunk]
            ).start()

    def rotate(chunk):
        def combine(tile):
            cols = pl.ds(128 * tile, 128)
            held = [had_in[chunk, source, :, cols].astype(F32) for source in range(TP)]
            apart = 1
            while apart < TP:
                held = [
                    held[i - apart] - held[i] if i & apart else held[i] + held[i + apart]
                    for i in range(TP)
                ]
                apart *= 2
            for target in range(TP):
                had_out[chunk, target, :, cols] = (held[target] * (1.0 / math.sqrt(TP))).astype(BF16)

        def give(out_cols, to_cols):
            @pl.loop(1, TP)
            def _(step):
                device = (me + 1 + (step + 6) % (TP - 1)) % TP
                pltpu.make_async_remote_copy(
                    src_ref=had_out.at[chunk, device, :, out_cols], dst_ref=rotated.at[chunk, row_tile, :, to_cols],
                    send_sem=b_send.at[chunk], recv_sem=b_recv.at[chunk],
                    device_id=member(chunk, device), device_id_type=MESH,
                ).start()

            pltpu.make_async_copy(
                had_out.at[chunk, me, :, out_cols], rotated.at[chunk, row_tile, :, to_cols], b_recv.at[chunk]
            ).start()

        @pl.when(wide)
        def _():
            everything = had_in.at[chunk]
            pltpu.make_async_copy(everything, everything, a_recv.at[chunk]).wait()
            combine(0)
            combine(1)
            give(pl.ds(0, 256), two(quarter))

        @pl.when(narrow)
        def _():
            everything = had_in.at[chunk, :, :, pl.ds(0, 128)]
            pltpu.make_async_copy(everything, everything, a_recv.at[chunk]).wait()
            combine(0)
            give(pl.ds(0, 128), last)

    x_of = [x, (x + 1) % 4, (x + 2) % 4, (x + 3) % 4]
    from_other = {}

    def down(chunk):
        everything = rotated.at[chunk]
        pltpu.make_async_copy(everything, everything, b_recv.at[chunk]).wait()
        for shift in (2, 1, 3, 0):
            place = x_of[shift]

            @pl.loop(0, 4)
            def _(z_to):
                both = jnp.dot(
                    rotated[chunk].reshape(CR, UNITS), w_down[z_to * 4 + place], preferred_element_type=F32
                ).astype(BF16)
                part[chunk, 0, place, z_to] = both[:, :128]
                part[chunk, 1, place, z_to] = both[:, 128:]

            from_other[chunk, shift] = remote(
                part.at[chunk, 1 - c, place], core_in.at[chunk, shift],
                c_send.at[chunk, shift], c_recv.at[chunk, shift], here(other),
            )

    top, bottom = pl.ds(0, HALF), pl.ds(HALF, HALF)

    def join(chunk, shift, rows):
        return part[chunk, c, x_of[shift], :, rows].astype(F32) + core_in[chunk, shift, :, rows].astype(F32)

    x_copies = {}

    def x_first(chunk):
        from_other[chunk, 2].wait_recv()
        sums[chunk, 2] = join(chunk, 2, pl.ds(0, CR)).astype(BF16)
        x_copies[chunk, "r1"] = remote(
            sums.at[chunk, 2, :, top], first_in.at[chunk, 0], x_send.at[chunk, 0], x_recv.at[chunk, 0], here(right)
        )
        x_copies[chunk, "l1"] = remote(
            sums.at[chunk, 2, :, bottom], first_in.at[chunk, 1], x_send.at[chunk, 1], x_recv.at[chunk, 1], here(left)
        )
        from_other[chunk, 1].wait_recv()
        sums[chunk, 1, :, bottom] = join(chunk, 1, bottom).astype(BF16)
        from_other[chunk, 3].wait_recv()
        sums[chunk, 3, :, top] = join(chunk, 3, top).astype(BF16)

    def x_second(chunk):
        x_copies[chunk, "r1"].wait_recv()
        sums[chunk, 1, :, top] = (join(chunk, 1, top) + first_in[chunk, 0].astype(F32)).astype(BF16)
        x_copies[chunk, "r2"] = remote(
            sums.at[chunk, 1], second_in.at[chunk, 0], y_send.at[chunk, 0], y_recv.at[chunk, 0], here(right)
        )
        x_copies[chunk, "l1"].wait_recv()
        sums[chunk, 3, :, bottom] = (join(chunk, 3, bottom) + first_in[chunk, 1].astype(F32)).astype(BF16)
        x_copies[chunk, "l2"] = remote(
            sums.at[chunk, 3], second_in.at[chunk, 1], y_send.at[chunk, 1], y_recv.at[chunk, 1], here(left)
        )
        from_other[chunk, 0].wait_recv()

    z_copies = {}

    def z_first(chunk):
        x_copies[chunk, "r2"].wait_recv()
        x_copies[chunk, "l2"].wait_recv()
        for near in (3, 2, 1, 0):
            to = z_of[near]
            value = (
                part[chunk, c, x, to].astype(F32) + core_in[chunk, 0, to].astype(F32)
                + second_in[chunk, 0, to].astype(F32) + second_in[chunk, 1, to].astype(F32)
            )
            mixed[chunk, near] = value.astype(BF16)
            if near:
                z_copies[chunk, near] = remote(
                    mixed.at[chunk, near], z_in.at[chunk, near], z_send.at[chunk, near], z_recv.at[chunk, near],
                    owner(chunk, to * 8 + x * 2 + c),
                )
        if chunk:
            @pl.when(low)
            def _():
                own_sum().start()

    def own_sum():
        return pltpu.make_async_remote_copy(
            src_ref=mixed.at[1, 0], dst_ref=z_in.at[1, 0], send_sem=z_send.at[1, 0], recv_sem=z_recv.at[1, 0],
            device_id=owner(1, me), device_id_type=MESH,
        )

    def z_last(chunk):
        for near in (1, 2, 3):
            z_copies[chunk, near].wait_recv()

        def finish(total):
            for near in (1, 2, 3):
                total = total + z_in[chunk, near].astype(F32)
            out_ref[pl.ds(chunk * CR, CR), :] = total.astype(BF16)

        if chunk:
            @pl.when(low)
            def _():
                own_sum().wait_recv()
                finish(z_in[chunk, 0].astype(F32))

            @pl.when(jnp.logical_not(low))
            def _():
                finish(mixed[chunk, 0].astype(F32))
        else:
            finish(mixed[chunk, 0].astype(F32))

    send_own(0)
    from_z(0, 0)
    decode_piece(0)
    decode_piece(1)
    from_z(0, 1)
    from_x(0, 0)
    decode_piece(2)
    from_z(0, 2)
    from_x(0, 1)
    decode_piece(3)
    from_z(0, 3)
    from_x(0, 2)
    from_far(0, 0)
    send_own(1)
    decode_piece(4)
    from_x(0, 3)
    from_far(0, 1)
    decode_piece(5)
    from_far(0, 2)
    from_far(0, 3)
    decode_piece(6)
    from_z(1, 1)
    from_z(1, 2)
    decode_piece(7)
    factor_load.wait()
    for tile in range(TILES):
        cols = pl.ds(128 * tile, 128)
        ordered[:, cols] = jnp.dot(factor[:, cols], order, preferred_element_type=F32).astype(BF16)
    from_z(1, 3)
    from_z(1, 0)
    from_x(1, 1)
    from_core(0)
    gate_up(0, 0, 2)
    from_x(1, 2)
    from_x(1, 3)
    gate_up(0, 2, 4)
    from_x(1, 0)
    from_far(1, 1)
    gate_up(0, 4, 6)
    from_far(1, 2)
    from_far(1, 3)
    gate_up(0, 6, 7)
    scatter(0)
    from_far(1, 0)
    from_core(1)
    gate_up(1, 0, 7)
    scatter(1)

    down_load.wait()

    @pl.loop(0, 16)
    def _(chip):
        for group in range(TILES):
            for side in range(2):
                cols = pl.ds(pl.multiple_of(chip * 256 + 128 * side, 128), 128)
                planes = decode(down_codes[pl.ds(32 * group, 32), cols], down_f32[group, :, cols])
                for field, plane_of in enumerate(planes):
                    w_down[chip, pl.ds(128 * group + 32 * field, 32), pl.ds(128 * side, 128)] = plane_of

    rotate(0)
    rotate(1)
    down(0)
    x_first(0)
    down(1)
    x_second(0)
    x_first(1)
    z_first(0)
    x_second(1)
    z_last(0)
    z_first(1)
    z_last(1)

    @pl.when(low)
    def _():
        own_copy().wait_send()
        own_sum().wait_send()

    for copy in waiting:
        copy.wait_send()
    for chunk in range(CHUNKS):
        for kind, tiles_sent, width in ((wide, 54, 256), (narrow, 55, 128)):
            @pl.when(kind)
            def _():
                sent = w_both.at[0, pl.ds(0, 16 * tiles_sent), pl.ds(0, 128)]
                pltpu.make_async_copy(sent, sent, a_send.at[chunk]).wait()
                sent = had_out.at[chunk, pl.ds(0, TP - 1), :, pl.ds(0, width)]
                pltpu.make_async_copy(sent, sent, b_send.at[chunk]).wait()


def shards(tokens, gate_codes, gate_scales, up_codes, up_scales, local_factor, down_codes, down_scales):
    vmem, hbm, dma = pl.BlockSpec(memory_space=pltpu.VMEM), pl.BlockSpec(memory_space=pl.ANY), pltpu.SemaphoreType.DMA
    return pl.pallas_call(
        kernel,
        out_shape=jax.ShapeDtypeStruct((ROWS, 128), BF16),
        in_specs=[vmem] * 4 + [hbm] * 4,
        out_specs=vmem,
        scratch_shapes=[
            pltpu.VMEM((ROWS, 128), BF16),
            pltpu.VMEM((1024, UNITS), jnp.int32),
            pltpu.VMEM((1024, UNITS), jnp.int32),
            pltpu.VMEM((224, 4096), jnp.int32),
            pltpu.VMEM((UNITS, UNITS), BF16),
            pltpu.VMEM((ROWS, 4096), BF16),
            pltpu.VMEM((TILES, 4096, 256), BF16),
            pltpu.VMEM((16, UNITS, 256), BF16),
            pltpu.VMEM((UNITS, UNITS), BF16),
            pltpu.VMEM((32, 8, UNITS), F32),
            pltpu.VMEM((32, 8, UNITS), F32),
            pltpu.VMEM((7, 8, 4096), F32),
            pltpu.VMEM((ROWS, UNITS), BF16),
            pltpu.VMEM((CHUNKS, CR // 16, 16, UNITS), BF16),
            pltpu.VMEM((CHUNKS, TP, 16, 256), BF16),
            pltpu.VMEM((CHUNKS, TP, 16, 256), BF16),
            pltpu.VMEM((CHUNKS, CR // 16, 16, UNITS), BF16),
            pltpu.VMEM((CHUNKS, 2, 4, 4, CR, 128), BF16),
            pltpu.VMEM((CHUNKS, 4, 4, CR, 128), BF16),
            pltpu.VMEM((CHUNKS, 4, 4, CR, 128), BF16),
            pltpu.VMEM((CHUNKS, 2, 4, HALF, 128), BF16),
            pltpu.VMEM((CHUNKS, 2, 4, CR, 128), BF16),
            pltpu.VMEM((CHUNKS, 4, CR, 128), BF16),
            pltpu.VMEM((CHUNKS, 4, CR, 128), BF16),
            dma((10,)),
            dma((96,)),
            dma((CHUNKS, TP, 2)),
            dma((CHUNKS,)),
            dma((CHUNKS,)),
            dma((CHUNKS,)),
            dma((CHUNKS,)),
            dma((CHUNKS, 4)),
            dma((CHUNKS, 4)),
            dma((CHUNKS, 2)),
            dma((CHUNKS, 2)),
            dma((CHUNKS, 2)),
            dma((CHUNKS, 2)),
            dma((CHUNKS, 4)),
            dma((CHUNKS, 4)),
        ],
        compiler_params=pltpu.CompilerParams(
            collective_id=0, has_side_effects=True, vmem_limit_bytes=58 * 1024 * 1024
        ),
        name="feed_forward",
    )(tokens, gate_scales, up_scales, down_scales, gate_codes, up_codes, local_factor, down_codes)


def solution(mesh):
    return jax.shard_map(
        shards,
        mesh=mesh,
        in_specs=(
            P("req", "tp"),
            P(None, "tp"),
            P(None, "tp"),
            P(None, "tp"),
            P(None, "tp"),
            P(),
            P("tp", None),
            P("tp", None),
        ),
        out_specs=P("req", "tp"),
        check_vma=False,
    )
```

```python
import functools
import math

import jax
import jax.numpy as jnp
from jax import lax
from jax.experimental import pallas as pl
from jax.experimental.pallas import tpu as pltpu
from jax.sharding import PartitionSpec as P

MESH = pl.DeviceIdType.MESH
TP = 32
ROWS = 256
UNITS = 896
TILES = 7
CHUNKS = 2
CR = ROWS // CHUNKS
HALF = CR // 2
F32 = jnp.float32
BF16 = jnp.bfloat16


def field_order():
    source = lax.broadcasted_iota(jnp.int32, (128, 128), 0)
    target = lax.broadcasted_iota(jnp.int32, (128, 128), 1)
    return jnp.where(target == (source % 4) * 32 + source // 4, 1.0, 0.0).astype(BF16)


def decode(words, scale):
    flipped = jnp.bitwise_xor(words, 0x0888)
    planes = []
    for field in range(4):
        if field == 3:
            value = jnp.right_shift(words, 12)
        else:
            value = jnp.right_shift(jnp.left_shift(flipped, 28 - 4 * field), 28)
        scaled = value.astype(F32).reshape(4, 8, 128) * scale
        planes.append(scaled.reshape(32, 128).astype(BF16))
    return planes


def kernel(
    tok_in, gate_scales, up_scales, down_scales, gate_hbm, up_hbm, factor_hbm, down_hbm, out_ref,
    gate_codes, up_codes, down_codes, factor, tok, w_both, w_down, ordered, gate_f32, up_f32, down_f32, total,
    hidden, had_in, had_out, rotated, turned, part, core_in, sums, first_in, second_in, mixed, z_in,
    load_sem, tok_send, tok_recv, a_send, a_recv, b_send, b_recv, c_send, c_recv, x_send, x_recv,
    y_send, y_recv, z_send, z_recv,
):
    me = lax.axis_index("tp")
    z, x, c = me // 8, (me // 2) % 4, me % 2
    other = me + 1 - 2 * c
    right = z * 8 + ((x + 1) % 4) * 2 + c
    left = z * 8 + ((x + 3) % 4) * 2 + c
    z_of = [z, z + 1 - 2 * (z % 2), (z + 2) % 4, 3 - z]

    barrier = pltpu.get_barrier_semaphore()

    @pl.loop(1, TP)
    def _(step):
        pl.semaphore_signal(barrier, inc=1, device_id={"tp": (me + step) % TP}, device_id_type=MESH)

    def column(shift):
        return (x + shift) % 4

    def code_rows(shift, z_at):
        return pl.ds(pl.multiple_of((z_at * 4 + column(shift)) * 64, 64), 64)

    loads = {}
    for place, shift in enumerate((0, 1, 3, 2)):
        for z_at in range(4):
            rows = code_rows(shift, z_at)
            first = (place * 4 + z_at) * 2
            loads[shift, z_at] = [
                pltpu.make_async_copy(gate_hbm.at[rows], gate_codes.at[rows], load_sem.at[first]),
                pltpu.make_async_copy(up_hbm.at[rows], up_codes.at[rows], load_sem.at[first + 1]),
            ]
            for copy in loads[shift, z_at]:
                copy.start()
    factor_load = pltpu.make_async_copy(factor_hbm, factor, load_sem.at[32])
    factor_load.start()
    down_load = pltpu.make_async_copy(down_hbm, down_codes, load_sem.at[33])
    down_load.start()

    order = field_order()

    def tokens_of(block, row, count):
        lanes = pl.ds(pl.multiple_of((block // 8) * 256 + (block % 2) * 128, 128), 128)
        return tok.at[(block // 2) % 4, pl.ds(row, count), lanes]

    tokens_of(me, 0, ROWS)[...] = jnp.dot(tok_in[...], order, preferred_element_type=F32).astype(BF16)

    pl.semaphore_wait(barrier, TP - 1)

    waiting = []

    def remote(src, dst, send, recv, device):
        copy = pltpu.make_async_remote_copy(
            src_ref=src, dst_ref=dst, send_sem=send, recv_sem=recv,
            device_id={"tp": device}, device_id_type=MESH,
        )
        copy.start()
        waiting.append(copy)
        return copy

    def pass_on(block, device, row=0, count=ROWS):
        where = tokens_of(block, row, count)
        remote(where, where, tok_send.at[len(waiting)], tok_recv.at[block, 1 if row else 0], device)

    def arrived(block, row=0, count=ROWS):
        where = tokens_of(block, row, count)
        pltpu.make_async_copy(where, where, tok_recv.at[block, 1 if row else 0]).wait()

    def at(near, shift):
        return z_of[near] * 8 + column(shift) * 2 + c

    def from_z(near):
        if near:
            arrived(at(near, 0))
        pass_on(at(near, 0), right)
        pass_on(at(near, 0), left)
        if not near:
            for peer in (1, 2, 3):
                pass_on(me, at(peer, 0))
        pass_on(at(near, 0), other)

    def from_x(near):
        block = at(near, 3)
        arrived(block)
        pass_on(block, right, 0, ROWS // 2)
        pass_on(block, other)
        block = at(near, 1)
        arrived(block)
        pass_on(block, left, ROWS // 2, ROWS // 2)
        pass_on(block, other)

    def from_far(near):
        block = at(near, 2)
        arrived(block, 0, ROWS // 2)
        arrived(block, ROWS // 2, ROWS // 2)
        pass_on(block, other)

    def from_core(shift):
        for z_at in range(4):
            arrived(z_at * 8 + column(shift) * 2 + 1 - c)

    def decode_piece(shift, z_at):
        for copy in loads[shift, z_at]:
            copy.wait()

        @pl.loop(0, 2)
        def _(side):
            group = (z_at * 4 + column(shift)) * 2 + side
            rows = pl.ds(pl.multiple_of(group * 32, 32), 32)
            for tile in range(TILES):
                cols = pl.ds(128 * tile, 128)
                for place, codes, scales in ((0, gate_codes, gate_f32), (128, up_codes, up_f32)):
                    planes = decode(codes[rows, cols], scales[group, :, cols])
                    for field, plane in enumerate(planes):
                        to = pl.ds(pl.multiple_of(z_at * 256 + side * 128 + 32 * field, 32), 32)
                        w_both[column(shift), tile, to, pl.ds(place, 128)] = plane

    def product(shift, tile):
        return jnp.dot(tok[column(shift)], w_both[column(shift), tile], preferred_element_type=F32)

    chip = me // 2
    wide, narrow = pl.ds(0, 256), pl.ds(0, 128)
    group_cols = [pl.ds(0, 256), pl.ds(256, 256), pl.ds(512, 256), pl.ds(768, 128)]
    group_width = [256, 256, 256, 128]

    def scatter(group):
        side, lanes = group % 2, pl.ds(0, group_width[group])

        def give(to_chip):
            pltpu.make_async_remote_copy(
                src_ref=hidden.at[to_chip, :, group_cols[group]], dst_ref=had_in.at[group // 2, me, :, lanes],
                send_sem=a_send.at[group], recv_sem=a_recv.at[group // 2],
                device_id={"tp": to_chip * 2 + side}, device_id_type=MESH,
            ).start()

        @pl.loop(1, 16)
        def _(step):
            give((chip + 1 + (step + 2) % 15) % 16)

        @pl.when(c == side)
        def _():
            pltpu.make_async_copy(
                hidden.at[chip, :, group_cols[group]], had_in.at[group // 2, me, :, lanes], a_recv.at[group // 2]
            ).start()

        @pl.when(c != side)
        def _():
            give(chip)

    def rotate(group):
        turn, lanes = group // 2, pl.ds(0, group_width[group])
        everything = had_in.at[turn, :, :, lanes]
        pltpu.make_async_copy(everything, everything, a_recv.at[turn]).wait()
        for tile in range(group_width[group] // 128):
            cols = pl.ds(128 * tile, 128)
            held = [had_in[turn, source, :, cols].astype(F32) * (1.0 / TP) for source in range(TP)]
            apart = 1
            while apart < TP:
                held = [
                    held[i - apart] - held[i] if i & apart else held[i] + held[i + apart]
                    for i in range(TP)
                ]
                apart *= 2
            for target in range(TP):
                had_out[turn, target, :, cols] = held[target].astype(BF16)

        @pl.loop(1, TP)
        def _(step):
            device = (me + 1 + (step + 6) % (TP - 1)) % TP
            pltpu.make_async_remote_copy(
                src_ref=had_out.at[turn, device, :, lanes], dst_ref=rotated.at[chip, :, group_cols[group]],
                send_sem=b_send.at[turn], recv_sem=b_recv.at[group],
                device_id={"tp": device}, device_id_type=MESH,
            ).start()

        pltpu.make_async_copy(
            had_out.at[turn, me, :, lanes], rotated.at[chip, :, group_cols[group]], b_recv.at[group]
        ).start()

    def rotate_turn(turn):
        for side in range(2):
            @pl.when(c == side)
            def _():
                rotate(2 * turn + side)

    def back(group):
        everything = rotated.at[:, :, group_cols[group]]
        pltpu.make_async_copy(everything, everything, b_recv.at[group]).wait()

    def decode_down(first, stop):
        @pl.loop(first, stop)
        def _(place):
            for group in range(TILES):
                for side in range(2):
                    cols = pl.ds(pl.multiple_of(place * 256 + 128 * side, 128), 128)
                    planes = decode(down_codes[pl.ds(32 * group, 32), cols], down_f32[group, :, cols])
                    for field, plane in enumerate(planes):
                        to = pl.ds(pl.multiple_of((place // 4) * 256 + 128 * side, 128), 128)
                        w_down[place % 4, pl.ds(128 * group + 32 * field, 32), to] = plane

    from_other = {}

    def down(shift):
        place = column(shift)
        for pair in range(2):
            both = jnp.dot(
                turned[...], w_down[place, :, pl.ds(512 * pair, 512)], preferred_element_type=F32
            ).astype(BF16)
            for chunk in range(CHUNKS):
                rows = slice(chunk * CR, (chunk + 1) * CR)
                for z_at in range(2):
                    for side in range(2):
                        lanes = slice(256 * z_at + 128 * side, 256 * z_at + 128 * side + 128)
                        part[chunk, side, place, 2 * pair + z_at] = both[rows, lanes]
        for chunk in range(CHUNKS):
            from_other[chunk, shift] = remote(
                part.at[chunk, 1 - c, place], core_in.at[chunk, shift],
                c_send.at[chunk, shift], c_recv.at[chunk, shift], other,
            )

    top, bottom = pl.ds(0, HALF), pl.ds(HALF, HALF)

    def join(chunk, shift, rows):
        return part[chunk, c, column(shift), :, rows].astype(F32) + core_in[chunk, shift, :, rows].astype(F32)

    x_copies = {}

    def x_first(chunk):
        from_other[chunk, 2].wait_recv()
        sums[chunk, 2] = join(chunk, 2, pl.ds(0, CR)).astype(BF16)
        x_copies[chunk, "r1"] = remote(
            sums.at[chunk, 2, :, top], first_in.at[chunk, 0], x_send.at[chunk, 0], x_recv.at[chunk, 0], right
        )
        x_copies[chunk, "l1"] = remote(
            sums.at[chunk, 2, :, bottom], first_in.at[chunk, 1], x_send.at[chunk, 1], x_recv.at[chunk, 1], left
        )

    def x_second(chunk):
        from_other[chunk, 1].wait_recv()
        sums[chunk, 1, :, bottom] = join(chunk, 1, bottom).astype(BF16)
        x_copies[chunk, "r1"].wait_recv()
        sums[chunk, 1, :, top] = (join(chunk, 1, top) + first_in[chunk, 0].astype(F32)).astype(BF16)
        x_copies[chunk, "r2"] = remote(
            sums.at[chunk, 1], second_in.at[chunk, 0], y_send.at[chunk, 0], y_recv.at[chunk, 0], right
        )
        from_other[chunk, 3].wait_recv()
        sums[chunk, 3, :, top] = join(chunk, 3, top).astype(BF16)
        x_copies[chunk, "l1"].wait_recv()
        sums[chunk, 3, :, bottom] = (join(chunk, 3, bottom) + first_in[chunk, 1].astype(F32)).astype(BF16)
        x_copies[chunk, "l2"] = remote(
            sums.at[chunk, 3], second_in.at[chunk, 1], y_send.at[chunk, 1], y_recv.at[chunk, 1], left
        )

    z_copies = {}

    def z_first(chunk):
        from_other[chunk, 0].wait_recv()
        x_copies[chunk, "r2"].wait_recv()
        x_copies[chunk, "l2"].wait_recv()
        for near in (3, 2, 1, 0):
            to = z_of[near]
            value = (
                part[chunk, c, x, to].astype(F32) + core_in[chunk, 0, to].astype(F32)
                + second_in[chunk, 0, to].astype(F32) + second_in[chunk, 1, to].astype(F32)
            )
            mixed[chunk, near] = value.astype(BF16)
            if near:
                z_copies[chunk, near] = remote(
                    mixed.at[chunk, near], z_in.at[chunk, near], z_send.at[chunk, near], z_recv.at[chunk, near],
                    to * 8 + x * 2 + c,
                )

    def z_last(chunk):
        total = mixed[chunk, 0].astype(F32)
        for near in (1, 2, 3):
            z_copies[chunk, near].wait_recv()
            total = total + z_in[chunk, near].astype(F32)
        out_ref[pl.ds(chunk * CR, CR), :] = total.astype(BF16)

    from_z(0)
    for source, spread, groups in ((gate_scales, gate_f32, 32), (up_scales, up_f32, 32), (down_scales, down_f32, 7)):
        scales = source[...].astype(F32)
        for group in range(groups):
            spread[group] = jnp.broadcast_to(scales[group : group + 1], spread.shape[1:])
    for z_at in range(4):
        decode_piece(0, z_at)
    from_z(1)
    from_x(0)
    decode_piece(1, 0)
    decode_piece(1, 1)
    from_z(2)
    from_x(1)
    decode_piece(1, 2)
    decode_piece(1, 3)
    from_z(3)
    from_x(2)
    from_far(0)
    decode_piece(3, 0)
    decode_piece(3, 1)
    from_far(1)
    from_x(3)
    decode_piece(3, 2)
    decode_piece(3, 3)
    from_far(2)
    from_core(0)

    @pl.loop(0, TILES)
    def _(tile):
        total[tile] = product(0, tile)

    from_far(3)
    for z_at in range(4):
        decode_piece(2, z_at)
    factor_load.wait()
    for tile in range(TILES):
        cols = pl.ds(128 * tile, 128)
        ordered[:, cols] = jnp.dot(factor[:, cols], order, preferred_element_type=F32).astype(BF16)
    from_core(1)
    from_core(3)

    @pl.loop(0, TILES)
    def _(tile):
        total[tile] += product(1, tile) + product(3, tile)

    from_core(2)
    for group in range(4):
        @pl.loop(2 * group, min(2 * group + 2, TILES))
        def _(tile):
            both = total[tile] + product(2, tile)
            gate, up = both[:, :128], both[:, 128:]
            value = gate / (1.0 + jnp.exp(-gate)) * up
            lanes = pl.ds(pl.multiple_of(tile * 128, 128), 128)
            hidden[:, :, lanes] = value.astype(BF16).reshape(16, 16, 128)

        scatter(group)

    down_load.wait()
    decode_down(0, 8)
    rotate_turn(0)
    decode_down(8, 16)
    rotate_turn(1)
    back(0)
    back(1)
    first_part = jnp.dot(
        rotated[:, :, pl.ds(0, 512)].reshape(ROWS, 512), ordered[pl.ds(0, 512), :], preferred_element_type=F32
    )
    back(2)
    back(3)
    whole = first_part + jnp.dot(
        rotated[:, :, pl.ds(512, 384)].reshape(ROWS, 384), ordered[pl.ds(512, 384), :], preferred_element_type=F32
    )
    turned[...] = (whole * math.sqrt(TP)).astype(BF16)
    down(2)
    down(1)
    x_first(0)
    x_first(1)
    down(3)
    down(0)
    x_second(0)
    x_second(1)
    z_first(0)
    z_first(1)
    z_last(0)
    z_last(1)

    for copy in waiting:
        copy.wait_send()
    for group in range(4):
        for kept in range(2):
            @pl.when((c == group % 2) if kept else (c != group % 2))
            def _():
                sent = hidden.at[pl.ds(0, 16 - kept), :, group_cols[group]]
                pltpu.make_async_copy(sent, sent, a_send.at[group]).wait()
                if kept:
                    sent = had_out.at[group // 2, pl.ds(0, TP - 1), :, pl.ds(0, group_width[group])]
                    pltpu.make_async_copy(sent, sent, b_send.at[group // 2]).wait()


def shards(tokens, gate_codes, gate_scales, up_codes, up_scales, local_factor, down_codes, down_scales):
    vmem, hbm, dma = pl.BlockSpec(memory_space=pltpu.VMEM), pl.BlockSpec(memory_space=pl.ANY), pltpu.SemaphoreType.DMA
    return pl.pallas_call(
        kernel,
        out_shape=jax.ShapeDtypeStruct((ROWS, 128), BF16),
        in_specs=[vmem] * 4 + [hbm] * 4,
        out_specs=vmem,
        scratch_shapes=[
            pltpu.VMEM((1024, UNITS), jnp.int32),
            pltpu.VMEM((1024, UNITS), jnp.int32),
            pltpu.VMEM((224, 4096), jnp.int32),
            pltpu.VMEM((UNITS, UNITS), BF16),
            pltpu.VMEM((4, ROWS, 1024), BF16),
            pltpu.VMEM((4, TILES, 1024, 256), BF16),
            pltpu.VMEM((4, UNITS, 1024), BF16),
            pltpu.VMEM((UNITS, UNITS), BF16),
            pltpu.VMEM((32, 8, UNITS), F32),
            pltpu.VMEM((32, 8, UNITS), F32),
            pltpu.VMEM((7, 8, 4096), F32),
            pltpu.VMEM((TILES, ROWS, 256), F32),
            pltpu.VMEM((16, 16, UNITS), BF16),
            pltpu.VMEM((2, TP, 16, 256), BF16),
            pltpu.VMEM((2, TP, 16, 256), BF16),
            pltpu.VMEM((16, 16, UNITS), BF16),
            pltpu.VMEM((ROWS, UNITS), BF16),
            pltpu.VMEM((CHUNKS, 2, 4, 4, CR, 128), BF16),
            pltpu.VMEM((CHUNKS, 4, 4, CR, 128), BF16),
            pltpu.VMEM((CHUNKS, 4, 4, CR, 128), BF16),
            pltpu.VMEM((CHUNKS, 2, 4, HALF, 128), BF16),
            pltpu.VMEM((CHUNKS, 2, 4, CR, 128), BF16),
            pltpu.VMEM((CHUNKS, 4, CR, 128), BF16),
            pltpu.VMEM((CHUNKS, 4, CR, 128), BF16),
            dma((34,)),
            dma((48,)),
            dma((TP, 2)),
            dma((4,)),
            dma((2,)),
            dma((2,)),
            dma((4,)),
            dma((CHUNKS, 4)),
            dma((CHUNKS, 4)),
            dma((CHUNKS, 2)),
            dma((CHUNKS, 2)),
            dma((CHUNKS, 2)),
            dma((CHUNKS, 2)),
            dma((CHUNKS, 4)),
            dma((CHUNKS, 4)),
        ],
        compiler_params=pltpu.CompilerParams(
            collective_id=0, has_side_effects=True, vmem_limit_bytes=58 * 1024 * 1024
        ),
        name="feed_forward",
    )(tokens, gate_scales, up_scales, down_scales, gate_codes, up_codes, local_factor, down_codes)


def solution(mesh):
    return jax.shard_map(
        shards,
        mesh=mesh,
        in_specs=(
            P("req", "tp"),
            P(None, "tp"),
            P(None, "tp"),
            P(None, "tp"),
            P(None, "tp"),
            P(),
            P("tp", None),
            P("tp", None),
        ),
        out_specs=P("req", "tp"),
        check_vma=False,
    )
```

```python
import functools
import math

import jax
import jax.numpy as jnp
from jax import lax
from jax.experimental import pallas as pl
from jax.experimental.pallas import tpu as pltpu
from jax.sharding import PartitionSpec as P

MESH = pl.DeviceIdType.MESH
TP = 32
ROWS = 256
UNITS = 896
TILES = 7
CHUNKS = 2
CR = ROWS // CHUNKS
HALF = CR // 2
F32 = jnp.float32
BF16 = jnp.bfloat16


def field_order():
    source = lax.broadcasted_iota(jnp.int32, (128, 128), 0)
    target = lax.broadcasted_iota(jnp.int32, (128, 128), 1)
    return jnp.where(target == (source % 4) * 32 + source // 4, 1.0, 0.0).astype(BF16)


def decode(words, scale):
    flipped = jnp.bitwise_xor(words, 0x0888)
    planes = []
    for field in range(4):
        if field == 3:
            value = jnp.right_shift(words, 12)
        else:
            value = jnp.right_shift(jnp.left_shift(flipped, 28 - 4 * field), 28)
        scaled = value.astype(F32).reshape(4, 8, 128) * scale
        planes.append(scaled.reshape(32, 128).astype(BF16))
    return planes


def kernel(
    tok_in, gate_scales, up_scales, down_scales, gate_hbm, up_hbm, factor_hbm, down_hbm, out_ref,
    gate_codes, up_codes, down_codes, factor, tok, w_both, w_down, ordered, gate_f32, up_f32, down_f32, total,
    hidden, had_in, had_out, rotated, turned, part, core_in, sums, first_in, second_in, mixed, z_in,
    load_sem, own_send, near_send, x_tok_send, far_send, tok_recv, a_send, a_recv, b_send, b_recv,
    c_send, c_recv, x_send, x_recv, y_send, y_recv, z_send, z_recv,
):
    me = lax.axis_index("tp")
    z, x, c = me // 8, (me // 2) % 4, me % 2
    chip = me // 2
    other = me + 1 - 2 * c
    right = z * 8 + ((x + 1) % 4) * 2 + c
    left = z * 8 + ((x + 3) % 4) * 2 + c

    def z_of(near):
        return 2 * ((z // 2 + near // 2) % 2) + (z + near) % 2

    def column(shift):
        return (x + shift) % 4

    def use_order(place):
        return place + (place // 2) * (1 - 2 * (place % 2))

    def lanes_at(start, width):
        return pl.ds(pl.multiple_of(start, 128), width)

    def send(src, dst, send_sem, recv_sem, device):
        pltpu.make_async_remote_copy(
            src_ref=src, dst_ref=dst, send_sem=send_sem, recv_sem=recv_sem,
            device_id={"tp": device}, device_id_type=MESH,
        ).start()

    def wait(shaped, sem):
        pltpu.make_async_copy(shaped, shaped, sem).wait()

    barrier = pltpu.get_barrier_semaphore()

    @pl.loop(1, TP)
    def _(step):
        pl.semaphore_signal(barrier, inc=1, device_id={"tp": (me + step) % TP}, device_id_type=MESH)

    def code_rows(step):
        return pl.ds(pl.multiple_of(((step % 4) * 4 + column(use_order(step // 4))) * 64, 64), 64)

    @pl.loop(0, 16)
    def _(step):
        rows = code_rows(step)
        pltpu.make_async_copy(gate_hbm.at[rows], gate_codes.at[rows], load_sem.at[step]).start()
        pltpu.make_async_copy(up_hbm.at[rows], up_codes.at[rows], load_sem.at[16 + step]).start()

    pltpu.make_async_copy(factor_hbm, factor, load_sem.at[32]).start()
    pltpu.make_async_copy(down_hbm, down_codes, load_sem.at[33]).start()

    order = field_order()

    def tokens_of(block, row=0, count=ROWS):
        return tok.at[(block // 2) % 4, pl.ds(row, count), lanes_at((block // 8) * 256 + (block % 2) * 128, 128)]

    tokens_of(me)[...] = jnp.dot(tok_in[...], order, preferred_element_type=F32).astype(BF16)

    @pl.loop(0, 2)
    def _(step):
        rows = pl.ds(pl.multiple_of(step * 16, 16), 16)
        for source, spread in ((gate_scales, gate_f32), (up_scales, up_f32)):
            scales = source[rows, :].astype(F32)
            for row in range(16):
                spread[step * 16 + row] = jnp.broadcast_to(scales[row : row + 1], (8, UNITS))

    @pl.loop(0, TILES)
    def _(tile):
        total[tile] = jnp.zeros((ROWS, 256), F32)

    pl.semaphore_wait(barrier, TP - 1)

    def pass_on(block, device, sem, row=0, count=ROWS):
        where = tokens_of(block, row, count)
        send(where, where, sem, tok_recv.at[block, 1 if row else 0], device)

    def arrived(block, row=0, count=ROWS):
        wait(tokens_of(block, row, count), tok_recv.at[block, 1 if row else 0])

    def block_at(near, shift):
        return z_of(near) * 8 + column(shift) * 2 + c

    def pass_near(near):
        block = block_at(near, 0)
        pass_on(block, right, near_send.at[near, 0])
        pass_on(block, left, near_send.at[near, 1])
        pass_on(block, other, near_send.at[near, 2])

    def from_z(near):
        arrived(block_at(near, 0))
        pass_near(near)

    def from_x(near):
        block = block_at(near, 3)
        arrived(block)
        pass_on(block, right, x_tok_send.at[near, 0], 0, ROWS // 2)
        pass_on(block, other, x_tok_send.at[near, 1])
        block = block_at(near, 1)
        arrived(block)
        pass_on(block, left, x_tok_send.at[near, 2], ROWS // 2, ROWS // 2)
        pass_on(block, other, x_tok_send.at[near, 3])

    def from_far(near):
        block = block_at(near, 2)
        arrived(block, 0, ROWS // 2)
        arrived(block, ROWS // 2, ROWS // 2)
        pass_on(block, other, far_send.at[near])

    def from_core(shift):
        @pl.loop(0, 4)
        def _(z_at):
            arrived(z_at * 8 + column(shift) * 2 + 1 - c)

    def decode_half(turn):
        shift = use_order(turn // 2)

        @pl.loop(0, 4)
        def _(piece):
            z_at, side = (turn % 2) * 2 + piece // 2, piece % 2

            @pl.when(side == 0)
            def _():
                step = (turn // 2) * 4 + z_at
                wait(gate_codes.at[code_rows(step)], load_sem.at[step])
                wait(up_codes.at[code_rows(step)], load_sem.at[16 + step])

            group = (z_at * 4 + column(shift)) * 2 + side
            rows = pl.ds(pl.multiple_of(group * 32, 32), 32)
            for tile in range(TILES):
                cols = pl.ds(128 * tile, 128)
                for place, codes, scales in ((0, gate_codes, gate_f32), (128, up_codes, up_f32)):
                    planes = decode(codes[rows, cols], scales[group, :, cols])
                    for field, plane in enumerate(planes):
                        to = pl.ds(pl.multiple_of(z_at * 256 + side * 128 + 32 * field, 32), 32)
                        w_both[column(shift), tile, to, pl.ds(place, 128)] = plane

    def product(shift, tile):
        return jnp.dot(tok[column(shift)], w_both[column(shift), tile], preferred_element_type=F32)

    pass_near(0)

    @pl.loop(1, 4)
    def _(near):
        pass_on(me, block_at(near, 0), own_send.at[near])

    @pl.loop(0, 10)
    def _(turn):
        @pl.when(turn < 8)
        def _():
            decode_half(turn)

        even = turn % 2 == 0

        @pl.when(jnp.logical_and(even, turn < 6))
        def _():
            from_z(turn // 2 + 1)

        @pl.when(jnp.logical_and(turn % 2 == 1, turn < 8))
        def _():
            from_x(turn // 2)

        @pl.when(jnp.logical_and(turn % 2 == 1, turn >= 3))
        def _():
            from_far(turn // 2 - 1)

        @pl.when(jnp.logical_or(turn == 6, turn >= 8))
        def _():
            shift = (turn // 8) * (1 + 2 * (turn % 2))
            from_core(shift)

            @pl.loop(0, TILES)
            def _(tile):
                total[tile] += product(shift, tile)

    def scatter(group, width):
        side, cols, lanes = group % 2, lanes_at(group * 256, width), pl.ds(0, width)

        def give(to_chip):
            send(
                hidden.at[to_chip, :, cols], had_in.at[group // 2, me, :, lanes],
                a_send.at[group], a_recv.at[group // 2], to_chip * 2 + side,
            )

        @pl.loop(1, 16)
        def _(step):
            give((chip + 1 + (step + 2) % 15) % 16)

        @pl.when(c == side)
        def _():
            pltpu.make_async_copy(
                hidden.at[chip, :, cols], had_in.at[group // 2, me, :, lanes], a_recv.at[group // 2]
            ).start()

        @pl.when(c != side)
        def _():
            give(chip)

    from_core(2)

    @pl.loop(0, TILES)
    def _(tile):
        both = total[tile] + product(2, tile)
        gate, up = both[:, :128], both[:, 128:]
        value = gate / (1.0 + jnp.exp(-gate)) * up
        hidden[:, :, lanes_at(tile * 128, 128)] = value.astype(BF16).reshape(16, 16, 128)

        @pl.when(tile % 2 == 1)
        def _():
            scatter(tile // 2, 256)

    scatter(3, 128)

    for group in range(7):
        down_f32[group] = jnp.broadcast_to(down_scales[group : group + 1, :].astype(F32), (8, 4096))
    wait(factor, load_sem.at[32])

    @pl.loop(0, TILES)
    def _(tile):
        cols = lanes_at(tile * 128, 128)
        ordered[:, cols] = jnp.dot(factor[:, cols], order, preferred_element_type=F32).astype(BF16)

    ordered[:, pl.ds(UNITS, 128)] = jnp.zeros((UNITS, 128), BF16)
    wait(down_codes, load_sem.at[33])

    def decode_down(place):
        for group in range(TILES):
            for side in range(2):
                cols = lanes_at(place * 256 + 128 * side, 128)
                planes = decode(down_codes[pl.ds(32 * group, 32), cols], down_f32[group, :, cols])
                for field, plane in enumerate(planes):
                    to = lanes_at((place // 4) * 256 + 128 * side, 128)
                    w_down[place % 4, pl.ds(128 * group + 32 * field, 32), to] = plane

    def combine(turn, tile):
        cols = lanes_at(tile * 128, 128)
        held = [had_in[turn, source, :, cols].astype(F32) * (1.0 / TP) for source in range(TP)]
        apart = 1
        while apart < TP:
            held = [
                held[i - apart] - held[i] if i & apart else held[i] + held[i + apart]
                for i in range(TP)
            ]
            apart *= 2
        for target in range(TP):
            had_out[turn, target, :, cols] = held[target].astype(BF16)

    def give_back(turn, group, width):
        cols, lanes = lanes_at(group * 256, width), pl.ds(0, width)

        @pl.loop(1, TP)
        def _(step):
            device = (me + 1 + (step + 6) % (TP - 1)) % TP
            send(
                had_out.at[turn, device, :, lanes], rotated.at[chip, :, cols],
                b_send.at[turn], b_recv.at[group], device,
            )

        pltpu.make_async_copy(
            had_out.at[turn, me, :, lanes], rotated.at[chip, :, cols], b_recv.at[group]
        ).start()

    @pl.loop(0, 2)
    def _(turn):
        @pl.loop(8 * turn, 8 * turn + 8)
        def _(place):
            decode_down(place)

        group = 2 * turn + c

        @pl.when(group < 3)
        def _():
            wait(had_in.at[turn], a_recv.at[turn])

        @pl.when(group == 3)
        def _():
            wait(had_in.at[turn, :, :, pl.ds(0, 128)], a_recv.at[turn])

        @pl.loop(0, 2 - group // 3)
        def _(tile):
            combine(turn, tile)

        @pl.when(group < 3)
        def _():
            give_back(turn, group, 256)

        @pl.when(group == 3)
        def _():
            give_back(turn, 3, 128)

    for group, width in enumerate((256, 256, 256, 128)):
        wait(rotated.at[:, :, pl.ds(256 * group, width)], b_recv.at[group])

    @pl.loop(0, 4)
    def _(tile):
        cols = lanes_at(tile * 256, 256)
        value = jnp.dot(rotated[...].reshape(ROWS, UNITS), ordered[:, cols], preferred_element_type=F32)
        turned[:, cols] = (value * math.sqrt(TP)).astype(BF16)

    top, bottom = pl.ds(0, HALF), pl.ds(HALF, HALF)

    def join(chunk, shift, rows):
        return part[chunk, c, column(shift), :, rows].astype(F32) + core_in[chunk, shift, :, rows].astype(F32)

    def from_other(chunk, shift):
        wait(core_in.at[chunk, shift], c_recv.at[chunk, shift])

    def x_first(chunk):
        from_other(chunk, 2)
        sums[chunk, 2] = join(chunk, 2, pl.ds(0, CR)).astype(BF16)
        send(sums.at[chunk, 2, :, top], first_in.at[chunk, 0], x_send.at[chunk, 0], x_recv.at[chunk, 0], right)
        send(sums.at[chunk, 2, :, bottom], first_in.at[chunk, 1], x_send.at[chunk, 1], x_recv.at[chunk, 1], left)

    def x_second(chunk):
        from_other(chunk, 1)
        sums[chunk, 1, :, bottom] = join(chunk, 1, bottom).astype(BF16)
        wait(first_in.at[chunk, 0], x_recv.at[chunk, 0])
        sums[chunk, 1, :, top] = (join(chunk, 1, top) + first_in[chunk, 0].astype(F32)).astype(BF16)
        send(sums.at[chunk, 1], second_in.at[chunk, 0], y_send.at[chunk, 0], y_recv.at[chunk, 0], right)
        from_other(chunk, 3)
        sums[chunk, 3, :, top] = join(chunk, 3, top).astype(BF16)
        wait(first_in.at[chunk, 1], x_recv.at[chunk, 1])
        sums[chunk, 3, :, bottom] = (join(chunk, 3, bottom) + first_in[chunk, 1].astype(F32)).astype(BF16)
        send(sums.at[chunk, 3], second_in.at[chunk, 1], y_send.at[chunk, 1], y_recv.at[chunk, 1], left)

    def z_first(chunk):
        from_other(chunk, 0)
        wait(second_in.at[chunk, 0], y_recv.at[chunk, 0])
        wait(second_in.at[chunk, 1], y_recv.at[chunk, 1])

        @pl.loop(0, 4)
        def _(step):
            near = 3 - step
            to = z_of(near)
            value = (
                part[chunk, c, x, to].astype(F32) + core_in[chunk, 0, to].astype(F32)
                + second_in[chunk, 0, to].astype(F32) + second_in[chunk, 1, to].astype(F32)
            )
            mixed[chunk, near] = value.astype(BF16)

            @pl.when(near > 0)
            def _():
                send(
                    mixed.at[chunk, near], z_in.at[chunk, near], z_send.at[chunk, near], z_recv.at[chunk, near],
                    to * 8 + x * 2 + c,
                )

    def z_last(chunk):
        value = mixed[chunk, 0].astype(F32)
        for near in (1, 2, 3):
            wait(z_in.at[chunk, near], z_recv.at[chunk, near])
            value = value + z_in[chunk, near].astype(F32)
        out_ref[pl.ds(pl.multiple_of(chunk * CR, CR), CR), :] = value.astype(BF16)

    @pl.loop(0, 8)
    def _(step):
        turn, pair = step // 2, step % 2
        shift = jnp.where(turn == 3, 0, jnp.where(turn == 2, 3, 2 - turn))
        place = column(shift)
        both = jnp.dot(
            turned[:, pl.ds(0, UNITS)], w_down[place, :, lanes_at(512 * pair, 512)], preferred_element_type=F32
        ).astype(BF16)
        for chunk in range(CHUNKS):
            for z_at in range(2):
                for side in range(2):
                    lane = 256 * z_at + 128 * side
                    part[chunk, side, place, 2 * pair + z_at] = both[chunk * CR : chunk * CR + CR, lane : lane + 128]

        @pl.when(pair == 1)
        def _():
            @pl.loop(0, CHUNKS)
            def _(chunk):
                send(
                    part.at[chunk, 1 - c, place], core_in.at[chunk, shift],
                    c_send.at[chunk, shift], c_recv.at[chunk, shift], other,
                )

        @pl.when(step == 4)
        def _():
            pl.loop(0, CHUNKS)(x_first)

    pl.loop(0, CHUNKS)(x_second)
    pl.loop(0, CHUNKS)(z_first)
    pl.loop(0, CHUNKS)(z_last)

    @pl.loop(0, 4)
    def _(near):
        whole, half = tokens_of(0), tokens_of(0, 0, ROWS // 2)
        for to in range(3):
            wait(whole, near_send.at[near, to])
        for to in range(4):
            wait(whole if to % 2 else half, x_tok_send.at[near, to])
        wait(whole, far_send.at[near])

        @pl.when(near > 0)
        def _():
            wait(whole, own_send.at[near])

        @pl.loop(0, CHUNKS)
        def _(chunk):
            wait(core_in.at[chunk, near], c_send.at[chunk, near])

            @pl.when(near > 0)
            def _():
                wait(z_in.at[chunk, near], z_send.at[chunk, near])

            @pl.when(near < 2)
            def _():
                wait(first_in.at[chunk, near], x_send.at[chunk, near])
                wait(second_in.at[chunk, near], y_send.at[chunk, near])

    for group, width in enumerate((256, 256, 256, 128)):
        for kept in range(2):
            @pl.when((c == group % 2) if kept else (c != group % 2))
            def _():
                wait(hidden.at[pl.ds(0, 16 - kept), :, pl.ds(256 * group, width)], a_send.at[group])
                if kept:
                    wait(had_out.at[group // 2, pl.ds(0, TP - 1), :, pl.ds(0, width)], b_send.at[group // 2])


def shards(tokens, gate_codes, gate_scales, up_codes, up_scales, local_factor, down_codes, down_scales):
    vmem, hbm, dma = pl.BlockSpec(memory_space=pltpu.VMEM), pl.BlockSpec(memory_space=pl.ANY), pltpu.SemaphoreType.DMA
    return pl.pallas_call(
        kernel,
        out_shape=jax.ShapeDtypeStruct((ROWS, 128), BF16),
        in_specs=[vmem] * 4 + [hbm] * 4,
        out_specs=vmem,
        scratch_shapes=[
            pltpu.VMEM((1024, UNITS), jnp.int32),
            pltpu.VMEM((1024, UNITS), jnp.int32),
            pltpu.VMEM((224, 4096), jnp.int32),
            pltpu.VMEM((UNITS, UNITS), BF16),
            pltpu.VMEM((4, ROWS, 1024), BF16),
            pltpu.VMEM((4, TILES, 1024, 256), BF16),
            pltpu.VMEM((4, UNITS, 1024), BF16),
            pltpu.VMEM((UNITS, 1024), BF16),
            pltpu.VMEM((32, 8, UNITS), F32),
            pltpu.VMEM((32, 8, UNITS), F32),
            pltpu.VMEM((7, 8, 4096), F32),
            pltpu.VMEM((TILES, ROWS, 256), F32),
            pltpu.VMEM((16, 16, UNITS), BF16),
            pltpu.VMEM((2, TP, 16, 256), BF16),
            pltpu.VMEM((2, TP, 16, 256), BF16),
            pltpu.VMEM((16, 16, UNITS), BF16),
            pltpu.VMEM((ROWS, 1024), BF16),
            pltpu.VMEM((CHUNKS, 2, 4, 4, CR, 128), BF16),
            pltpu.VMEM((CHUNKS, 4, 4, CR, 128), BF16),
            pltpu.VMEM((CHUNKS, 4, 4, CR, 128), BF16),
            pltpu.VMEM((CHUNKS, 2, 4, HALF, 128), BF16),
            pltpu.VMEM((CHUNKS, 2, 4, CR, 128), BF16),
            pltpu.VMEM((CHUNKS, 4, CR, 128), BF16),
            pltpu.VMEM((CHUNKS, 4, CR, 128), BF16),
            dma((34,)),
            dma((4,)),
            dma((4, 3)),
            dma((4, 4)),
            dma((4,)),
            dma((TP, 2)),
            dma((4,)),
            dma((2,)),
            dma((2,)),
            dma((4,)),
            dma((CHUNKS, 4)),
            dma((CHUNKS, 4)),
            dma((CHUNKS, 2)),
            dma((CHUNKS, 2)),
            dma((CHUNKS, 2)),
            dma((CHUNKS, 2)),
            dma((CHUNKS, 4)),
            dma((CHUNKS, 4)),
        ],
        compiler_params=pltpu.CompilerParams(
            collective_id=0, has_side_effects=True, vmem_limit_bytes=58 * 1024 * 1024
        ),
        name="feed_forward",
    )(tokens, gate_scales, up_scales, down_scales, gate_codes, up_codes, local_factor, down_codes)


def solution(mesh):
    return jax.shard_map(
        shards,
        mesh=mesh,
        in_specs=(
            P("req", "tp"),
            P(None, "tp"),
            P(None, "tp"),
            P(None, "tp"),
            P(None, "tp"),
            P(),
            P("tp", None),
            P("tp", None),
        ),
        out_specs=P("req", "tp"),
        check_vma=False,
    )
```

```python
import functools
import math

import jax
import jax.numpy as jnp
from jax import lax
from jax.experimental import pallas as pl
from jax.experimental.pallas import tpu as pltpu
from jax.sharding import PartitionSpec as P

MESH = pl.DeviceIdType.MESH
TP = 32
ROWS = 256
UNITS = 896
TILES = 7
CHUNKS = 2
CR = ROWS // CHUNKS
HALF = CR // 2
F32 = jnp.float32
BF16 = jnp.bfloat16


def field_order():
    source = lax.broadcasted_iota(jnp.int32, (128, 128), 0)
    target = lax.broadcasted_iota(jnp.int32, (128, 128), 1)
    return jnp.where(target == (source % 4) * 32 + source // 4, 1.0, 0.0).astype(BF16)


def decode(words, scale):
    flipped = jnp.bitwise_xor(words, 0x0888)
    planes = []
    for field in range(4):
        if field == 3:
            value = jnp.right_shift(words, 12)
        else:
            value = jnp.right_shift(jnp.left_shift(flipped, 28 - 4 * field), 28)
        scaled = value.astype(F32).reshape(4, 8, 128) * scale
        planes.append(scaled.reshape(32, 128).astype(BF16))
    return planes


def kernel(
    tok_in, gate_scales, up_scales, down_scales, gate_hbm, up_hbm, factor_hbm, down_hbm, out_ref,
    gate_codes, up_codes, down_codes, factor, tok, w_both, w_down, ordered, gate_f32, up_f32, down_f32,
    hidden, had_in, had_out, rotated, turned, part, core_in, sums, first_in, second_in, mixed, z_in,
    load_sem, tok_send, tok_recv, a_send, a_recv, b_send, b_recv, c_send, c_recv, x_send, x_recv,
    y_send, y_recv, z_send, z_recv,
):
    me = lax.axis_index("tp")
    z, x, c = me // 8, (me // 2) % 4, me % 2
    other = me + 1 - 2 * c
    right = z * 8 + ((x + 1) % 4) * 2 + c
    left = z * 8 + ((x + 3) % 4) * 2 + c
    z_of = [z, z + 1 - 2 * (z % 2), (z + 2) % 4, 3 - z]

    def here(device):
        return {"tp": device}

    barrier = pltpu.get_barrier_semaphore()

    @pl.loop(1, TP)
    def _(step):
        pl.semaphore_signal(barrier, inc=1, device_id=here((me + step) % TP), device_id_type=MESH)

    loads = []
    for piece in range(4):
        rows = pl.ds(256 * piece, 256)
        loads.append([
            pltpu.make_async_copy(gate_hbm.at[rows], gate_codes.at[rows], load_sem.at[piece]),
            pltpu.make_async_copy(up_hbm.at[rows], up_codes.at[rows], load_sem.at[4 + piece]),
        ])
        for copy in loads[-1]:
            copy.start()
    factor_load = pltpu.make_async_copy(factor_hbm, factor, load_sem.at[8])
    factor_load.start()
    down_load = pltpu.make_async_copy(down_hbm, down_codes, load_sem.at[9])
    down_load.start()

    order = field_order()

    def column(shift):
        return (x + shift) % 4

    def columns(block):
        return pl.ds(pl.multiple_of(block * 128, 128), 128)

    tok[:, columns(me)] = jnp.dot(tok_in[...], order, preferred_element_type=F32).astype(BF16)

    def spread_scales(source, spread, groups):
        scales = source[...].astype(F32)
        for group in range(groups):
            spread[group] = jnp.broadcast_to(scales[group : group + 1], spread.shape[1:])

    def decode_piece(piece):
        if piece % 2 == 0:
            for copy in loads[piece // 2]:
                copy.wait()

        @pl.loop(4 * piece, 4 * piece + 4)
        def _(group):
            rows = pl.ds(pl.multiple_of(group * 32, 32), 32)
            for tile in range(TILES):
                cols = pl.ds(128 * tile, 128)
                for place, codes, scales in ((0, gate_codes, gate_f32), (128, up_codes, up_f32)):
                    planes = decode(codes[rows, cols], scales[group, :, cols])
                    for field, plane in enumerate(planes):
                        to = pl.ds(pl.multiple_of(group * 128 + 32 * field, 32), 32)
                        w_both[tile, to, pl.ds(place, 128)] = plane

    spread_scales(gate_scales, gate_f32, 32)
    spread_scales(up_scales, up_f32, 32)
    decode_piece(0)

    pl.semaphore_wait(barrier, TP - 1)

    waiting = []

    def remote(src, dst, send, recv, device):
        copy = pltpu.make_async_remote_copy(
            src_ref=src, dst_ref=dst, send_sem=send, recv_sem=recv, device_id=device, device_id_type=MESH,
        )
        copy.start()
        waiting.append(copy)
        return copy

    def rows_of(chunk, part):
        if part is None:
            return pl.ds(chunk * CR, CR)
        return pl.ds(chunk * CR + part * HALF, HALF)

    def slot(chunk, block, part):
        return tok_recv.at[chunk, block, part or 0]

    def pass_on(chunk, block, device, part=None):
        where = tok.at[rows_of(chunk, part), columns(block)]
        remote(where, where, tok_send.at[len(waiting)], slot(chunk, block, part), here(device))

    def arrived(chunk, block, part=None):
        where = tok.at[rows_of(chunk, part), columns(block)]
        pltpu.make_async_copy(where, where, slot(chunk, block, part)).wait()

    def at(near, shift):
        return z_of[near] * 8 + ((x + shift) % 4) * 2 + c

    def send_own(chunk):
        for near in (1, 2, 3):
            pass_on(chunk, me, at(near, 0))

    def from_z(chunk, near):
        block = at(near, 0)
        if near:
            arrived(chunk, block)
        pass_on(chunk, block, right)
        pass_on(chunk, block, left)
        pass_on(chunk, block, other)

    def from_x(chunk, near):
        block = at(near, 3)
        arrived(chunk, block)
        pass_on(chunk, block, right, 0)
        pass_on(chunk, block, other)
        block = at(near, 1)
        arrived(chunk, block)
        pass_on(chunk, block, left, 1)
        pass_on(chunk, block, other)

    def from_far(chunk, near):
        block = at(near, 2)
        arrived(chunk, block, 0)
        arrived(chunk, block, 1)
        pass_on(chunk, block, other)

    def from_core(chunk):
        @pl.loop(0, TP // 2)
        def _(chip):
            arrived(chunk, chip * 2 + 1 - c)

    def gate_up(chunk, first, stop):
        for tile in range(first, stop):
            rows = rows_of(chunk, None)
            both = jnp.dot(tok[rows, :], w_both[tile], preferred_element_type=F32)
            gate, up = both[:, :128], both[:, 128:]
            value = gate / (1.0 + jnp.exp(-gate)) * up
            hidden[pl.ds(8 * chunk, 8), :, pl.ds(128 * tile, 128)] = value.astype(BF16).reshape(8, 16, 128)

    group_cols = [pl.ds(0, 256), pl.ds(256, 256), pl.ds(512, 256), pl.ds(768, 128)]
    group_width = [256, 256, 256, 128]

    row_tile = z * 2 + x // 2

    def scatter(chunk, group):
        side, lanes = group % 2, pl.ds(0, group_width[group])
        parity = (group // 2 + chunk) % 2

        def give(step):
            dz, half = (z + 1 + step // 2) % 4, (x // 2 + step) % 2
            device, tile = dz * 8 + (parity + 2 * half) * 2 + side, chunk * 8 + dz * 2 + half
            pltpu.make_async_remote_copy(
                src_ref=hidden.at[tile, :, group_cols[group]], dst_ref=had_in.at[chunk, me, :, lanes],
                send_sem=a_send.at[group], recv_sem=a_recv.at[chunk],
                device_id=here(device), device_id_type=MESH,
            ).start()

        for step in range(6):
            give(step)
        give(7)
        own = jnp.logical_and(c == side, x % 2 == parity)

        @pl.when(own)
        def _():
            pltpu.make_async_copy(
                hidden.at[chunk * 8 + row_tile, :, group_cols[group]], had_in.at[chunk, me, :, lanes],
                a_recv.at[chunk],
            ).start()

        @pl.when(jnp.logical_not(own))
        def _():
            give(6)

    def my_group(chunk):
        return 2 * ((x + chunk) % 2) + c

    def rotate_part(chunk, width, to_cols):
        lanes = pl.ds(0, width)
        everything = had_in.at[chunk, :, :, lanes]
        pltpu.make_async_copy(everything, everything, a_recv.at[chunk]).wait()
        for tile in range(width // 128):
            cols = pl.ds(128 * tile, 128)
            held = [had_in[chunk, source, :, cols].astype(F32) * (1.0 / TP) for source in range(TP)]
            apart = 1
            while apart < TP:
                held = [
                    held[i - apart] - held[i] if i & apart else held[i] + held[i + apart]
                    for i in range(TP)
                ]
                apart *= 2
            for target in range(TP):
                had_out[chunk, target, :, cols] = held[target].astype(BF16)

        @pl.loop(1, TP)
        def _(step):
            device = (me + 1 + (step + 6) % (TP - 1)) % TP
            pltpu.make_async_remote_copy(
                src_ref=had_out.at[chunk, device, :, lanes], dst_ref=rotated.at[chunk * 8 + row_tile, :, to_cols],
                send_sem=b_send.at[chunk], recv_sem=b_recv.at[chunk],
                device_id=here(device), device_id_type=MESH,
            ).start()

        pltpu.make_async_copy(
            had_out.at[chunk, me, :, lanes], rotated.at[chunk * 8 + row_tile, :, to_cols], b_recv.at[chunk]
        ).start()

    def rotate(chunk):
        group = my_group(chunk)

        @pl.when(group < 3)
        def _():
            rotate_part(chunk, 256, pl.ds(pl.multiple_of(group * 256, 256), 256))

        @pl.when(group == 3)
        def _():
            rotate_part(chunk, 128, group_cols[3])

    def turn(chunk):
        tiles = pl.ds(8 * chunk, 8)
        everything = rotated.at[tiles]
        pltpu.make_async_copy(everything, everything, b_recv.at[chunk]).wait()
        value = jnp.dot(rotated[tiles].reshape(CR, UNITS), ordered[...], preferred_element_type=F32)
        turned[pl.ds(chunk * CR, CR), :] = (value * math.sqrt(TP)).astype(BF16)

    def decode_down(first, stop):
        @pl.loop(first, stop)
        def _(place):
            for group in range(TILES):
                for side in range(2):
                    cols = pl.ds(pl.multiple_of(place * 256 + 128 * side, 128), 128)
                    planes = decode(down_codes[pl.ds(32 * group, 32), cols], down_f32[group, :, cols])
                    for field, plane_of in enumerate(planes):
                        to = pl.ds(pl.multiple_of((place // 4) * 256 + 128 * side, 128), 128)
                        w_down[place % 4, pl.ds(128 * group + 32 * field, 32), to] = plane_of

    from_other = {}

    def down(chunk, shift):
        place = column(shift)
        for pair in range(2):
            both = jnp.dot(
                turned[pl.ds(chunk * CR, CR), :], w_down[place, :, pl.ds(512 * pair, 512)],
                preferred_element_type=F32,
            ).astype(BF16)
            for z_at in range(2):
                for side in range(2):
                    lanes = slice(256 * z_at + 128 * side, 256 * z_at + 128 * side + 128)
                    part[chunk, side, place, 2 * pair + z_at] = both[:, lanes]
        from_other[chunk, shift] = remote(
            part.at[chunk, 1 - c, place], core_in.at[chunk, shift],
            c_send.at[chunk, shift], c_recv.at[chunk, shift], here(other),
        )

    top, bottom = pl.ds(0, HALF), pl.ds(HALF, HALF)

    def join(chunk, shift, rows):
        return part[chunk, c, column(shift), :, rows].astype(F32) + core_in[chunk, shift, :, rows].astype(F32)

    x_copies = {}

    def x_first(chunk):
        from_other[chunk, 2].wait_recv()
        sums[chunk, 2] = join(chunk, 2, pl.ds(0, CR)).astype(BF16)
        x_copies[chunk, "r1"] = remote(
            sums.at[chunk, 2, :, top], first_in.at[chunk, 0], x_send.at[chunk, 0], x_recv.at[chunk, 0], here(right)
        )
        x_copies[chunk, "l1"] = remote(
            sums.at[chunk, 2, :, bottom], first_in.at[chunk, 1], x_send.at[chunk, 1], x_recv.at[chunk, 1], here(left)
        )

    def x_second(chunk):
        from_other[chunk, 1].wait_recv()
        sums[chunk, 1, :, bottom] = join(chunk, 1, bottom).astype(BF16)
        x_copies[chunk, "r1"].wait_recv()
        sums[chunk, 1, :, top] = (join(chunk, 1, top) + first_in[chunk, 0].astype(F32)).astype(BF16)
        x_copies[chunk, "r2"] = remote(
            sums.at[chunk, 1], second_in.at[chunk, 0], y_send.at[chunk, 0], y_recv.at[chunk, 0], here(right)
        )
        from_other[chunk, 3].wait_recv()
        sums[chunk, 3, :, top] = join(chunk, 3, top).astype(BF16)
        x_copies[chunk, "l1"].wait_recv()
        sums[chunk, 3, :, bottom] = (join(chunk, 3, bottom) + first_in[chunk, 1].astype(F32)).astype(BF16)
        x_copies[chunk, "l2"] = remote(
            sums.at[chunk, 3], second_in.at[chunk, 1], y_send.at[chunk, 1], y_recv.at[chunk, 1], here(left)
        )

    z_copies = {}

    def z_first(chunk):
        from_other[chunk, 0].wait_recv()
        x_copies[chunk, "r2"].wait_recv()
        x_copies[chunk, "l2"].wait_recv()
        for near in (3, 2, 1, 0):
            to = z_of[near]
            value = (
                part[chunk, c, x, to].astype(F32) + core_in[chunk, 0, to].astype(F32)
                + second_in[chunk, 0, to].astype(F32) + second_in[chunk, 1, to].astype(F32)
            )
            mixed[chunk, near] = value.astype(BF16)
            if near:
                z_copies[chunk, near] = remote(
                    mixed.at[chunk, near], z_in.at[chunk, near], z_send.at[chunk, near], z_recv.at[chunk, near],
                    here(to * 8 + x * 2 + c),
                )

    def z_last(chunk):
        value = mixed[chunk, 0].astype(F32)
        for near in (1, 2, 3):
            z_copies[chunk, near].wait_recv()
            value = value + z_in[chunk, near].astype(F32)
        out_ref[pl.ds(chunk * CR, CR), :] = value.astype(BF16)

    send_own(0)
    from_z(0, 0)
    decode_piece(1)
    from_z(0, 1)
    from_x(0, 0)
    send_own(1)
    decode_piece(2)
    from_z(0, 2)
    from_x(0, 1)
    from_far(0, 0)
    decode_piece(3)
    from_z(0, 3)
    from_x(0, 2)
    from_far(0, 1)
    decode_piece(4)
    from_x(0, 3)
    from_far(0, 2)
    from_z(1, 0)
    decode_piece(5)
    from_far(0, 3)
    from_z(1, 1)
    decode_piece(6)
    from_z(1, 2)
    from_x(1, 0)
    decode_piece(7)
    from_z(1, 3)
    from_x(1, 1)
    from_core(0)
    gate_up(0, 0, 2)
    scatter(0, 0)
    from_x(1, 2)
    from_far(1, 0)
    gate_up(0, 2, 4)
    scatter(0, 1)
    from_x(1, 3)
    from_far(1, 1)
    gate_up(0, 4, 6)
    scatter(0, 2)
    from_far(1, 2)
    gate_up(0, 6, 7)
    scatter(0, 3)
    from_far(1, 3)
    from_core(1)
    for group in range(4):
        gate_up(1, 2 * group, min(2 * group + 2, TILES))
        scatter(1, group)
    rotate(0)
    spread_scales(down_scales, down_f32, 7)
    factor_load.wait()
    for tile in range(TILES):
        cols = pl.ds(128 * tile, 128)
        ordered[:, cols] = jnp.dot(factor[:, cols], order, preferred_element_type=F32).astype(BF16)
    down_load.wait()
    decode_down(0, 16)
    rotate(1)
    turn(0)
    down(0, 2)
    down(0, 1)
    x_first(0)
    down(0, 3)
    down(0, 0)
    x_second(0)
    turn(1)
    down(1, 2)
    down(1, 1)
    x_first(1)
    down(1, 3)
    down(1, 0)
    z_first(0)
    x_second(1)
    z_last(0)
    z_first(1)
    z_last(1)

    for copy in waiting:
        copy.wait_send()
    for group in range(4):
        for kept in range(2):
            @pl.when((c == group % 2) if kept else (c != group % 2))
            def _():
                sent = hidden.at[pl.ds(0, 16 - kept), :, group_cols[group]]
                pltpu.make_async_copy(sent, sent, a_send.at[group]).wait()
    for chunk in range(CHUNKS):
        for width in (256, 128):
            @pl.when((my_group(chunk) == 3) if width == 128 else (my_group(chunk) < 3))
            def _():
                sent = had_out.at[chunk, pl.ds(0, TP - 1), :, pl.ds(0, width)]
                pltpu.make_async_copy(sent, sent, b_send.at[chunk]).wait()


def shards(tokens, gate_codes, gate_scales, up_codes, up_scales, local_factor, down_codes, down_scales):
    vmem, hbm, dma = pl.BlockSpec(memory_space=pltpu.VMEM), pl.BlockSpec(memory_space=pl.ANY), pltpu.SemaphoreType.DMA
    return pl.pallas_call(
        kernel,
        out_shape=jax.ShapeDtypeStruct((ROWS, 128), BF16),
        in_specs=[vmem] * 4 + [hbm] * 4,
        out_specs=vmem,
        scratch_shapes=[
            pltpu.VMEM((1024, UNITS), jnp.int32),
            pltpu.VMEM((1024, UNITS), jnp.int32),
            pltpu.VMEM((224, 4096), jnp.int32),
            pltpu.VMEM((UNITS, UNITS), BF16),
            pltpu.VMEM((ROWS, 4096), BF16),
            pltpu.VMEM((TILES, 4096, 256), BF16),
            pltpu.VMEM((4, UNITS, 1024), BF16),
            pltpu.VMEM((UNITS, UNITS), BF16),
            pltpu.VMEM((32, 8, UNITS), F32),
            pltpu.VMEM((32, 8, UNITS), F32),
            pltpu.VMEM((7, 8, 4096), F32),
            pltpu.VMEM((16, 16, UNITS), BF16),
            pltpu.VMEM((2, TP, 16, 256), BF16),
            pltpu.VMEM((2, TP, 16, 256), BF16),
            pltpu.VMEM((16, 16, UNITS), BF16),
            pltpu.VMEM((ROWS, UNITS), BF16),
            pltpu.VMEM((CHUNKS, 2, 4, 4, CR, 128), BF16),
            pltpu.VMEM((CHUNKS, 4, 4, CR, 128), BF16),
            pltpu.VMEM((CHUNKS, 4, 4, CR, 128), BF16),
            pltpu.VMEM((CHUNKS, 2, 4, HALF, 128), BF16),
            pltpu.VMEM((CHUNKS, 2, 4, CR, 128), BF16),
            pltpu.VMEM((CHUNKS, 4, CR, 128), BF16),
            pltpu.VMEM((CHUNKS, 4, CR, 128), BF16),
            dma((10,)),
            dma((96,)),
            dma((CHUNKS, TP, 2)),
            dma((4,)),
            dma((CHUNKS,)),
            dma((CHUNKS,)),
            dma((CHUNKS,)),
            dma((CHUNKS, 4)),
            dma((CHUNKS, 4)),
            dma((CHUNKS, 2)),
            dma((CHUNKS, 2)),
            dma((CHUNKS, 2)),
            dma((CHUNKS, 2)),
            dma((CHUNKS, 4)),
            dma((CHUNKS, 4)),
        ],
        compiler_params=pltpu.CompilerParams(
            collective_id=0, has_side_effects=True, vmem_limit_bytes=58 * 1024 * 1024
        ),
        name="feed_forward",
    )(tokens, gate_scales, up_scales, down_scales, gate_codes, up_codes, local_factor, down_codes)


def solution(mesh):
    return jax.shard_map(
        shards,
        mesh=mesh,
        in_specs=(
            P("req", "tp"),
            P(None, "tp"),
            P(None, "tp"),
            P(None, "tp"),
            P(None, "tp"),
            P(),
            P("tp", None),
            P("tp", None),
        ),
        out_specs=P("req", "tp"),
        check_vma=False,
    )
```

```python
import functools
import math

import jax
import jax.numpy as jnp
from jax import lax
from jax.experimental import pallas as pl
from jax.experimental.pallas import tpu as pltpu
from jax.sharding import PartitionSpec as P

MESH = pl.DeviceIdType.MESH
TP = 32
ROWS = 256
UNITS = 896
TILES = 7
CHUNKS = 2
CR = ROWS // CHUNKS
HALF = CR // 2
F32 = jnp.float32
BF16 = jnp.bfloat16


def field_order():
    source = lax.broadcasted_iota(jnp.int32, (128, 128), 0)
    target = lax.broadcasted_iota(jnp.int32, (128, 128), 1)
    return jnp.where(target == (source % 4) * 32 + source // 4, 1.0, 0.0).astype(BF16)


def decode(words, scale):
    flipped = jnp.bitwise_xor(words, 0x0888)
    planes = []
    for field in range(4):
        if field == 3:
            value = jnp.right_shift(words, 12)
        else:
            value = jnp.right_shift(jnp.left_shift(flipped, 28 - 4 * field), 28)
        scaled = value.astype(F32).reshape(4, 8, 128) * scale
        planes.append(scaled.reshape(32, 128).astype(BF16))
    return planes


def kernel(
    tok_in, gate_scales, up_scales, down_scales, gate_hbm, up_hbm, factor_hbm, down_hbm, out_ref,
    gate_codes, up_codes, down_codes, factor, tok, w_both, w_down, ordered, gate_f32, up_f32, down_f32, total,
    hidden, had_in, had_out, rotated, turned, part, core_in, sums, first_in, second_in, mixed, z_in,
    load_sem, tok_send, tok_recv, a_send, a_recv, b_send, b_recv, c_send, c_recv, x_send, x_recv,
    y_send, y_recv, z_send, z_recv,
):
    me = lax.axis_index("tp")
    z, x, c = me // 8, (me // 2) % 4, me % 2
    other = me + 1 - 2 * c
    right = z * 8 + ((x + 1) % 4) * 2 + c
    left = z * 8 + ((x + 3) % 4) * 2 + c
    z_of = [z, z + 1 - 2 * (z % 2), (z + 2) % 4, 3 - z]

    barrier = pltpu.get_barrier_semaphore()

    @pl.loop(1, TP)
    def _(step):
        pl.semaphore_signal(barrier, inc=1, device_id={"tp": (me + step) % TP}, device_id_type=MESH)

    def column(shift):
        return (x + shift) % 4

    def code_rows(shift, z_at):
        return pl.ds(pl.multiple_of((z_at * 4 + column(shift)) * 64, 64), 64)

    loads = {}
    for place, shift in enumerate((0, 1, 3, 2)):
        for z_at in range(4):
            rows = code_rows(shift, z_at)
            first = (place * 4 + z_at) * 2
            loads[shift, z_at] = [
                pltpu.make_async_copy(gate_hbm.at[rows], gate_codes.at[rows], load_sem.at[first]),
                pltpu.make_async_copy(up_hbm.at[rows], up_codes.at[rows], load_sem.at[first + 1]),
            ]
            for copy in loads[shift, z_at]:
                copy.start()
    factor_load = pltpu.make_async_copy(factor_hbm, factor, load_sem.at[32])
    factor_load.start()
    down_load = pltpu.make_async_copy(down_hbm, down_codes, load_sem.at[33])
    down_load.start()

    order = field_order()

    def tokens_of(block, row, count):
        lanes = pl.ds(pl.multiple_of((block // 8) * 256 + (block % 2) * 128, 128), 128)
        return tok.at[(block // 2) % 4, pl.ds(row, count), lanes]

    tokens_of(me, 0, ROWS)[...] = jnp.dot(tok_in[...], order, preferred_element_type=F32).astype(BF16)

    pl.semaphore_wait(barrier, TP - 1)

    waiting = []

    def remote(src, dst, send, recv, device):
        copy = pltpu.make_async_remote_copy(
            src_ref=src, dst_ref=dst, send_sem=send, recv_sem=recv,
            device_id={"tp": device}, device_id_type=MESH,
        )
        copy.start()
        waiting.append(copy)
        return copy

    def pass_on(block, device, row=0, count=ROWS):
        where = tokens_of(block, row, count)
        remote(where, where, tok_send.at[len(waiting)], tok_recv.at[block, 1 if row else 0], device)

    def arrived(block, row=0, count=ROWS):
        where = tokens_of(block, row, count)
        pltpu.make_async_copy(where, where, tok_recv.at[block, 1 if row else 0]).wait()

    def at(near, shift):
        return z_of[near] * 8 + column(shift) * 2 + c

    def from_z(near):
        if near:
            arrived(at(near, 0))
        pass_on(at(near, 0), right)
        pass_on(at(near, 0), left)
        if not near:
            for peer in (1, 2, 3):
                pass_on(me, at(peer, 0))
        pass_on(at(near, 0), other)

    def from_x(near):
        block = at(near, 3)
        arrived(block)
        pass_on(block, right, 0, ROWS // 2)
        pass_on(block, other)
        block = at(near, 1)
        arrived(block)
        pass_on(block, left, ROWS // 2, ROWS // 2)
        pass_on(block, other)

    def from_far(near):
        block = at(near, 2)
        arrived(block, 0, ROWS // 2)
        arrived(block, ROWS // 2, ROWS // 2)
        pass_on(block, other)

    def from_core(shift):
        for z_at in range(4):
            arrived(z_at * 8 + column(shift) * 2 + 1 - c)

    def decode_piece(shift, z_at):
        for copy in loads[shift, z_at]:
            copy.wait()

        @pl.loop(0, 2)
        def _(side):
            group = (z_at * 4 + column(shift)) * 2 + side
            rows = pl.ds(pl.multiple_of(group * 32, 32), 32)
            for place, codes, scales in ((0, gate_codes, gate_f32), (128, up_codes, up_f32)):
                words = [codes[rows, pl.ds(128 * tile, 128)] for tile in range(TILES)]
                factors = [scales[group, :, pl.ds(128 * tile, 128)] for tile in range(TILES)]
                for tile in range(TILES):
                    for field, plane in enumerate(decode(words[tile], factors[tile])):
                        to = pl.ds(pl.multiple_of(z_at * 256 + side * 128 + 32 * field, 32), 32)
                        w_both[column(shift), tile, to, pl.ds(place, 128)] = plane

    def product(shift, tile):
        return jnp.dot(tok[column(shift)], w_both[column(shift), tile], preferred_element_type=F32)

    chip = me // 2
    wide, narrow = pl.ds(0, 256), pl.ds(0, 128)
    group_cols = [pl.ds(0, 256), pl.ds(256, 256), pl.ds(512, 256), pl.ds(768, 128)]
    group_width = [256, 256, 256, 128]

    def scatter(group):
        side, lanes = group % 2, pl.ds(0, group_width[group])

        def give(to_chip):
            pltpu.make_async_remote_copy(
                src_ref=hidden.at[to_chip, :, group_cols[group]], dst_ref=had_in.at[group // 2, me, :, lanes],
                send_sem=a_send.at[group], recv_sem=a_recv.at[group // 2],
                device_id={"tp": to_chip * 2 + side}, device_id_type=MESH,
            ).start()

        @pl.loop(1, 16)
        def _(step):
            give((chip + 1 + (step + 2) % 15) % 16)

        @pl.when(c == side)
        def _():
            pltpu.make_async_copy(
                hidden.at[chip, :, group_cols[group]], had_in.at[group // 2, me, :, lanes], a_recv.at[group // 2]
            ).start()

        @pl.when(c != side)
        def _():
            give(chip)

    def rotate(group):
        turn, lanes = group // 2, pl.ds(0, group_width[group])
        everything = had_in.at[turn, :, :, lanes]
        pltpu.make_async_copy(everything, everything, a_recv.at[turn]).wait()
        for tile in range(group_width[group] // 128):
            cols = pl.ds(128 * tile, 128)
            held = [had_in[turn, source, :, cols].astype(F32) * (1.0 / TP) for source in range(TP)]
            apart = 1
            while apart < TP:
                held = [
                    held[i - apart] - held[i] if i & apart else held[i] + held[i + apart]
                    for i in range(TP)
                ]
                apart *= 2
            for target in range(TP):
                had_out[turn, target, :, cols] = held[target].astype(BF16)

        @pl.loop(1, TP)
        def _(step):
            device = (me + 1 + (step + 6) % (TP - 1)) % TP
            pltpu.make_async_remote_copy(
                src_ref=had_out.at[turn, device, :, lanes], dst_ref=rotated.at[chip, :, group_cols[group]],
                send_sem=b_send.at[turn], recv_sem=b_recv.at[group],
                device_id={"tp": device}, device_id_type=MESH,
            ).start()

        pltpu.make_async_copy(
            had_out.at[turn, me, :, lanes], rotated.at[chip, :, group_cols[group]], b_recv.at[group]
        ).start()

    def rotate_turn(turn):
        for side in range(2):
            @pl.when(c == side)
            def _():
                rotate(2 * turn + side)

    def back(group):
        everything = rotated.at[:, :, group_cols[group]]
        pltpu.make_async_copy(everything, everything, b_recv.at[group]).wait()

    def decode_down(first, stop):
        @pl.loop(first, stop)
        def _(place):
            for side in range(2):
                cols = pl.ds(pl.multiple_of(place * 256 + 128 * side, 128), 128)
                to = pl.ds(pl.multiple_of((place // 4) * 256 + 128 * side, 128), 128)
                words = [down_codes[pl.ds(32 * group, 32), cols] for group in range(TILES)]
                factors = [down_f32[group, :, cols] for group in range(TILES)]
                for group in range(TILES):
                    for field, plane in enumerate(decode(words[group], factors[group])):
                        w_down[place % 4, pl.ds(128 * group + 32 * field, 32), to] = plane

    from_other = {}

    def down(shift):
        place = column(shift)
        for pair in range(2):
            both = jnp.dot(
                turned[...], w_down[place, :, pl.ds(512 * pair, 512)], preferred_element_type=F32
            ).astype(BF16)
            for chunk in range(CHUNKS):
                rows = slice(chunk * CR, (chunk + 1) * CR)
                for z_at in range(2):
                    for side in range(2):
                        lanes = slice(256 * z_at + 128 * side, 256 * z_at + 128 * side + 128)
                        part[chunk, side, place, 2 * pair + z_at] = both[rows, lanes]
        for chunk in range(CHUNKS):
            from_other[chunk, shift] = remote(
                part.at[chunk, 1 - c, place], core_in.at[chunk, shift],
                c_send.at[chunk, shift], c_recv.at[chunk, shift], other,
            )

    top, bottom = pl.ds(0, HALF), pl.ds(HALF, HALF)

    def join(chunk, shift, rows):
        return part[chunk, c, column(shift), :, rows].astype(F32) + core_in[chunk, shift, :, rows].astype(F32)

    x_copies = {}

    def x_first(chunk):
        from_other[chunk, 2].wait_recv()
        sums[chunk, 2] = join(chunk, 2, pl.ds(0, CR)).astype(BF16)
        x_copies[chunk, "r1"] = remote(
            sums.at[chunk, 2, :, top], first_in.at[chunk, 0], x_send.at[chunk, 0], x_recv.at[chunk, 0], right
        )
        x_copies[chunk, "l1"] = remote(
            sums.at[chunk, 2, :, bottom], first_in.at[chunk, 1], x_send.at[chunk, 1], x_recv.at[chunk, 1], left
        )

    def x_second(chunk):
        from_other[chunk, 1].wait_recv()
        sums[chunk, 1, :, bottom] = join(chunk, 1, bottom).astype(BF16)
        x_copies[chunk, "r1"].wait_recv()
        sums[chunk, 1, :, top] = (join(chunk, 1, top) + first_in[chunk, 0].astype(F32)).astype(BF16)
        x_copies[chunk, "r2"] = remote(
            sums.at[chunk, 1], second_in.at[chunk, 0], y_send.at[chunk, 0], y_recv.at[chunk, 0], right
        )
        from_other[chunk, 3].wait_recv()
        sums[chunk, 3, :, top] = join(chunk, 3, top).astype(BF16)
        x_copies[chunk, "l1"].wait_recv()
        sums[chunk, 3, :, bottom] = (join(chunk, 3, bottom) + first_in[chunk, 1].astype(F32)).astype(BF16)
        x_copies[chunk, "l2"] = remote(
            sums.at[chunk, 3], second_in.at[chunk, 1], y_send.at[chunk, 1], y_recv.at[chunk, 1], left
        )

    z_copies = {}

    def z_first(chunk):
        from_other[chunk, 0].wait_recv()
        x_copies[chunk, "r2"].wait_recv()
        x_copies[chunk, "l2"].wait_recv()
        for near in (3, 2, 1, 0):
            to = z_of[near]
            value = (
                part[chunk, c, x, to].astype(F32) + core_in[chunk, 0, to].astype(F32)
                + second_in[chunk, 0, to].astype(F32) + second_in[chunk, 1, to].astype(F32)
            )
            mixed[chunk, near] = value.astype(BF16)
            if near:
                z_copies[chunk, near] = remote(
                    mixed.at[chunk, near], z_in.at[chunk, near], z_send.at[chunk, near], z_recv.at[chunk, near],
                    to * 8 + x * 2 + c,
                )

    def z_last(chunk):
        total = mixed[chunk, 0].astype(F32)
        for near in (1, 2, 3):
            z_copies[chunk, near].wait_recv()
            total = total + z_in[chunk, near].astype(F32)
        out_ref[pl.ds(chunk * CR, CR), :] = total.astype(BF16)

    from_z(0)
    for source, spread, groups in ((gate_scales, gate_f32, 32), (up_scales, up_f32, 32), (down_scales, down_f32, 7)):
        scales = source[...].astype(F32)
        for group in range(groups):
            spread[group] = jnp.broadcast_to(scales[group : group + 1], spread.shape[1:])
    for z_at in range(4):
        decode_piece(0, z_at)
    from_z(1)
    from_x(0)
    decode_piece(1, 0)
    decode_piece(1, 1)
    from_z(2)
    from_x(1)
    decode_piece(1, 2)
    decode_piece(1, 3)
    from_z(3)
    from_x(2)
    from_far(0)
    decode_piece(3, 0)
    decode_piece(3, 1)
    from_far(1)
    from_x(3)
    decode_piece(3, 2)
    decode_piece(3, 3)
    from_far(2)
    from_core(0)

    @pl.loop(0, TILES)
    def _(tile):
        total[tile] = product(0, tile)

    from_far(3)
    for z_at in range(4):
        decode_piece(2, z_at)
    factor_load.wait()
    for tile in range(TILES):
        cols = pl.ds(128 * tile, 128)
        ordered[:, cols] = jnp.dot(factor[:, cols], order, preferred_element_type=F32).astype(BF16)
    from_core(1)
    from_core(3)

    @pl.loop(0, TILES)
    def _(tile):
        total[tile] += product(1, tile) + product(3, tile)

    from_core(2)
    for group in range(4):
        @pl.loop(2 * group, min(2 * group + 2, TILES))
        def _(tile):
            both = total[tile] + product(2, tile)
            gate, up = both[:, :128], both[:, 128:]
            value = gate / (1.0 + jnp.exp(-gate)) * up
            lanes = pl.ds(pl.multiple_of(tile * 128, 128), 128)
            hidden[:, :, lanes] = value.astype(BF16).reshape(16, 16, 128)

        scatter(group)

    down_load.wait()
    decode_down(0, 8)
    rotate_turn(0)
    decode_down(8, 16)
    rotate_turn(1)
    back(0)
    back(1)
    first_part = jnp.dot(
        rotated[:, :, pl.ds(0, 512)].reshape(ROWS, 512), ordered[pl.ds(0, 512), :], preferred_element_type=F32
    )
    back(2)
    back(3)
    whole = first_part + jnp.dot(
        rotated[:, :, pl.ds(512, 384)].reshape(ROWS, 384), ordered[pl.ds(512, 384), :], preferred_element_type=F32
    )
    turned[...] = (whole * math.sqrt(TP)).astype(BF16)
    down(2)
    down(1)
    x_first(0)
    x_first(1)
    down(3)
    down(0)
    x_second(0)
    x_second(1)
    z_first(0)
    z_first(1)
    z_last(0)
    z_last(1)

    for copy in waiting:
        copy.wait_send()
    for group in range(4):
        for kept in range(2):
            @pl.when((c == group % 2) if kept else (c != group % 2))
            def _():
                sent = hidden.at[pl.ds(0, 16 - kept), :, group_cols[group]]
                pltpu.make_async_copy(sent, sent, a_send.at[group]).wait()
                if kept:
                    sent = had_out.at[group // 2, pl.ds(0, TP - 1), :, pl.ds(0, group_width[group])]
                    pltpu.make_async_copy(sent, sent, b_send.at[group // 2]).wait()


def shards(tokens, gate_codes, gate_scales, up_codes, up_scales, local_factor, down_codes, down_scales):
    vmem, hbm, dma = pl.BlockSpec(memory_space=pltpu.VMEM), pl.BlockSpec(memory_space=pl.ANY), pltpu.SemaphoreType.DMA
    return pl.pallas_call(
        kernel,
        out_shape=jax.ShapeDtypeStruct((ROWS, 128), BF16),
        in_specs=[vmem] * 4 + [hbm] * 4,
        out_specs=vmem,
        scratch_shapes=[
            pltpu.VMEM((1024, UNITS), jnp.int32),
            pltpu.VMEM((1024, UNITS), jnp.int32),
            pltpu.VMEM((224, 4096), jnp.int32),
            pltpu.VMEM((UNITS, UNITS), BF16),
            pltpu.VMEM((4, ROWS, 1024), BF16),
            pltpu.VMEM((4, TILES, 1024, 256), BF16),
            pltpu.VMEM((4, UNITS, 1024), BF16),
            pltpu.VMEM((UNITS, UNITS), BF16),
            pltpu.VMEM((32, 8, UNITS), F32),
            pltpu.VMEM((32, 8, UNITS), F32),
            pltpu.VMEM((7, 8, 4096), F32),
            pltpu.VMEM((TILES, ROWS, 256), F32),
            pltpu.VMEM((16, 16, UNITS), BF16),
            pltpu.VMEM((2, TP, 16, 256), BF16),
            pltpu.VMEM((2, TP, 16, 256), BF16),
            pltpu.VMEM((16, 16, UNITS), BF16),
            pltpu.VMEM((ROWS, UNITS), BF16),
            pltpu.VMEM((CHUNKS, 2, 4, 4, CR, 128), BF16),
            pltpu.VMEM((CHUNKS, 4, 4, CR, 128), BF16),
            pltpu.VMEM((CHUNKS, 4, 4, CR, 128), BF16),
            pltpu.VMEM((CHUNKS, 2, 4, HALF, 128), BF16),
            pltpu.VMEM((CHUNKS, 2, 4, CR, 128), BF16),
            pltpu.VMEM((CHUNKS, 4, CR, 128), BF16),
            pltpu.VMEM((CHUNKS, 4, CR, 128), BF16),
            dma((34,)),
            dma((48,)),
            dma((TP, 2)),
            dma((4,)),
            dma((2,)),
            dma((2,)),
            dma((4,)),
            dma((CHUNKS, 4)),
            dma((CHUNKS, 4)),
            dma((CHUNKS, 2)),
            dma((CHUNKS, 2)),
            dma((CHUNKS, 2)),
            dma((CHUNKS, 2)),
            dma((CHUNKS, 4)),
            dma((CHUNKS, 4)),
        ],
        compiler_params=pltpu.CompilerParams(
            collective_id=0, has_side_effects=True, vmem_limit_bytes=58 * 1024 * 1024
        ),
        name="feed_forward",
    )(tokens, gate_scales, up_scales, down_scales, gate_codes, up_codes, local_factor, down_codes)


def solution(mesh):
    return jax.shard_map(
        shards,
        mesh=mesh,
        in_specs=(
            P("req", "tp"),
            P(None, "tp"),
            P(None, "tp"),
            P(None, "tp"),
            P(None, "tp"),
            P(),
            P("tp", None),
            P("tp", None),
        ),
        out_specs=P("req", "tp"),
        check_vma=False,
    )
```

```python
import functools
import math

import jax
import jax.numpy as jnp
from jax import lax
from jax.experimental import pallas as pl
from jax.experimental.pallas import tpu as pltpu
from jax.sharding import PartitionSpec as P

MESH = pl.DeviceIdType.MESH
TP = 32
ROWS = 256
UNITS = 896
TILES = 7
CHUNKS = 2
CR = ROWS // CHUNKS
HALF = CR // 2
F32 = jnp.float32
BF16 = jnp.bfloat16


def field_order():
    source = lax.broadcasted_iota(jnp.int32, (128, 128), 0)
    target = lax.broadcasted_iota(jnp.int32, (128, 128), 1)
    return jnp.where(target == (source % 4) * 32 + source // 4, 1.0, 0.0).astype(BF16)


def decode(words, scale):
    flipped = jnp.bitwise_xor(words, 0x0888)
    planes = []
    for field in range(4):
        if field == 3:
            value = jnp.right_shift(words, 12)
        else:
            value = jnp.right_shift(jnp.left_shift(flipped, 28 - 4 * field), 28)
        scaled = value.astype(F32).reshape(4, 8, 128) * scale
        planes.append(scaled.reshape(32, 128).astype(BF16))
    return planes


def kernel(
    tok_in, gate_scales, up_scales, down_scales, gate_hbm, up_hbm, factor_hbm, down_hbm, out_ref,
    gate_codes, up_codes, down_codes, factor, tok, w_both, w_down, ordered, gate_f32, up_f32, down_f32, total,
    hidden, had_in, had_out, rotated, turned, part, core_in, sums, first_in, second_in, mixed, z_in,
    load_sem, tok_send, tok_recv, a_send, a_recv, b_send, b_recv, c_send, c_recv, x_send, x_recv,
    y_send, y_recv, z_send, z_recv,
):
    me = lax.axis_index("tp")
    z, x, c = me // 8, (me // 2) % 4, me % 2
    other = me + 1 - 2 * c
    right = z * 8 + ((x + 1) % 4) * 2 + c
    left = z * 8 + ((x + 3) % 4) * 2 + c
    z_of = [z, z + 1 - 2 * (z % 2), (z + 2) % 4, 3 - z]

    barrier = pltpu.get_barrier_semaphore()

    @pl.loop(1, TP)
    def _(step):
        pl.semaphore_signal(barrier, inc=1, device_id={"tp": (me + step) % TP}, device_id_type=MESH)

    def column(shift):
        return (x + shift) % 4

    def code_rows(shift, z_at):
        return pl.ds(pl.multiple_of((z_at * 4 + column(shift)) * 64, 64), 64)

    loads = {}
    for place, shift in enumerate((0, 1, 3, 2)):
        for z_at in range(4):
            rows = code_rows(shift, z_at)
            first = (place * 4 + z_at) * 2
            loads[shift, z_at] = [
                pltpu.make_async_copy(gate_hbm.at[rows], gate_codes.at[rows], load_sem.at[first]),
                pltpu.make_async_copy(up_hbm.at[rows], up_codes.at[rows], load_sem.at[first + 1]),
            ]
            for copy in loads[shift, z_at]:
                copy.start()
    factor_load = pltpu.make_async_copy(factor_hbm, factor, load_sem.at[32])
    factor_load.start()
    down_load = pltpu.make_async_copy(down_hbm, down_codes, load_sem.at[33])
    down_load.start()

    order = field_order()

    def tokens_of(block, row, count):
        lanes = pl.ds(pl.multiple_of((block // 8) * 256 + (block % 2) * 128, 128), 128)
        return tok.at[(block // 2) % 4, pl.ds(row, count), lanes]

    tokens_of(me, 0, ROWS)[...] = jnp.dot(tok_in[...], order, preferred_element_type=F32).astype(BF16)

    pl.semaphore_wait(barrier, TP - 1)

    def spread_scales(source, spread, groups):
        scales = source[...].astype(F32)
        for group in range(groups):
            spread[group] = jnp.broadcast_to(scales[group : group + 1], spread.shape[1:])

    waiting = []

    def remote(src, dst, send, recv, device):
        copy = pltpu.make_async_remote_copy(
            src_ref=src, dst_ref=dst, send_sem=send, recv_sem=recv,
            device_id={"tp": device}, device_id_type=MESH,
        )
        copy.start()
        waiting.append(copy)
        return copy

    def pass_on(block, device, row=0, count=ROWS):
        where = tokens_of(block, row, count)
        remote(where, where, tok_send.at[len(waiting)], tok_recv.at[block, 1 if row else 0], device)

    def arrived(block, row=0, count=ROWS):
        where = tokens_of(block, row, count)
        pltpu.make_async_copy(where, where, tok_recv.at[block, 1 if row else 0]).wait()

    def at(near, shift):
        return z_of[near] * 8 + column(shift) * 2 + c

    def from_z(near):
        if near:
            arrived(at(near, 0))
        pass_on(at(near, 0), right)
        pass_on(at(near, 0), left)
        if not near:
            for peer in (1, 2, 3):
                pass_on(me, at(peer, 0))
        pass_on(at(near, 0), other)

    def from_x(near):
        block = at(near, 3)
        arrived(block)
        pass_on(block, right, 0, ROWS // 2)
        pass_on(block, other)
        block = at(near, 1)
        arrived(block)
        pass_on(block, left, ROWS // 2, ROWS // 2)
        pass_on(block, other)

    def from_far(near):
        block = at(near, 2)
        arrived(block, 0, ROWS // 2)
        arrived(block, ROWS // 2, ROWS // 2)
        pass_on(block, other)

    def from_core(shift):
        for z_at in range(4):
            arrived(z_at * 8 + column(shift) * 2 + 1 - c)

    def decode_piece(shift, z_at):
        for copy in loads[shift, z_at]:
            copy.wait()

        @pl.loop(0, 2)
        def _(side):
            group = (z_at * 4 + column(shift)) * 2 + side
            rows = pl.ds(pl.multiple_of(group * 32, 32), 32)
            for place, codes, scales in ((0, gate_codes, gate_f32), (128, up_codes, up_f32)):
                words = [codes[rows, pl.ds(128 * tile, 128)] for tile in range(TILES)]
                factors = [scales[group, :, pl.ds(128 * tile, 128)] for tile in range(TILES)]
                for tile in range(TILES):
                    for field, plane in enumerate(decode(words[tile], factors[tile])):
                        to = pl.ds(pl.multiple_of(z_at * 256 + side * 128 + 32 * field, 32), 32)
                        w_both[column(shift), to, pl.ds(256 * tile + place, 128)] = plane

    both_cols = [pl.ds(0, 512), pl.ds(512, 512), pl.ds(1024, 512), pl.ds(1536, 256)]

    def product(shift, group):
        return jnp.dot(tok[column(shift)], w_both[column(shift), :, both_cols[group]], preferred_element_type=F32)

    chip = me // 2
    wide, narrow = pl.ds(0, 256), pl.ds(0, 128)
    group_cols = [pl.ds(0, 256), pl.ds(256, 256), pl.ds(512, 256), pl.ds(768, 128)]
    group_width = [256, 256, 256, 128]

    def scatter(group):
        side, lanes = group % 2, pl.ds(0, group_width[group])

        def give(to_chip):
            pltpu.make_async_remote_copy(
                src_ref=hidden.at[to_chip, :, group_cols[group]], dst_ref=had_in.at[group // 2, me, :, lanes],
                send_sem=a_send.at[group], recv_sem=a_recv.at[group // 2],
                device_id={"tp": to_chip * 2 + side}, device_id_type=MESH,
            ).start()

        @pl.loop(1, 16)
        def _(step):
            give((chip + 1 + (step + 2) % 15) % 16)

        @pl.when(c == side)
        def _():
            pltpu.make_async_copy(
                hidden.at[chip, :, group_cols[group]], had_in.at[group // 2, me, :, lanes], a_recv.at[group // 2]
            ).start()

        @pl.when(c != side)
        def _():
            give(chip)

    def rotate(group):
        turn, lanes = group // 2, pl.ds(0, group_width[group])
        everything = had_in.at[turn, :, :, lanes]
        pltpu.make_async_copy(everything, everything, a_recv.at[turn]).wait()
        for tile in range(group_width[group] // 128):
            cols = pl.ds(128 * tile, 128)
            held = [had_in[turn, source, :, cols].astype(F32) * (1.0 / TP) for source in range(TP)]
            apart = 1
            while apart < TP:
                held = [
                    held[i - apart] - held[i] if i & apart else held[i] + held[i + apart]
                    for i in range(TP)
                ]
                apart *= 2
            for target in range(TP):
                had_out[turn, target, :, cols] = held[target].astype(BF16)

        @pl.loop(1, TP)
        def _(step):
            device = (me + 1 + (step + 6) % (TP - 1)) % TP
            pltpu.make_async_remote_copy(
                src_ref=had_out.at[turn, device, :, lanes], dst_ref=rotated.at[chip, :, group_cols[group]],
                send_sem=b_send.at[turn], recv_sem=b_recv.at[group],
                device_id={"tp": device}, device_id_type=MESH,
            ).start()

        pltpu.make_async_copy(
            had_out.at[turn, me, :, lanes], rotated.at[chip, :, group_cols[group]], b_recv.at[group]
        ).start()

    def rotate_turn(turn):
        for side in range(2):
            @pl.when(c == side)
            def _():
                rotate(2 * turn + side)

    def back(group):
        everything = rotated.at[:, :, group_cols[group]]
        pltpu.make_async_copy(everything, everything, b_recv.at[group]).wait()

    def decode_down(first, stop):
        @pl.loop(first, stop)
        def _(place):
            for side in range(2):
                cols = pl.ds(pl.multiple_of(place * 256 + 128 * side, 128), 128)
                to = pl.ds(pl.multiple_of((place // 4) * 256 + 128 * side, 128), 128)
                words = [down_codes[pl.ds(32 * group, 32), cols] for group in range(TILES)]
                factors = [down_f32[group, :, cols] for group in range(TILES)]
                for group in range(TILES):
                    for field, plane in enumerate(decode(words[group], factors[group])):
                        w_down[place % 4, pl.ds(128 * group + 32 * field, 32), to] = plane

    from_other = {}

    def down(shift):
        place = column(shift)
        for pair in range(2):
            both = jnp.dot(
                turned[...], w_down[place, :, pl.ds(512 * pair, 512)], preferred_element_type=F32
            ).astype(BF16)
            for chunk in range(CHUNKS):
                rows = slice(chunk * CR, (chunk + 1) * CR)
                for z_at in range(2):
                    for side in range(2):
                        lanes = slice(256 * z_at + 128 * side, 256 * z_at + 128 * side + 128)
                        part[chunk, side, place, 2 * pair + z_at] = both[rows, lanes]
        for chunk in range(CHUNKS):
            from_other[chunk, shift] = remote(
                part.at[chunk, 1 - c, place], core_in.at[chunk, shift],
                c_send.at[chunk, shift], c_recv.at[chunk, shift], other,
            )

    top, bottom = pl.ds(0, HALF), pl.ds(HALF, HALF)

    def join(chunk, shift, rows):
        return part[chunk, c, column(shift), :, rows].astype(F32) + core_in[chunk, shift, :, rows].astype(F32)

    x_copies = {}

    def x_first(chunk):
        from_other[chunk, 2].wait_recv()
        sums[chunk, 2] = join(chunk, 2, pl.ds(0, CR)).astype(BF16)
        x_copies[chunk, "r1"] = remote(
            sums.at[chunk, 2, :, top], first_in.at[chunk, 0], x_send.at[chunk, 0], x_recv.at[chunk, 0], right
        )
        x_copies[chunk, "l1"] = remote(
            sums.at[chunk, 2, :, bottom], first_in.at[chunk, 1], x_send.at[chunk, 1], x_recv.at[chunk, 1], left
        )

    def x_second(chunk):
        from_other[chunk, 1].wait_recv()
        sums[chunk, 1, :, bottom] = join(chunk, 1, bottom).astype(BF16)
        x_copies[chunk, "r1"].wait_recv()
        sums[chunk, 1, :, top] = (join(chunk, 1, top) + first_in[chunk, 0].astype(F32)).astype(BF16)
        x_copies[chunk, "r2"] = remote(
            sums.at[chunk, 1], second_in.at[chunk, 0], y_send.at[chunk, 0], y_recv.at[chunk, 0], right
        )
        from_other[chunk, 3].wait_recv()
        sums[chunk, 3, :, top] = join(chunk, 3, top).astype(BF16)
        x_copies[chunk, "l1"].wait_recv()
        sums[chunk, 3, :, bottom] = (join(chunk, 3, bottom) + first_in[chunk, 1].astype(F32)).astype(BF16)
        x_copies[chunk, "l2"] = remote(
            sums.at[chunk, 3], second_in.at[chunk, 1], y_send.at[chunk, 1], y_recv.at[chunk, 1], left
        )

    z_copies = {}

    def z_first(chunk):
        from_other[chunk, 0].wait_recv()
        x_copies[chunk, "r2"].wait_recv()
        x_copies[chunk, "l2"].wait_recv()
        for near in (3, 2, 1, 0):
            to = z_of[near]
            value = (
                part[chunk, c, x, to].astype(F32) + core_in[chunk, 0, to].astype(F32)
                + second_in[chunk, 0, to].astype(F32) + second_in[chunk, 1, to].astype(F32)
            )
            mixed[chunk, near] = value.astype(BF16)
            if near:
                z_copies[chunk, near] = remote(
                    mixed.at[chunk, near], z_in.at[chunk, near], z_send.at[chunk, near], z_recv.at[chunk, near],
                    to * 8 + x * 2 + c,
                )

    def z_last(chunk):
        total = mixed[chunk, 0].astype(F32)
        for near in (1, 2, 3):
            z_copies[chunk, near].wait_recv()
            total = total + z_in[chunk, near].astype(F32)
        out_ref[pl.ds(chunk * CR, CR), :] = total.astype(BF16)

    from_z(0)
    spread_scales(gate_scales, gate_f32, 32)
    spread_scales(up_scales, up_f32, 32)
    for z_at in range(4):
        decode_piece(0, z_at)
    from_z(1)
    from_x(0)
    decode_piece(1, 0)
    decode_piece(1, 1)
    from_z(2)
    from_x(1)
    decode_piece(1, 2)
    decode_piece(1, 3)
    from_z(3)
    from_x(2)
    from_far(0)
    decode_piece(3, 0)
    decode_piece(3, 1)
    from_far(1)
    from_x(3)
    decode_piece(3, 2)
    decode_piece(3, 3)
    from_far(2)
    from_core(0)

    for group in range(4):
        total[:, both_cols[group]] = product(0, group)

    from_far(3)
    for z_at in range(4):
        decode_piece(2, z_at)
    from_core(1)
    from_core(3)

    for group in range(4):
        total[:, both_cols[group]] += product(1, group) + product(3, group)

    from_core(2)
    for group in range(4):
        both = total[:, both_cols[group]] + product(2, group)
        for tile in range(2 * group, min(2 * group + 2, TILES)):
            start = 256 * (tile - 2 * group)
            gate, up = both[:, start : start + 128], both[:, start + 128 : start + 256]
            value = gate / (1.0 + jnp.exp(-gate)) * up
            hidden[:, :, pl.ds(128 * tile, 128)] = value.astype(BF16).reshape(16, 16, 128)

        scatter(group)

    factor_load.wait()
    for tile in range(TILES):
        cols = pl.ds(128 * tile, 128)
        ordered[:, cols] = jnp.dot(factor[:, cols], order, preferred_element_type=F32).astype(BF16)
    spread_scales(down_scales, down_f32, 7)
    down_load.wait()
    decode_down(0, 8)
    rotate_turn(0)
    decode_down(8, 16)
    rotate_turn(1)
    back(0)
    back(1)
    first_part = jnp.dot(
        rotated[:, :, pl.ds(0, 512)].reshape(ROWS, 512), ordered[pl.ds(0, 512), :], preferred_element_type=F32
    )
    back(2)
    back(3)
    whole = first_part + jnp.dot(
        rotated[:, :, pl.ds(512, 384)].reshape(ROWS, 384), ordered[pl.ds(512, 384), :], preferred_element_type=F32
    )
    turned[...] = (whole * math.sqrt(TP)).astype(BF16)
    down(2)
    down(1)
    x_first(0)
    x_first(1)
    down(3)
    down(0)
    x_second(0)
    x_second(1)
    z_first(0)
    z_first(1)
    z_last(0)
    z_last(1)

    for copy in waiting:
        copy.wait_send()
    for group in range(4):
        for kept in range(2):
            @pl.when((c == group % 2) if kept else (c != group % 2))
            def _():
                sent = hidden.at[pl.ds(0, 16 - kept), :, group_cols[group]]
                pltpu.make_async_copy(sent, sent, a_send.at[group]).wait()
                if kept:
                    sent = had_out.at[group // 2, pl.ds(0, TP - 1), :, pl.ds(0, group_width[group])]
                    pltpu.make_async_copy(sent, sent, b_send.at[group // 2]).wait()


def shards(tokens, gate_codes, gate_scales, up_codes, up_scales, local_factor, down_codes, down_scales):
    vmem, hbm, dma = pl.BlockSpec(memory_space=pltpu.VMEM), pl.BlockSpec(memory_space=pl.ANY), pltpu.SemaphoreType.DMA
    return pl.pallas_call(
        kernel,
        out_shape=jax.ShapeDtypeStruct((ROWS, 128), BF16),
        in_specs=[vmem] * 4 + [hbm] * 4,
        out_specs=vmem,
        scratch_shapes=[
            pltpu.VMEM((1024, UNITS), jnp.int32),
            pltpu.VMEM((1024, UNITS), jnp.int32),
            pltpu.VMEM((224, 4096), jnp.int32),
            pltpu.VMEM((UNITS, UNITS), BF16),
            pltpu.VMEM((4, ROWS, 1024), BF16),
            pltpu.VMEM((4, 1024, 2 * UNITS), BF16),
            pltpu.VMEM((4, UNITS, 1024), BF16),
            pltpu.VMEM((UNITS, UNITS), BF16),
            pltpu.VMEM((32, 8, UNITS), F32),
            pltpu.VMEM((32, 8, UNITS), F32),
            pltpu.VMEM((7, 8, 4096), F32),
            pltpu.VMEM((ROWS, 2 * UNITS), F32),
            pltpu.VMEM((16, 16, UNITS), BF16),
            pltpu.VMEM((2, TP, 16, 256), BF16),
            pltpu.VMEM((2, TP, 16, 256), BF16),
            pltpu.VMEM((16, 16, UNITS), BF16),
            pltpu.VMEM((ROWS, UNITS), BF16),
            pltpu.VMEM((CHUNKS, 2, 4, 4, CR, 128), BF16),
            pltpu.VMEM((CHUNKS, 4, 4, CR, 128), BF16),
            pltpu.VMEM((CHUNKS, 4, 4, CR, 128), BF16),
            pltpu.VMEM((CHUNKS, 2, 4, HALF, 128), BF16),
            pltpu.VMEM((CHUNKS, 2, 4, CR, 128), BF16),
            pltpu.VMEM((CHUNKS, 4, CR, 128), BF16),
            pltpu.VMEM((CHUNKS, 4, CR, 128), BF16),
            dma((34,)),
            dma((48,)),
            dma((TP, 2)),
            dma((4,)),
            dma((2,)),
            dma((2,)),
            dma((4,)),
            dma((CHUNKS, 4)),
            dma((CHUNKS, 4)),
            dma((CHUNKS, 2)),
            dma((CHUNKS, 2)),
            dma((CHUNKS, 2)),
            dma((CHUNKS, 2)),
            dma((CHUNKS, 4)),
            dma((CHUNKS, 4)),
        ],
        compiler_params=pltpu.CompilerParams(
            collective_id=0, has_side_effects=True, vmem_limit_bytes=58 * 1024 * 1024
        ),
        name="feed_forward",
    )(tokens, gate_scales, up_scales, down_scales, gate_codes, up_codes, local_factor, down_codes)


def solution(mesh):
    return jax.shard_map(
        shards,
        mesh=mesh,
        in_specs=(
            P("req", "tp"),
            P(None, "tp"),
            P(None, "tp"),
            P(None, "tp"),
            P(None, "tp"),
            P(),
            P("tp", None),
            P("tp", None),
        ),
        out_specs=P("req", "tp"),
        check_vma=False,
    )
```

```python
import functools
import math

import jax
import jax.numpy as jnp
from jax import lax
from jax.experimental import pallas as pl
from jax.experimental.pallas import tpu as pltpu
from jax.sharding import PartitionSpec as P

MESH = pl.DeviceIdType.MESH
TP = 32
ROWS = 256
UNITS = 896
TILES = 7
CHUNKS = 2
CR = ROWS // CHUNKS
F32 = jnp.float32
BF16 = jnp.bfloat16


def field_order():
    source = lax.broadcasted_iota(jnp.int32, (128, 128), 0)
    target = lax.broadcasted_iota(jnp.int32, (128, 128), 1)
    return jnp.where(target == (source % 4) * 32 + source // 4, 1.0, 0.0).astype(BF16)


def decode(words, scale):
    flipped = jnp.bitwise_xor(words, 0x0888)
    planes = []
    for field in range(4):
        if field == 3:
            value = jnp.right_shift(words, 12)
        else:
            value = jnp.right_shift(jnp.left_shift(flipped, 28 - 4 * field), 28)
        scaled = value.astype(F32).reshape(4, 8, 128) * scale
        planes.append(scaled.reshape(32, 128).astype(BF16))
    return planes


def kernel(
    tok_in, gate_scales, up_scales, down_scales, gate_hbm, up_hbm, factor_hbm, down_hbm, out_ref,
    gate_codes, up_codes, down_codes, factor, tok, w_both, w_down, ordered, gate_f32, up_f32, down_f32, total,
    hidden, had_in, had_out, rotated, turned, part, core_in, sums, x_in, mixed, z_in,
    load_sem, tok_send, tok_recv, a_send, a_recv, b_send, b_recv, c_send, c_recv, x_send, x_recv, z_send, z_recv,
):
    me = lax.axis_index("tp")
    z, x, c = me // 8, (me // 2) % 4, me % 2
    other = me + 1 - 2 * c
    right = z * 8 + ((x + 1) % 4) * 2 + c
    left = z * 8 + ((x + 3) % 4) * 2 + c
    far = z * 8 + ((x + 2) % 4) * 2 + c
    z_of = [z, z + 1 - 2 * (z % 2), (z + 2) % 4, 3 - z]

    barrier = pltpu.get_barrier_semaphore()

    @pl.loop(1, TP)
    def _(step):
        pl.semaphore_signal(barrier, inc=1, device_id={"tp": (me + step) % TP}, device_id_type=MESH)

    def column(shift):
        return (x + shift) % 4

    def code_rows(shift, z_at):
        return pl.ds(pl.multiple_of((z_at * 4 + column(shift)) * 64, 64), 64)

    loads = {}
    for place, shift in enumerate((0, 1, 3, 2)):
        for z_at in range(4):
            rows = code_rows(shift, z_at)
            first = (place * 4 + z_at) * 2
            loads[shift, z_at] = [
                pltpu.make_async_copy(gate_hbm.at[rows], gate_codes.at[rows], load_sem.at[first]),
                pltpu.make_async_copy(up_hbm.at[rows], up_codes.at[rows], load_sem.at[first + 1]),
            ]
            for copy in loads[shift, z_at]:
                copy.start()
    factor_load = pltpu.make_async_copy(factor_hbm, factor, load_sem.at[32])
    factor_load.start()
    down_load = pltpu.make_async_copy(down_hbm, down_codes, load_sem.at[33])
    down_load.start()

    order = field_order()

    def tokens_of(block, row, count):
        lanes = pl.ds(pl.multiple_of((block // 8) * 256 + (block % 2) * 128, 128), 128)
        return tok.at[(block // 2) % 4, pl.ds(row, count), lanes]

    tokens_of(me, 0, ROWS)[...] = jnp.dot(tok_in[...], order, preferred_element_type=F32).astype(BF16)

    pl.semaphore_wait(barrier, TP - 1)

    def spread_scales(source, spread, groups):
        scales = source[...].astype(F32)
        for group in range(groups):
            spread[group] = jnp.broadcast_to(scales[group : group + 1], spread.shape[1:])

    waiting = []

    def remote(src, dst, send, recv, device):
        copy = pltpu.make_async_remote_copy(
            src_ref=src, dst_ref=dst, send_sem=send, recv_sem=recv,
            device_id={"tp": device}, device_id_type=MESH,
        )
        copy.start()
        waiting.append(copy)
        return copy

    def pass_on(block, device):
        where = tokens_of(block, 0, ROWS)
        remote(where, where, tok_send.at[len(waiting)], tok_recv.at[block], device)

    def arrived(block):
        where = tokens_of(block, 0, ROWS)
        pltpu.make_async_copy(where, where, tok_recv.at[block]).wait()

    def at(near, shift):
        return z_of[near] * 8 + column(shift) * 2 + c

    def from_z(near):
        if near:
            arrived(at(near, 0))
        else:
            for peer in (1, 2, 3):
                pass_on(me, at(peer, 0))
        for device in (right, left, far, other):
            pass_on(at(near, 0), device)

    def from_x(near):
        for shift in (3, 1):
            arrived(at(near, shift))
            pass_on(at(near, shift), other)

    def from_far(near):
        arrived(at(near, 2))
        pass_on(at(near, 2), other)

    def from_core(shift):
        for z_at in range(4):
            arrived(z_at * 8 + column(shift) * 2 + 1 - c)

    def decode_piece(shift, z_at):
        for copy in loads[shift, z_at]:
            copy.wait()

        @pl.loop(0, 2)
        def _(side):
            group = (z_at * 4 + column(shift)) * 2 + side
            rows = pl.ds(pl.multiple_of(group * 32, 32), 32)
            for place, codes, scales in ((0, gate_codes, gate_f32), (128, up_codes, up_f32)):
                words = [codes[rows, pl.ds(128 * tile, 128)] for tile in range(TILES)]
                factors = [scales[group, :, pl.ds(128 * tile, 128)] for tile in range(TILES)]
                for tile in range(TILES):
                    for field, plane in enumerate(decode(words[tile], factors[tile])):
                        to = pl.ds(pl.multiple_of(z_at * 256 + side * 128 + 32 * field, 32), 32)
                        w_both[column(shift), to, pl.ds(256 * tile + place, 128)] = plane

    both_cols = [pl.ds(0, 512), pl.ds(512, 512), pl.ds(1024, 512), pl.ds(1536, 256)]

    def product(shift, group):
        return jnp.dot(tok[column(shift)], w_both[column(shift), :, both_cols[group]], preferred_element_type=F32)

    chip = me // 2
    wide, narrow = pl.ds(0, 256), pl.ds(0, 128)
    group_cols = [pl.ds(0, 256), pl.ds(256, 256), pl.ds(512, 256), pl.ds(768, 128)]
    group_width = [256, 256, 256, 128]

    def scatter(group):
        side, lanes = group % 2, pl.ds(0, group_width[group])

        def give(to_chip):
            pltpu.make_async_remote_copy(
                src_ref=hidden.at[to_chip, :, group_cols[group]], dst_ref=had_in.at[group // 2, me, :, lanes],
                send_sem=a_send.at[group], recv_sem=a_recv.at[group // 2],
                device_id={"tp": to_chip * 2 + side}, device_id_type=MESH,
            ).start()

        @pl.loop(1, 16)
        def _(step):
            give((chip + 1 + (step + 2) % 15) % 16)

        @pl.when(c == side)
        def _():
            pltpu.make_async_copy(
                hidden.at[chip, :, group_cols[group]], had_in.at[group // 2, me, :, lanes], a_recv.at[group // 2]
            ).start()

        @pl.when(c != side)
        def _():
            give(chip)

    def rotate(group):
        turn, lanes = group // 2, pl.ds(0, group_width[group])
        everything = had_in.at[turn, :, :, lanes]
        pltpu.make_async_copy(everything, everything, a_recv.at[turn]).wait()
        for tile in range(group_width[group] // 128):
            cols = pl.ds(128 * tile, 128)
            held = [had_in[turn, source, :, cols].astype(F32) * (1.0 / TP) for source in range(TP)]
            apart = 1
            while apart < TP:
                held = [
                    held[i - apart] - held[i] if i & apart else held[i] + held[i + apart]
                    for i in range(TP)
                ]
                apart *= 2
            for target in range(TP):
                had_out[turn, target, :, cols] = held[target].astype(BF16)

        @pl.loop(1, TP)
        def _(step):
            device = (me + 1 + (step + 6) % (TP - 1)) % TP
            pltpu.make_async_remote_copy(
                src_ref=had_out.at[turn, device, :, lanes], dst_ref=rotated.at[chip, :, group_cols[group]],
                send_sem=b_send.at[turn], recv_sem=b_recv.at[group],
                device_id={"tp": device}, device_id_type=MESH,
            ).start()

        pltpu.make_async_copy(
            had_out.at[turn, me, :, lanes], rotated.at[chip, :, group_cols[group]], b_recv.at[group]
        ).start()

    def rotate_turn(turn):
        for side in range(2):
            @pl.when(c == side)
            def _():
                rotate(2 * turn + side)

    def back(group):
        everything = rotated.at[:, :, group_cols[group]]
        pltpu.make_async_copy(everything, everything, b_recv.at[group]).wait()

    def decode_down(first, stop):
        @pl.loop(first, stop)
        def _(place):
            for side in range(2):
                cols = pl.ds(pl.multiple_of(place * 256 + 128 * side, 128), 128)
                to = pl.ds(pl.multiple_of((place // 4) * 256 + 128 * side, 128), 128)
                words = [down_codes[pl.ds(32 * group, 32), cols] for group in range(TILES)]
                factors = [down_f32[group, :, cols] for group in range(TILES)]
                for group in range(TILES):
                    for field, plane in enumerate(decode(words[group], factors[group])):
                        w_down[place % 4, pl.ds(128 * group + 32 * field, 32), to] = plane

    from_other = {}

    def down(shift):
        place = column(shift)
        for pair in range(2):
            both = jnp.dot(
                turned[...], w_down[place, :, pl.ds(512 * pair, 512)], preferred_element_type=F32
            ).astype(BF16)
            for chunk in range(CHUNKS):
                rows = slice(chunk * CR, (chunk + 1) * CR)
                for z_at in range(2):
                    for side in range(2):
                        lanes = slice(256 * z_at + 128 * side, 256 * z_at + 128 * side + 128)
                        part[chunk, side, place, 2 * pair + z_at] = both[rows, lanes]
        for chunk in range(CHUNKS):
            from_other[chunk, shift] = remote(
                part.at[chunk, 1 - c, place], core_in.at[chunk, shift],
                c_send.at[chunk, shift], c_recv.at[chunk, shift], other,
            )

    x_copies = {}

    def to_x(chunk, shift, device):
        from_other[chunk, shift].wait_recv()
        value = part[chunk, c, column(shift)].astype(F32) + core_in[chunk, shift].astype(F32)
        sums[chunk, shift] = value.astype(BF16)
        x_copies[chunk, shift] = remote(
            sums.at[chunk, shift], x_in.at[chunk, shift], x_send.at[chunk, shift], x_recv.at[chunk, shift], device
        )

    z_copies = {}

    def z_first(chunk):
        from_other[chunk, 0].wait_recv()
        for shift in (1, 3, 2):
            x_copies[chunk, shift].wait_recv()
        for near in (3, 2, 1, 0):
            to = z_of[near]
            value = (
                part[chunk, c, x, to].astype(F32) + core_in[chunk, 0, to].astype(F32)
                + x_in[chunk, 1, to].astype(F32) + x_in[chunk, 2, to].astype(F32) + x_in[chunk, 3, to].astype(F32)
            )
            mixed[chunk, near] = value.astype(BF16)
            if near:
                z_copies[chunk, near] = remote(
                    mixed.at[chunk, near], z_in.at[chunk, near], z_send.at[chunk, near], z_recv.at[chunk, near],
                    to * 8 + x * 2 + c,
                )

    def z_last(chunk):
        total = mixed[chunk, 0].astype(F32)
        for near in (1, 2, 3):
            z_copies[chunk, near].wait_recv()
            total = total + z_in[chunk, near].astype(F32)
        out_ref[pl.ds(chunk * CR, CR), :] = total.astype(BF16)

    from_z(0)
    spread_scales(gate_scales, gate_f32, 32)
    spread_scales(up_scales, up_f32, 32)
    for z_at in range(4):
        decode_piece(0, z_at)
    from_z(1)
    from_x(0)
    decode_piece(1, 0)
    decode_piece(1, 1)
    from_z(2)
    from_x(1)
    decode_piece(1, 2)
    decode_piece(1, 3)
    from_z(3)
    from_x(2)
    from_far(0)
    decode_piece(3, 0)
    decode_piece(3, 1)
    from_far(1)
    from_x(3)
    decode_piece(3, 2)
    decode_piece(3, 3)
    from_far(2)
    from_core(0)

    for group in range(4):
        total[:, both_cols[group]] = product(0, group)

    from_far(3)
    for z_at in range(4):
        decode_piece(2, z_at)
    from_core(1)
    from_core(3)

    for group in range(4):
        total[:, both_cols[group]] += product(1, group) + product(3, group)

    from_core(2)
    for group in range(4):
        both = total[:, both_cols[group]] + product(2, group)
        for tile in range(2 * group, min(2 * group + 2, TILES)):
            start = 256 * (tile - 2 * group)
            gate, up = both[:, start : start + 128], both[:, start + 128 : start + 256]
            value = gate / (1.0 + jnp.exp(-gate)) * up
            hidden[:, :, pl.ds(128 * tile, 128)] = value.astype(BF16).reshape(16, 16, 128)

        scatter(group)

    factor_load.wait()
    for tile in range(TILES):
        cols = pl.ds(128 * tile, 128)
        ordered[:, cols] = jnp.dot(factor[:, cols], order, preferred_element_type=F32).astype(BF16)
    spread_scales(down_scales, down_f32, 7)
    down_load.wait()
    decode_down(0, 8)
    rotate_turn(0)
    decode_down(8, 16)
    rotate_turn(1)
    back(0)
    back(1)
    first_part = jnp.dot(
        rotated[:, :, pl.ds(0, 512)].reshape(ROWS, 512), ordered[pl.ds(0, 512), :], preferred_element_type=F32
    )
    back(2)
    back(3)
    whole = first_part + jnp.dot(
        rotated[:, :, pl.ds(512, 384)].reshape(ROWS, 384), ordered[pl.ds(512, 384), :], preferred_element_type=F32
    )
    turned[...] = (whole * math.sqrt(TP)).astype(BF16)
    down(2)
    down(1)
    for chunk in range(CHUNKS):
        to_x(chunk, 2, far)
    down(3)
    for chunk in range(CHUNKS):
        to_x(chunk, 1, right)
    down(0)
    for chunk in range(CHUNKS):
        to_x(chunk, 3, left)
    z_first(0)
    z_first(1)
    z_last(0)
    z_last(1)

    for copy in waiting:
        copy.wait_send()
    for group in range(4):
        for kept in range(2):
            @pl.when((c == group % 2) if kept else (c != group % 2))
            def _():
                sent = hidden.at[pl.ds(0, 16 - kept), :, group_cols[group]]
                pltpu.make_async_copy(sent, sent, a_send.at[group]).wait()
                if kept:
                    sent = had_out.at[group // 2, pl.ds(0, TP - 1), :, pl.ds(0, group_width[group])]
                    pltpu.make_async_copy(sent, sent, b_send.at[group // 2]).wait()


def shards(tokens, gate_codes, gate_scales, up_codes, up_scales, local_factor, down_codes, down_scales):
    vmem, hbm, dma = pl.BlockSpec(memory_space=pltpu.VMEM), pl.BlockSpec(memory_space=pl.ANY), pltpu.SemaphoreType.DMA
    return pl.pallas_call(
        kernel,
        out_shape=jax.ShapeDtypeStruct((ROWS, 128), BF16),
        in_specs=[vmem] * 4 + [hbm] * 4,
        out_specs=vmem,
        scratch_shapes=[
            pltpu.VMEM((1024, UNITS), jnp.int32),
            pltpu.VMEM((1024, UNITS), jnp.int32),
            pltpu.VMEM((224, 4096), jnp.int32),
            pltpu.VMEM((UNITS, UNITS), BF16),
            pltpu.VMEM((4, ROWS, 1024), BF16),
            pltpu.VMEM((4, 1024, 2 * UNITS), BF16),
            pltpu.VMEM((4, UNITS, 1024), BF16),
            pltpu.VMEM((UNITS, UNITS), BF16),
            pltpu.VMEM((32, 8, UNITS), F32),
            pltpu.VMEM((32, 8, UNITS), F32),
            pltpu.VMEM((7, 8, 4096), F32),
            pltpu.VMEM((ROWS, 2 * UNITS), F32),
            pltpu.VMEM((16, 16, UNITS), BF16),
            pltpu.VMEM((2, TP, 16, 256), BF16),
            pltpu.VMEM((2, TP, 16, 256), BF16),
            pltpu.VMEM((16, 16, UNITS), BF16),
            pltpu.VMEM((ROWS, UNITS), BF16),
            pltpu.VMEM((CHUNKS, 2, 4, 4, CR, 128), BF16),
            pltpu.VMEM((CHUNKS, 4, 4, CR, 128), BF16),
            pltpu.VMEM((CHUNKS, 4, 4, CR, 128), BF16),
            pltpu.VMEM((CHUNKS, 4, 4, CR, 128), BF16),
            pltpu.VMEM((CHUNKS, 4, CR, 128), BF16),
            pltpu.VMEM((CHUNKS, 4, CR, 128), BF16),
            dma((34,)),
            dma((48,)),
            dma((TP,)),
            dma((4,)),
            dma((2,)),
            dma((2,)),
            dma((4,)),
            dma((CHUNKS, 4)),
            dma((CHUNKS, 4)),
            dma((CHUNKS, 4)),
            dma((CHUNKS, 4)),
            dma((CHUNKS, 4)),
            dma((CHUNKS, 4)),
        ],
        compiler_params=pltpu.CompilerParams(
            collective_id=0, has_side_effects=True, vmem_limit_bytes=58 * 1024 * 1024
        ),
        name="feed_forward",
    )(tokens, gate_scales, up_scales, down_scales, gate_codes, up_codes, local_factor, down_codes)


def solution(mesh):
    return jax.shard_map(
        shards,
        mesh=mesh,
        in_specs=(
            P("req", "tp"),
            P(None, "tp"),
            P(None, "tp"),
            P(None, "tp"),
            P(None, "tp"),
            P(),
            P("tp", None),
            P("tp", None),
        ),
        out_specs=P("req", "tp"),
        check_vma=False,
    )
```

```python
import functools
import math

import jax
import jax.numpy as jnp
from jax import lax
from jax.experimental import pallas as pl
from jax.experimental.pallas import tpu as pltpu
from jax.sharding import PartitionSpec as P

MESH = pl.DeviceIdType.MESH
TP = 32
ROWS = 256
UNITS = 896
TILES = 7
CHUNKS = 4
CR = ROWS // CHUNKS
HALF = CR // 2
F32 = jnp.float32
BF16 = jnp.bfloat16


def field_order():
    source = lax.broadcasted_iota(jnp.int32, (128, 128), 0)
    target = lax.broadcasted_iota(jnp.int32, (128, 128), 1)
    return jnp.where(target == (source % 4) * 32 + source // 4, 1.0, 0.0).astype(BF16)


def decode(words, scale):
    flipped = jnp.bitwise_xor(words, 0x0888)
    planes = []
    for field in range(4):
        if field == 3:
            value = jnp.right_shift(words, 12)
        else:
            value = jnp.right_shift(jnp.left_shift(flipped, 28 - 4 * field), 28)
        scaled = value.astype(F32).reshape(4, 8, 128) * scale
        planes.append(scaled.reshape(32, 128).astype(BF16))
    return planes


def kernel(
    tok_in, gate_scales, up_scales, down_scales, gate_hbm, up_hbm, factor_hbm, down_hbm, out_ref,
    gate_codes, up_codes, down_codes, factor, tok, w_both, w_down, ordered, gate_f32, up_f32, down_f32, total,
    hidden, had_in, had_out, rotated, turned, part, core_in, sums, first_in, second_in, mixed, z_in,
    load_sem, tok_send, tok_recv, a_send, a_recv, b_send, b_recv, c_send, c_recv, x_send, x_recv,
    y_send, y_recv, z_send, z_recv,
):
    me = lax.axis_index("tp")
    z, x, c = me // 8, (me // 2) % 4, me % 2
    other = me + 1 - 2 * c
    right = z * 8 + ((x + 1) % 4) * 2 + c
    left = z * 8 + ((x + 3) % 4) * 2 + c
    z_of = [z, z + 1 - 2 * (z % 2), (z + 2) % 4, 3 - z]

    barrier = pltpu.get_barrier_semaphore()

    @pl.loop(1, TP)
    def _(step):
        pl.semaphore_signal(barrier, inc=1, device_id={"tp": (me + step) % TP}, device_id_type=MESH)

    def column(shift):
        return (x + shift) % 4

    def code_rows(shift, z_at):
        return pl.ds(pl.multiple_of((z_at * 4 + column(shift)) * 64, 64), 64)

    loads = {}
    for place, shift in enumerate((0, 1, 3, 2)):
        for z_at in range(4):
            rows = code_rows(shift, z_at)
            first = (place * 4 + z_at) * 2
            loads[shift, z_at] = [
                pltpu.make_async_copy(gate_hbm.at[rows], gate_codes.at[rows], load_sem.at[first]),
                pltpu.make_async_copy(up_hbm.at[rows], up_codes.at[rows], load_sem.at[first + 1]),
            ]
            for copy in loads[shift, z_at]:
                copy.start()
    factor_load = pltpu.make_async_copy(factor_hbm, factor, load_sem.at[32])
    factor_load.start()
    down_load = pltpu.make_async_copy(down_hbm, down_codes, load_sem.at[33])
    down_load.start()

    order = field_order()

    def tokens_of(block, row, count):
        lanes = pl.ds(pl.multiple_of((block // 8) * 256 + (block % 2) * 128, 128), 128)
        return tok.at[(block // 2) % 4, pl.ds(row, count), lanes]

    tokens_of(me, 0, ROWS)[...] = jnp.dot(tok_in[...], order, preferred_element_type=F32).astype(BF16)

    def spread_scales(source, spread, groups):
        scales = source[...].astype(F32)
        for group in range(groups):
            spread[group] = jnp.broadcast_to(scales[group : group + 1], spread.shape[1:])

    def decode_piece(shift, z_at):
        for copy in loads[shift, z_at]:
            copy.wait()

        @pl.loop(0, 2)
        def _(side):
            group = (z_at * 4 + column(shift)) * 2 + side
            rows = pl.ds(pl.multiple_of(group * 32, 32), 32)
            for place, codes, scales in ((0, gate_codes, gate_f32), (128, up_codes, up_f32)):
                words = [codes[rows, pl.ds(128 * tile, 128)] for tile in range(TILES)]
                factors = [scales[group, :, pl.ds(128 * tile, 128)] for tile in range(TILES)]
                for tile in range(TILES):
                    for field, plane in enumerate(decode(words[tile], factors[tile])):
                        to = pl.ds(pl.multiple_of(z_at * 256 + side * 128 + 32 * field, 32), 32)
                        w_both[column(shift), to, pl.ds(256 * tile + place, 128)] = plane

    spread_scales(gate_scales, gate_f32, 32)
    spread_scales(up_scales, up_f32, 32)
    decode_piece(0, 0)

    pl.semaphore_wait(barrier, TP - 1)

    waiting = []

    def remote(src, dst, send, recv, device):
        copy = pltpu.make_async_remote_copy(
            src_ref=src, dst_ref=dst, send_sem=send, recv_sem=recv,
            device_id={"tp": device}, device_id_type=MESH,
        )
        copy.start()
        waiting.append(copy)
        return copy

    def pass_on(block, device, row=0, count=ROWS):
        where = tokens_of(block, row, count)
        remote(where, where, tok_send.at[len(waiting)], tok_recv.at[block, 1 if row else 0], device)

    def arrived(block, row=0, count=ROWS):
        where = tokens_of(block, row, count)
        pltpu.make_async_copy(where, where, tok_recv.at[block, 1 if row else 0]).wait()

    def at(near, shift):
        return z_of[near] * 8 + column(shift) * 2 + c

    def from_z(near):
        if near:
            arrived(at(near, 0))
        pass_on(at(near, 0), right)
        pass_on(at(near, 0), left)
        if not near:
            for peer in (1, 2, 3):
                pass_on(me, at(peer, 0))
        pass_on(at(near, 0), other)

    def from_x(near):
        block = at(near, 3)
        arrived(block)
        pass_on(block, right, 0, ROWS // 2)
        pass_on(block, other)
        block = at(near, 1)
        arrived(block)
        pass_on(block, left, ROWS // 2, ROWS // 2)
        pass_on(block, other)

    def from_far(near):
        block = at(near, 2)
        arrived(block, 0, ROWS // 2)
        arrived(block, ROWS // 2, ROWS // 2)
        pass_on(block, other)

    def from_core(shift):
        for z_at in range(4):
            arrived(z_at * 8 + column(shift) * 2 + 1 - c)

    both_cols = [pl.ds(0, 512), pl.ds(512, 512), pl.ds(1024, 512), pl.ds(1536, 256)]

    def product(shift, group):
        return jnp.dot(tok[column(shift)], w_both[column(shift), :, both_cols[group]], preferred_element_type=F32)

    chip = me // 2
    wide, narrow = pl.ds(0, 256), pl.ds(0, 128)
    group_cols = [pl.ds(0, 256), pl.ds(256, 256), pl.ds(512, 256), pl.ds(768, 128)]
    group_width = [256, 256, 256, 128]

    def scatter(group):
        side, lanes = group % 2, pl.ds(0, group_width[group])

        def give(to_chip):
            pltpu.make_async_remote_copy(
                src_ref=hidden.at[to_chip, :, group_cols[group]], dst_ref=had_in.at[group // 2, me, :, lanes],
                send_sem=a_send.at[group], recv_sem=a_recv.at[group // 2],
                device_id={"tp": to_chip * 2 + side}, device_id_type=MESH,
            ).start()

        @pl.loop(1, 16)
        def _(step):
            give((chip + 1 + (step + 2) % 15) % 16)

        @pl.when(c == side)
        def _():
            pltpu.make_async_copy(
                hidden.at[chip, :, group_cols[group]], had_in.at[group // 2, me, :, lanes], a_recv.at[group // 2]
            ).start()

        @pl.when(c != side)
        def _():
            give(chip)

    def rotate(group):
        turn, lanes = group // 2, pl.ds(0, group_width[group])
        everything = had_in.at[turn, :, :, lanes]
        pltpu.make_async_copy(everything, everything, a_recv.at[turn]).wait()
        for tile in range(group_width[group] // 128):
            cols = pl.ds(128 * tile, 128)
            held = [had_in[turn, source, :, cols].astype(F32) * (1.0 / TP) for source in range(TP)]
            apart = 1
            while apart < TP:
                held = [
                    held[i - apart] - held[i] if i & apart else held[i] + held[i + apart]
                    for i in range(TP)
                ]
                apart *= 2
            for target in range(TP):
                had_out[turn, target, :, cols] = held[target].astype(BF16)

        @pl.loop(1, TP)
        def _(step):
            device = (me + 1 + (step + 6) % (TP - 1)) % TP
            pltpu.make_async_remote_copy(
                src_ref=had_out.at[turn, device, :, lanes], dst_ref=rotated.at[chip, :, group_cols[group]],
                send_sem=b_send.at[turn], recv_sem=b_recv.at[group],
                device_id={"tp": device}, device_id_type=MESH,
            ).start()

        pltpu.make_async_copy(
            had_out.at[turn, me, :, lanes], rotated.at[chip, :, group_cols[group]], b_recv.at[group]
        ).start()

    def rotate_turn(turn):
        for side in range(2):
            @pl.when(c == side)
            def _():
                rotate(2 * turn + side)

    def back(group):
        everything = rotated.at[:, :, group_cols[group]]
        pltpu.make_async_copy(everything, everything, b_recv.at[group]).wait()

    def decode_down(first, stop):
        @pl.loop(first, stop)
        def _(place):
            for side in range(2):
                cols = pl.ds(pl.multiple_of(place * 256 + 128 * side, 128), 128)
                to = pl.ds(pl.multiple_of((place // 4) * 256 + 128 * side, 128), 128)
                words = [down_codes[pl.ds(32 * group, 32), cols] for group in range(TILES)]
                factors = [down_f32[group, :, cols] for group in range(TILES)]
                for group in range(TILES):
                    for field, plane in enumerate(decode(words[group], factors[group])):
                        w_down[place % 4, pl.ds(128 * group + 32 * field, 32), to] = plane

    from_other = {}

    def down(shift):
        place = column(shift)
        for pair in range(2):
            both = jnp.dot(
                turned[...], w_down[place, :, pl.ds(512 * pair, 512)], preferred_element_type=F32
            ).astype(BF16)
            for chunk in range(CHUNKS):
                rows = slice(chunk * CR, (chunk + 1) * CR)
                for z_at in range(2):
                    for side in range(2):
                        lanes = slice(256 * z_at + 128 * side, 256 * z_at + 128 * side + 128)
                        part[chunk, side, place, 2 * pair + z_at] = both[rows, lanes]
        for chunk in range(CHUNKS):
            from_other[chunk, shift] = remote(
                part.at[chunk, 1 - c, place], core_in.at[chunk, shift],
                c_send.at[chunk, shift], c_recv.at[chunk, shift], other,
            )

    top, bottom = pl.ds(0, HALF), pl.ds(HALF, HALF)

    def join(chunk, shift, rows):
        return part[chunk, c, column(shift), :, rows].astype(F32) + core_in[chunk, shift, :, rows].astype(F32)

    x_copies = {}

    def x_first(chunk):
        from_other[chunk, 2].wait_recv()
        sums[chunk, 2] = join(chunk, 2, pl.ds(0, CR)).astype(BF16)
        x_copies[chunk, "r1"] = remote(
            sums.at[chunk, 2, :, top], first_in.at[chunk, 0], x_send.at[chunk, 0], x_recv.at[chunk, 0], right
        )
        x_copies[chunk, "l1"] = remote(
            sums.at[chunk, 2, :, bottom], first_in.at[chunk, 1], x_send.at[chunk, 1], x_recv.at[chunk, 1], left
        )

    def x_second(chunk):
        from_other[chunk, 1].wait_recv()
        sums[chunk, 1, :, bottom] = join(chunk, 1, bottom).astype(BF16)
        x_copies[chunk, "r1"].wait_recv()
        sums[chunk, 1, :, top] = (join(chunk, 1, top) + first_in[chunk, 0].astype(F32)).astype(BF16)
        x_copies[chunk, "r2"] = remote(
            sums.at[chunk, 1], second_in.at[chunk, 0], y_send.at[chunk, 0], y_recv.at[chunk, 0], right
        )
        from_other[chunk, 3].wait_recv()
        sums[chunk, 3, :, top] = join(chunk, 3, top).astype(BF16)
        x_copies[chunk, "l1"].wait_recv()
        sums[chunk, 3, :, bottom] = (join(chunk, 3, bottom) + first_in[chunk, 1].astype(F32)).astype(BF16)
        x_copies[chunk, "l2"] = remote(
            sums.at[chunk, 3], second_in.at[chunk, 1], y_send.at[chunk, 1], y_recv.at[chunk, 1], left
        )

    z_copies = {}

    def z_first(chunk):
        from_other[chunk, 0].wait_recv()
        x_copies[chunk, "r2"].wait_recv()
        x_copies[chunk, "l2"].wait_recv()
        for near in (3, 2, 1, 0):
            to = z_of[near]
            value = (
                part[chunk, c, x, to].astype(F32) + core_in[chunk, 0, to].astype(F32)
                + second_in[chunk, 0, to].astype(F32) + second_in[chunk, 1, to].astype(F32)
            )
            mixed[chunk, near] = value.astype(BF16)
            if near:
                z_copies[chunk, near] = remote(
                    mixed.at[chunk, near], z_in.at[chunk, near], z_send.at[chunk, near], z_recv.at[chunk, near],
                    to * 8 + x * 2 + c,
                )

    def z_last(chunk):
        total = mixed[chunk, 0].astype(F32)
        for near in (1, 2, 3):
            z_copies[chunk, near].wait_recv()
            total = total + z_in[chunk, near].astype(F32)
        out_ref[pl.ds(chunk * CR, CR), :] = total.astype(BF16)

    from_z(0)
    for z_at in range(1, 4):
        decode_piece(0, z_at)
    from_z(1)
    from_x(0)
    decode_piece(1, 0)
    decode_piece(1, 1)
    from_z(2)
    from_x(1)
    decode_piece(1, 2)
    decode_piece(1, 3)
    from_z(3)
    from_x(2)
    from_far(0)
    decode_piece(3, 0)
    decode_piece(3, 1)
    from_far(1)
    from_x(3)
    decode_piece(3, 2)
    decode_piece(3, 3)
    from_far(2)
    from_core(0)

    for group in range(4):
        total[:, both_cols[group]] = product(0, group)

    for z_at in range(4):
        decode_piece(2, z_at)
    from_core(1)
    for group in range(4):
        total[:, both_cols[group]] += product(1, group)
    from_far(3)
    from_core(3)
    for group in range(4):
        total[:, both_cols[group]] += product(3, group)
    from_core(2)
    for group in range(4):
        both = total[:, both_cols[group]] + product(2, group)
        for tile in range(2 * group, min(2 * group + 2, TILES)):
            start = 256 * (tile - 2 * group)
            gate, up = both[:, start : start + 128], both[:, start + 128 : start + 256]
            value = gate / (1.0 + jnp.exp(-gate)) * up
            hidden[:, :, pl.ds(128 * tile, 128)] = value.astype(BF16).reshape(16, 16, 128)

        scatter(group)

    factor_load.wait()
    for tile in range(TILES):
        cols = pl.ds(128 * tile, 128)
        ordered[:, cols] = jnp.dot(factor[:, cols], order, preferred_element_type=F32).astype(BF16)
    spread_scales(down_scales, down_f32, 7)
    down_load.wait()
    decode_down(0, 8)
    rotate_turn(0)
    decode_down(8, 16)
    rotate_turn(1)
    back(0)
    back(1)
    first_part = jnp.dot(
        rotated[:, :, pl.ds(0, 512)].reshape(ROWS, 512), ordered[pl.ds(0, 512), :], preferred_element_type=F32
    )
    back(2)
    back(3)
    whole = first_part + jnp.dot(
        rotated[:, :, pl.ds(512, 384)].reshape(ROWS, 384), ordered[pl.ds(512, 384), :], preferred_element_type=F32
    )
    turned[...] = (whole * math.sqrt(TP)).astype(BF16)
    down(2)
    down(1)
    for chunk in range(CHUNKS):
        x_first(chunk)
    down(3)
    down(0)
    for chunk in range(CHUNKS):
        x_second(chunk)
    for chunk in range(CHUNKS):
        z_first(chunk)
    for chunk in range(CHUNKS):
        z_last(chunk)

    for copy in waiting:
        copy.wait_send()
    for group in range(4):
        for kept in range(2):
            @pl.when((c == group % 2) if kept else (c != group % 2))
            def _():
                sent = hidden.at[pl.ds(0, 16 - kept), :, group_cols[group]]
                pltpu.make_async_copy(sent, sent, a_send.at[group]).wait()
                if kept:
                    sent = had_out.at[group // 2, pl.ds(0, TP - 1), :, pl.ds(0, group_width[group])]
                    pltpu.make_async_copy(sent, sent, b_send.at[group // 2]).wait()


def shards(tokens, gate_codes, gate_scales, up_codes, up_scales, local_factor, down_codes, down_scales):
    vmem, hbm, dma = pl.BlockSpec(memory_space=pltpu.VMEM), pl.BlockSpec(memory_space=pl.ANY), pltpu.SemaphoreType.DMA
    return pl.pallas_call(
        kernel,
        out_shape=jax.ShapeDtypeStruct((ROWS, 128), BF16),
        in_specs=[vmem] * 4 + [hbm] * 4,
        out_specs=vmem,
        scratch_shapes=[
            pltpu.VMEM((1024, UNITS), jnp.int32),
            pltpu.VMEM((1024, UNITS), jnp.int32),
            pltpu.VMEM((224, 4096), jnp.int32),
            pltpu.VMEM((UNITS, UNITS), BF16),
            pltpu.VMEM((4, ROWS, 1024), BF16),
            pltpu.VMEM((4, 1024, 2 * UNITS), BF16),
            pltpu.VMEM((4, UNITS, 1024), BF16),
            pltpu.VMEM((UNITS, UNITS), BF16),
            pltpu.VMEM((32, 8, UNITS), F32),
            pltpu.VMEM((32, 8, UNITS), F32),
            pltpu.VMEM((7, 8, 4096), F32),
            pltpu.VMEM((ROWS, 2 * UNITS), F32),
            pltpu.VMEM((16, 16, UNITS), BF16),
            pltpu.VMEM((2, TP, 16, 256), BF16),
            pltpu.VMEM((2, TP, 16, 256), BF16),
            pltpu.VMEM((16, 16, UNITS), BF16),
            pltpu.VMEM((ROWS, UNITS), BF16),
            pltpu.VMEM((CHUNKS, 2, 4, 4, CR, 128), BF16),
            pltpu.VMEM((CHUNKS, 4, 4, CR, 128), BF16),
            pltpu.VMEM((CHUNKS, 4, 4, CR, 128), BF16),
            pltpu.VMEM((CHUNKS, 2, 4, HALF, 128), BF16),
            pltpu.VMEM((CHUNKS, 2, 4, CR, 128), BF16),
            pltpu.VMEM((CHUNKS, 4, CR, 128), BF16),
            pltpu.VMEM((CHUNKS, 4, CR, 128), BF16),
            dma((34,)),
            dma((48,)),
            dma((TP, 2)),
            dma((4,)),
            dma((2,)),
            dma((2,)),
            dma((4,)),
            dma((CHUNKS, 4)),
            dma((CHUNKS, 4)),
            dma((CHUNKS, 2)),
            dma((CHUNKS, 2)),
            dma((CHUNKS, 2)),
            dma((CHUNKS, 2)),
            dma((CHUNKS, 4)),
            dma((CHUNKS, 4)),
        ],
        compiler_params=pltpu.CompilerParams(
            collective_id=0, has_side_effects=True, vmem_limit_bytes=58 * 1024 * 1024
        ),
        name="feed_forward",
    )(tokens, gate_scales, up_scales, down_scales, gate_codes, up_codes, local_factor, down_codes)


def solution(mesh):
    return jax.shard_map(
        shards,
        mesh=mesh,
        in_specs=(
            P("req", "tp"),
            P(None, "tp"),
            P(None, "tp"),
            P(None, "tp"),
            P(None, "tp"),
            P(),
            P("tp", None),
            P("tp", None),
        ),
        out_specs=P("req", "tp"),
        check_vma=False,
    )
```

```python
import functools
import math

import jax
import jax.numpy as jnp
from jax import lax
from jax.experimental import pallas as pl
from jax.experimental.pallas import tpu as pltpu
from jax.sharding import PartitionSpec as P

MESH = pl.DeviceIdType.MESH
TP = 32
ROWS = 256
UNITS = 896
TILES = 7
CHUNKS = 2
CR = ROWS // CHUNKS
HALF = CR // 2
F32 = jnp.float32
BF16 = jnp.bfloat16


def field_order():
    source = lax.broadcasted_iota(jnp.int32, (128, 128), 0)
    target = lax.broadcasted_iota(jnp.int32, (128, 128), 1)
    return jnp.where(target == (source % 4) * 32 + source // 4, 1.0, 0.0).astype(BF16)


def decode(words, scale):
    flipped = jnp.bitwise_xor(words, 0x0888)
    planes = []
    for field in range(4):
        if field == 3:
            value = jnp.right_shift(words, 12)
        else:
            value = jnp.right_shift(jnp.left_shift(flipped, 28 - 4 * field), 28)
        scaled = value.astype(F32).reshape(4, 8, 128) * scale
        planes.append(scaled.reshape(32, 128).astype(BF16))
    return planes


def kernel(
    tok_in, gate_scales, up_scales, down_scales, gate_hbm, up_hbm, factor_hbm, down_hbm, out_ref,
    gate_codes, up_codes, down_codes, factor, tok, w_both, w_down, ordered, gate_f32, up_f32, down_f32, total,
    hidden, had_in, had_out, rotated, turned, part, core_in, sums, first_in, second_in, mixed, z_in,
    load_sem, tok_send, tok_recv, a_send, a_recv, b_send, b_recv, c_send, c_recv, x_send, x_recv,
    y_send, y_recv, z_send, z_recv,
):
    me = lax.axis_index("tp")
    z, x, c = me // 8, (me // 2) % 4, me % 2
    other = me + 1 - 2 * c
    right = z * 8 + ((x + 1) % 4) * 2 + c
    left = z * 8 + ((x + 3) % 4) * 2 + c
    z_of = [z, z + 1 - 2 * (z % 2), (z + 2) % 4, 3 - z]

    barrier = pltpu.get_barrier_semaphore()

    @pl.loop(1, TP)
    def _(step):
        pl.semaphore_signal(barrier, inc=1, device_id={"tp": (me + step) % TP}, device_id_type=MESH)

    def column(shift):
        return (x + shift) % 4

    def code_rows(shift, z_at):
        return pl.ds(pl.multiple_of((z_at * 4 + column(shift)) * 64, 64), 64)

    loads = {}
    for place, shift in enumerate((0, 1, 3, 2)):
        for z_at in range(4):
            rows = code_rows(shift, z_at)
            first = (place * 4 + z_at) * 2
            loads[shift, z_at] = [
                pltpu.make_async_copy(gate_hbm.at[rows], gate_codes.at[rows], load_sem.at[first]),
                pltpu.make_async_copy(up_hbm.at[rows], up_codes.at[rows], load_sem.at[first + 1]),
            ]
            for copy in loads[shift, z_at]:
                copy.start()
    factor_load = pltpu.make_async_copy(factor_hbm, factor, load_sem.at[32])
    factor_load.start()
    down_load = pltpu.make_async_copy(down_hbm, down_codes, load_sem.at[33])
    down_load.start()

    order = field_order()

    def tokens_of(block, row, count):
        lanes = pl.ds(pl.multiple_of((block // 8) * 256 + (block % 2) * 128, 128), 128)
        return tok.at[(block // 2) % 4, pl.ds(row, count), lanes]

    tokens_of(me, 0, ROWS)[...] = jnp.dot(tok_in[...], order, preferred_element_type=F32).astype(BF16)

    pl.semaphore_wait(barrier, TP - 1)

    def spread_scales(source, spread, groups):
        scales = source[...].astype(F32)
        for group in range(groups):
            spread[group] = jnp.broadcast_to(scales[group : group + 1], spread.shape[1:])

    waiting = []

    def here(device):
        return {"tp": device}

    def remote(src, dst, send, recv, device):
        copy = pltpu.make_async_remote_copy(
            src_ref=src, dst_ref=dst, send_sem=send, recv_sem=recv, device_id=device, device_id_type=MESH,
        )
        copy.start()
        waiting.append(copy)
        return copy

    def pass_on(block, device, row=0, count=ROWS):
        where = tokens_of(block, row, count)
        remote(where, where, tok_send.at[len(waiting)], tok_recv.at[block, 1 if row else 0], here(device))

    def arrived(block, row=0, count=ROWS):
        where = tokens_of(block, row, count)
        pltpu.make_async_copy(where, where, tok_recv.at[block, 1 if row else 0]).wait()

    def at(near, shift):
        return z_of[near] * 8 + column(shift) * 2 + c

    def from_z(near):
        if near:
            arrived(at(near, 0))
        pass_on(at(near, 0), right)
        pass_on(at(near, 0), left)
        if not near:
            for peer in (1, 2, 3):
                pass_on(me, at(peer, 0))
        pass_on(at(near, 0), other)

    def from_x(near):
        block = at(near, 3)
        arrived(block)
        pass_on(block, right, 0, ROWS // 2)
        pass_on(block, other)
        block = at(near, 1)
        arrived(block)
        pass_on(block, left, ROWS // 2, ROWS // 2)
        pass_on(block, other)

    def from_far(near):
        block = at(near, 2)
        arrived(block, 0, ROWS // 2)
        arrived(block, ROWS // 2, ROWS // 2)
        pass_on(block, other)

    def from_core(shift):
        for z_at in range(4):
            arrived(z_at * 8 + column(shift) * 2 + 1 - c)

    def decode_piece(shift, z_at):
        for copy in loads[shift, z_at]:
            copy.wait()

        @pl.loop(0, 2)
        def _(side):
            group = (z_at * 4 + column(shift)) * 2 + side
            rows = pl.ds(pl.multiple_of(group * 32, 32), 32)
            for place, codes, scales in ((0, gate_codes, gate_f32), (128, up_codes, up_f32)):
                words = [codes[rows, pl.ds(128 * tile, 128)] for tile in range(TILES)]
                factors = [scales[group, :, pl.ds(128 * tile, 128)] for tile in range(TILES)]
                for tile in range(TILES):
                    for field, plane in enumerate(decode(words[tile], factors[tile])):
                        to = pl.ds(pl.multiple_of(z_at * 256 + side * 128 + 32 * field, 32), 32)
                        w_both[column(shift), to, pl.ds(256 * tile + place, 128)] = plane

    both_cols = [pl.ds(0, 512), pl.ds(512, 512), pl.ds(1024, 512), pl.ds(1536, 256)]

    def product(shift, group, rows=pl.ds(0, ROWS)):
        return jnp.dot(
            tok[column(shift), rows, :], w_both[column(shift), :, both_cols[group]], preferred_element_type=F32
        )

    group_cols = [pl.ds(0, 256), pl.ds(256, 256), pl.ds(512, 256), pl.ds(768, 128)]
    group_width = [256, 256, 256, 128]

    row_tile = z * 2 + x // 2

    def scatter(chunk, group):
        side, lanes = group % 2, pl.ds(0, group_width[group])
        parity = (group // 2 + chunk) % 2

        def give(step):
            dz, half = (z + 1 + step // 2) % 4, (x // 2 + step) % 2
            device, tile = dz * 8 + (parity + 2 * half) * 2 + side, chunk * 8 + dz * 2 + half
            pltpu.make_async_remote_copy(
                src_ref=hidden.at[tile, :, group_cols[group]], dst_ref=had_in.at[chunk, me, :, lanes],
                send_sem=a_send.at[group], recv_sem=a_recv.at[chunk],
                device_id=here(device), device_id_type=MESH,
            ).start()

        for step in range(6):
            give(step)
        give(7)
        own = jnp.logical_and(c == side, x % 2 == parity)

        @pl.when(own)
        def _():
            pltpu.make_async_copy(
                hidden.at[chunk * 8 + row_tile, :, group_cols[group]], had_in.at[chunk, me, :, lanes],
                a_recv.at[chunk],
            ).start()

        @pl.when(jnp.logical_not(own))
        def _():
            give(6)

    def my_group(chunk):
        return 2 * ((x + chunk) % 2) + c

    def rotate_part(chunk, width, to_cols):
        lanes = pl.ds(0, width)
        everything = had_in.at[chunk, :, :, lanes]
        pltpu.make_async_copy(everything, everything, a_recv.at[chunk]).wait()
        for tile in range(width // 128):
            cols = pl.ds(128 * tile, 128)
            held = [had_in[chunk, source, :, cols].astype(F32) * (1.0 / TP) for source in range(TP)]
            apart = 1
            while apart < TP:
                held = [
                    held[i - apart] - held[i] if i & apart else held[i] + held[i + apart]
                    for i in range(TP)
                ]
                apart *= 2
            for target in range(TP):
                had_out[chunk, target, :, cols] = held[target].astype(BF16)

        @pl.loop(1, TP)
        def _(step):
            device = (me + 1 + (step + 6) % (TP - 1)) % TP
            pltpu.make_async_remote_copy(
                src_ref=had_out.at[chunk, device, :, lanes], dst_ref=rotated.at[chunk * 8 + row_tile, :, to_cols],
                send_sem=b_send.at[chunk], recv_sem=b_recv.at[chunk],
                device_id=here(device), device_id_type=MESH,
            ).start()

        pltpu.make_async_copy(
            had_out.at[chunk, me, :, lanes], rotated.at[chunk * 8 + row_tile, :, to_cols], b_recv.at[chunk]
        ).start()

    def rotate(chunk):
        group = my_group(chunk)

        @pl.when(group < 3)
        def _():
            rotate_part(chunk, 256, pl.ds(pl.multiple_of(group * 256, 256), 256))

        @pl.when(group == 3)
        def _():
            rotate_part(chunk, 128, group_cols[3])

    def turn(chunk):
        tiles = pl.ds(8 * chunk, 8)
        everything = rotated.at[tiles]
        pltpu.make_async_copy(everything, everything, b_recv.at[chunk]).wait()
        value = jnp.dot(rotated[tiles].reshape(CR, UNITS), ordered[...], preferred_element_type=F32)
        turned[pl.ds(chunk * CR, CR), :] = (value * math.sqrt(TP)).astype(BF16)

    def decode_down(first, stop):
        @pl.loop(first, stop)
        def _(place):
            for side in range(2):
                cols = pl.ds(pl.multiple_of(place * 256 + 128 * side, 128), 128)
                to = pl.ds(pl.multiple_of((place // 4) * 256 + 128 * side, 128), 128)
                words = [down_codes[pl.ds(32 * group, 32), cols] for group in range(TILES)]
                factors = [down_f32[group, :, cols] for group in range(TILES)]
                for group in range(TILES):
                    for field, plane in enumerate(decode(words[group], factors[group])):
                        w_down[place % 4, pl.ds(128 * group + 32 * field, 32), to] = plane

    from_other = {}

    def down(chunk, shift):
        place = column(shift)
        for pair in range(2):
            both = jnp.dot(
                turned[pl.ds(chunk * CR, CR), :], w_down[place, :, pl.ds(512 * pair, 512)],
                preferred_element_type=F32,
            ).astype(BF16)
            for z_at in range(2):
                for side in range(2):
                    lanes = slice(256 * z_at + 128 * side, 256 * z_at + 128 * side + 128)
                    part[chunk, side, place, 2 * pair + z_at] = both[:, lanes]
        from_other[chunk, shift] = remote(
            part.at[chunk, 1 - c, place], core_in.at[chunk, shift],
            c_send.at[chunk, shift], c_recv.at[chunk, shift], here(other),
        )

    top, bottom = pl.ds(0, HALF), pl.ds(HALF, HALF)

    def join(chunk, shift, rows):
        return part[chunk, c, column(shift), :, rows].astype(F32) + core_in[chunk, shift, :, rows].astype(F32)

    x_copies = {}

    def x_first(chunk):
        from_other[chunk, 2].wait_recv()
        sums[chunk, 2] = join(chunk, 2, pl.ds(0, CR)).astype(BF16)
        x_copies[chunk, "r1"] = remote(
            sums.at[chunk, 2, :, top], first_in.at[chunk, 0], x_send.at[chunk, 0], x_recv.at[chunk, 0], here(right)
        )
        x_copies[chunk, "l1"] = remote(
            sums.at[chunk, 2, :, bottom], first_in.at[chunk, 1], x_send.at[chunk, 1], x_recv.at[chunk, 1], here(left)
        )

    def x_second(chunk):
        from_other[chunk, 1].wait_recv()
        sums[chunk, 1, :, bottom] = join(chunk, 1, bottom).astype(BF16)
        x_copies[chunk, "r1"].wait_recv()
        sums[chunk, 1, :, top] = (join(chunk, 1, top) + first_in[chunk, 0].astype(F32)).astype(BF16)
        x_copies[chunk, "r2"] = remote(
            sums.at[chunk, 1], second_in.at[chunk, 0], y_send.at[chunk, 0], y_recv.at[chunk, 0], here(right)
        )
        from_other[chunk, 3].wait_recv()
        sums[chunk, 3, :, top] = join(chunk, 3, top).astype(BF16)
        x_copies[chunk, "l1"].wait_recv()
        sums[chunk, 3, :, bottom] = (join(chunk, 3, bottom) + first_in[chunk, 1].astype(F32)).astype(BF16)
        x_copies[chunk, "l2"] = remote(
            sums.at[chunk, 3], second_in.at[chunk, 1], y_send.at[chunk, 1], y_recv.at[chunk, 1], here(left)
        )

    z_copies = {}

    def z_first(chunk):
        from_other[chunk, 0].wait_recv()
        x_copies[chunk, "r2"].wait_recv()
        x_copies[chunk, "l2"].wait_recv()
        for near in (3, 2, 1, 0):
            to = z_of[near]
            value = (
                part[chunk, c, x, to].astype(F32) + core_in[chunk, 0, to].astype(F32)
                + second_in[chunk, 0, to].astype(F32) + second_in[chunk, 1, to].astype(F32)
            )
            mixed[chunk, near] = value.astype(BF16)
            if near:
                z_copies[chunk, near] = remote(
                    mixed.at[chunk, near], z_in.at[chunk, near], z_send.at[chunk, near], z_recv.at[chunk, near],
                    here(to * 8 + x * 2 + c),
                )

    def z_last(chunk):
        value = mixed[chunk, 0].astype(F32)
        for near in (1, 2, 3):
            z_copies[chunk, near].wait_recv()
            value = value + z_in[chunk, near].astype(F32)
        out_ref[pl.ds(chunk * CR, CR), :] = value.astype(BF16)

    from_z(0)
    spread_scales(gate_scales, gate_f32, 32)
    spread_scales(up_scales, up_f32, 32)
    for z_at in range(4):
        decode_piece(0, z_at)
    from_z(1)
    from_x(0)
    decode_piece(1, 0)
    decode_piece(1, 1)
    from_z(2)
    from_x(1)
    decode_piece(1, 2)
    decode_piece(1, 3)
    from_z(3)
    from_x(2)
    from_far(0)
    decode_piece(3, 0)
    decode_piece(3, 1)
    from_far(1)
    from_x(3)
    decode_piece(3, 2)
    decode_piece(3, 3)
    from_far(2)
    from_core(0)
    for group in range(4):
        total[:, both_cols[group]] = product(0, group)
    for z_at in range(4):
        decode_piece(2, z_at)
    from_core(1)
    for group in range(4):
        total[:, both_cols[group]] += product(1, group)
    from_far(3)
    from_core(3)
    for group in range(4):
        total[:, both_cols[group]] += product(3, group)
    from_core(2)
    for chunk in range(CHUNKS):
        rows = pl.ds(chunk * CR, CR)
        for group in range(4):
            both = total[rows, both_cols[group]] + product(2, group, rows)
            for tile in range(2 * group, min(2 * group + 2, TILES)):
                start = 256 * (tile - 2 * group)
                gate, up = both[:, start : start + 128], both[:, start + 128 : start + 256]
                value = gate / (1.0 + jnp.exp(-gate)) * up
                hidden[pl.ds(8 * chunk, 8), :, pl.ds(128 * tile, 128)] = value.astype(BF16).reshape(8, 16, 128)
            scatter(chunk, group)

    spread_scales(down_scales, down_f32, 7)
    factor_load.wait()
    for tile in range(TILES):
        cols = pl.ds(128 * tile, 128)
        ordered[:, cols] = jnp.dot(factor[:, cols], order, preferred_element_type=F32).astype(BF16)
    down_load.wait()
    decode_down(0, 8)
    rotate(0)
    decode_down(8, 16)
    rotate(1)
    turn(0)
    down(0, 2)
    down(0, 1)
    x_first(0)
    down(0, 3)
    down(0, 0)
    x_second(0)
    turn(1)
    down(1, 2)
    down(1, 1)
    x_first(1)
    down(1, 3)
    down(1, 0)
    z_first(0)
    x_second(1)
    z_last(0)
    z_first(1)
    z_last(1)

    for copy in waiting:
        copy.wait_send()
    for group in range(4):
        for kept in range(2):
            @pl.when((c == group % 2) if kept else (c != group % 2))
            def _():
                sent = hidden.at[pl.ds(0, 16 - kept), :, group_cols[group]]
                pltpu.make_async_copy(sent, sent, a_send.at[group]).wait()
    for chunk in range(CHUNKS):
        for width in (256, 128):
            @pl.when((my_group(chunk) == 3) if width == 128 else (my_group(chunk) < 3))
            def _():
                sent = had_out.at[chunk, pl.ds(0, TP - 1), :, pl.ds(0, width)]
                pltpu.make_async_copy(sent, sent, b_send.at[chunk]).wait()


def shards(tokens, gate_codes, gate_scales, up_codes, up_scales, local_factor, down_codes, down_scales):
    vmem, hbm, dma = pl.BlockSpec(memory_space=pltpu.VMEM), pl.BlockSpec(memory_space=pl.ANY), pltpu.SemaphoreType.DMA
    return pl.pallas_call(
        kernel,
        out_shape=jax.ShapeDtypeStruct((ROWS, 128), BF16),
        in_specs=[vmem] * 4 + [hbm] * 4,
        out_specs=vmem,
        scratch_shapes=[
            pltpu.VMEM((1024, UNITS), jnp.int32),
            pltpu.VMEM((1024, UNITS), jnp.int32),
            pltpu.VMEM((224, 4096), jnp.int32),
            pltpu.VMEM((UNITS, UNITS), BF16),
            pltpu.VMEM((4, ROWS, 1024), BF16),
            pltpu.VMEM((4, 1024, 2 * UNITS), BF16),
            pltpu.VMEM((4, UNITS, 1024), BF16),
            pltpu.VMEM((UNITS, UNITS), BF16),
            pltpu.VMEM((32, 8, UNITS), F32),
            pltpu.VMEM((32, 8, UNITS), F32),
            pltpu.VMEM((7, 8, 4096), F32),
            pltpu.VMEM((ROWS, 2 * UNITS), F32),
            pltpu.VMEM((16, 16, UNITS), BF16),
            pltpu.VMEM((2, TP, 16, 256), BF16),
            pltpu.VMEM((2, TP, 16, 256), BF16),
            pltpu.VMEM((16, 16, UNITS), BF16),
            pltpu.VMEM((ROWS, UNITS), BF16),
            pltpu.VMEM((CHUNKS, 2, 4, 4, CR, 128), BF16),
            pltpu.VMEM((CHUNKS, 4, 4, CR, 128), BF16),
            pltpu.VMEM((CHUNKS, 4, 4, CR, 128), BF16),
            pltpu.VMEM((CHUNKS, 2, 4, HALF, 128), BF16),
            pltpu.VMEM((CHUNKS, 2, 4, CR, 128), BF16),
            pltpu.VMEM((CHUNKS, 4, CR, 128), BF16),
            pltpu.VMEM((CHUNKS, 4, CR, 128), BF16),
            dma((34,)),
            dma((48,)),
            dma((TP, 2)),
            dma((4,)),
            dma((CHUNKS,)),
            dma((CHUNKS,)),
            dma((CHUNKS,)),
            dma((CHUNKS, 4)),
            dma((CHUNKS, 4)),
            dma((CHUNKS, 2)),
            dma((CHUNKS, 2)),
            dma((CHUNKS, 2)),
            dma((CHUNKS, 2)),
            dma((CHUNKS, 4)),
            dma((CHUNKS, 4)),
        ],
        compiler_params=pltpu.CompilerParams(
            collective_id=0, has_side_effects=True, vmem_limit_bytes=58 * 1024 * 1024
        ),
        name="feed_forward",
    )(tokens, gate_scales, up_scales, down_scales, gate_codes, up_codes, local_factor, down_codes)


def solution(mesh):
    return jax.shard_map(
        shards,
        mesh=mesh,
        in_specs=(
            P("req", "tp"),
            P(None, "tp"),
            P(None, "tp"),
            P(None, "tp"),
            P(None, "tp"),
            P(),
            P("tp", None),
            P("tp", None),
        ),
        out_specs=P("req", "tp"),
        check_vma=False,
    )
```

```python
import functools
import math

import jax
import jax.numpy as jnp
from jax import lax
from jax.experimental import pallas as pl
from jax.experimental.pallas import tpu as pltpu
from jax.sharding import PartitionSpec as P

MESH = pl.DeviceIdType.MESH
TP = 32
ROWS = 256
UNITS = 896
TILES = 7
CHUNKS = 4
CR = ROWS // CHUNKS
HALF = CR // 2
F32 = jnp.float32
BF16 = jnp.bfloat16


def field_order():
    source = lax.broadcasted_iota(jnp.int32, (128, 128), 0)
    target = lax.broadcasted_iota(jnp.int32, (128, 128), 1)
    return jnp.where(target == (source % 4) * 32 + source // 4, 1.0, 0.0).astype(BF16)


def decode(words, scale):
    flipped = jnp.bitwise_xor(words, 0x0888)
    planes = []
    for field in range(4):
        if field == 3:
            value = jnp.right_shift(words, 12)
        else:
            value = jnp.right_shift(jnp.left_shift(flipped, 28 - 4 * field), 28)
        scaled = value.astype(F32).reshape(4, 8, 128) * scale
        planes.append(scaled.reshape(32, 128).astype(BF16))
    return planes


def kernel(
    tok_in, gate_scales, up_scales, down_scales, gate_hbm, up_hbm, factor_hbm, down_hbm, out_ref,
    gate_codes, up_codes, down_codes, factor, tok, w_both, w_down, ordered, gate_f32, up_f32, down_f32, total,
    hidden, had_in, had_out, rotated, turned, part, core_in, sums, first_in, second_in, mixed, z_in,
    load_sem, tok_send, tok_recv, a_send, a_recv, b_send, b_recv, c_send, c_recv, x_send, x_recv,
    y_send, y_recv, z_send, z_recv,
):
    me = lax.axis_index("tp")
    z, x, c = me // 8, (me // 2) % 4, me % 2
    other = me + 1 - 2 * c
    right = z * 8 + ((x + 1) % 4) * 2 + c
    left = z * 8 + ((x + 3) % 4) * 2 + c
    z_of = [z, z + 1 - 2 * (z % 2), (z + 2) % 4, 3 - z]

    barrier = pltpu.get_barrier_semaphore()

    @pl.loop(1, TP)
    def _(step):
        pl.semaphore_signal(barrier, inc=1, device_id={"tp": (me + step) % TP}, device_id_type=MESH)

    def column(shift):
        return (x + shift) % 4

    def code_rows(shift, z_at):
        return pl.ds(pl.multiple_of((z_at * 4 + column(shift)) * 64, 64), 64)

    loads = {}
    for place, shift in enumerate((0, 1, 3, 2)):
        for z_at in range(4):
            rows = code_rows(shift, z_at)
            first = (place * 4 + z_at) * 2
            loads[shift, z_at] = [
                pltpu.make_async_copy(gate_hbm.at[rows], gate_codes.at[rows], load_sem.at[first]),
                pltpu.make_async_copy(up_hbm.at[rows], up_codes.at[rows], load_sem.at[first + 1]),
            ]
            if not shift:
                for copy in loads[shift, z_at]:
                    copy.start(priority=1)
    factor_load = pltpu.make_async_copy(factor_hbm, factor, load_sem.at[32])
    down_load = pltpu.make_async_copy(down_hbm, down_codes, load_sem.at[33])

    order = field_order()

    def tokens_of(block, row, count):
        lanes = pl.ds(pl.multiple_of((block // 8) * 256 + (block % 2) * 128, 128), 128)
        return tok.at[(block // 2) % 4, pl.ds(row, count), lanes]

    tokens_of(me, 0, ROWS)[...] = jnp.dot(tok_in[...], order, preferred_element_type=F32).astype(BF16)

    def spread_scales(source, spread, groups):
        scales = source[...].astype(F32)
        for group in range(groups):
            spread[group] = jnp.broadcast_to(scales[group : group + 1], spread.shape[1:])

    def decode_piece(shift, z_at):
        for copy in loads[shift, z_at]:
            copy.wait()

        @pl.loop(0, 2)
        def _(side):
            group = (z_at * 4 + column(shift)) * 2 + side
            rows = pl.ds(pl.multiple_of(group * 32, 32), 32)
            for place, codes, scales in ((0, gate_codes, gate_f32), (128, up_codes, up_f32)):
                words = [codes[rows, pl.ds(128 * tile, 128)] for tile in range(TILES)]
                factors = [scales[group, :, pl.ds(128 * tile, 128)] for tile in range(TILES)]
                for tile in range(TILES):
                    for field, plane in enumerate(decode(words[tile], factors[tile])):
                        to = pl.ds(pl.multiple_of(z_at * 256 + side * 128 + 32 * field, 32), 32)
                        w_both[column(shift), to, pl.ds(256 * tile + place, 128)] = plane

    spread_scales(gate_scales, gate_f32, 32)
    spread_scales(up_scales, up_f32, 32)
    decode_piece(0, 0)

    pl.semaphore_wait(barrier, TP - 1)

    waiting = []

    def remote(src, dst, send, recv, device):
        copy = pltpu.make_async_remote_copy(
            src_ref=src, dst_ref=dst, send_sem=send, recv_sem=recv,
            device_id={"tp": device}, device_id_type=MESH,
        )
        copy.start()
        waiting.append(copy)
        return copy

    def pass_on(block, device, row=0, count=ROWS):
        where = tokens_of(block, row, count)
        remote(where, where, tok_send.at[len(waiting)], tok_recv.at[block, 1 if row else 0], device)

    def arrived(block, row=0, count=ROWS):
        where = tokens_of(block, row, count)
        pltpu.make_async_copy(where, where, tok_recv.at[block, 1 if row else 0]).wait()

    def at(near, shift):
        return z_of[near] * 8 + column(shift) * 2 + c

    def from_z(near):
        block = at(near, 0)
        if near:
            arrived(block)
        else:
            for peer in (1, 2, 3):
                pass_on(block, at(peer, 0))
        pass_on(block, right)
        pass_on(block, left)
        pass_on(block, other)

    def from_x(near):
        block = at(near, 3)
        arrived(block)
        pass_on(block, right, 0, ROWS // 2)
        pass_on(block, other)
        block = at(near, 1)
        arrived(block)
        pass_on(block, left, ROWS // 2, ROWS // 2)
        pass_on(block, other)

    def from_far(near):
        block = at(near, 2)
        arrived(block, 0, ROWS // 2)
        arrived(block, ROWS // 2, ROWS // 2)
        pass_on(block, other)

    def from_core(shift):
        for z_at in range(4):
            arrived(z_at * 8 + column(shift) * 2 + 1 - c)

    both_cols = [pl.ds(0, 512), pl.ds(512, 512), pl.ds(1024, 512), pl.ds(1536, 256)]

    def product(shift, group):
        return jnp.dot(tok[column(shift)], w_both[column(shift), :, both_cols[group]], preferred_element_type=F32)

    chip = me // 2
    wide, narrow = pl.ds(0, 256), pl.ds(0, 128)
    group_cols = [pl.ds(0, 256), pl.ds(256, 256), pl.ds(512, 256), pl.ds(768, 128)]
    group_width = [256, 256, 256, 128]

    def scatter(group):
        side, lanes = group % 2, pl.ds(0, group_width[group])

        def give(to_chip):
            pltpu.make_async_remote_copy(
                src_ref=hidden.at[to_chip, :, group_cols[group]], dst_ref=had_in.at[group // 2, me, :, lanes],
                send_sem=a_send.at[group], recv_sem=a_recv.at[group // 2],
                device_id={"tp": to_chip * 2 + side}, device_id_type=MESH,
            ).start()

        @pl.loop(1, 16)
        def _(step):
            give((chip + 1 + (step + 2) % 15) % 16)

        @pl.when(c == side)
        def _():
            pltpu.make_async_copy(
                hidden.at[chip, :, group_cols[group]], had_in.at[group // 2, me, :, lanes], a_recv.at[group // 2]
            ).start()

        @pl.when(c != side)
        def _():
            give(chip)

    def rotate(group):
        turn, lanes = group // 2, pl.ds(0, group_width[group])
        everything = had_in.at[turn, :, :, lanes]
        pltpu.make_async_copy(everything, everything, a_recv.at[turn]).wait()
        for tile in range(group_width[group] // 128):
            cols = pl.ds(128 * tile, 128)
            held = [had_in[turn, source, :, cols].astype(F32) * (1.0 / TP) for source in range(TP)]
            apart = 1
            while apart < TP:
                held = [
                    held[i - apart] - held[i] if i & apart else held[i] + held[i + apart]
                    for i in range(TP)
                ]
                apart *= 2
            for target in range(TP):
                had_out[turn, target, :, cols] = held[target].astype(BF16)

        @pl.loop(1, TP)
        def _(step):
            device = (me + 1 + (step + 6) % (TP - 1)) % TP
            pltpu.make_async_remote_copy(
                src_ref=had_out.at[turn, device, :, lanes], dst_ref=rotated.at[chip, :, group_cols[group]],
                send_sem=b_send.at[turn], recv_sem=b_recv.at[group],
                device_id={"tp": device}, device_id_type=MESH,
            ).start()

        pltpu.make_async_copy(
            had_out.at[turn, me, :, lanes], rotated.at[chip, :, group_cols[group]], b_recv.at[group]
        ).start()

    def rotate_turn(turn):
        for side in range(2):
            @pl.when(c == side)
            def _():
                rotate(2 * turn + side)

    def back(group):
        everything = rotated.at[:, :, group_cols[group]]
        pltpu.make_async_copy(everything, everything, b_recv.at[group]).wait()

    def decode_down(first, stop):
        @pl.loop(first, stop)
        def _(place):
            for side in range(2):
                cols = pl.ds(pl.multiple_of(place * 256 + 128 * side, 128), 128)
                to = pl.ds(pl.multiple_of((place // 4) * 256 + 128 * side, 128), 128)
                words = [down_codes[pl.ds(32 * group, 32), cols] for group in range(TILES)]
                factors = [down_f32[group, :, cols] for group in range(TILES)]
                for group in range(TILES):
                    for field, plane in enumerate(decode(words[group], factors[group])):
                        w_down[place % 4, pl.ds(128 * group + 32 * field, 32), to] = plane

    from_other = {}

    def down(shift):
        place = column(shift)
        for pair in range(2):
            both = jnp.dot(
                turned[...], w_down[place, :, pl.ds(512 * pair, 512)], preferred_element_type=F32
            ).astype(BF16)
            for chunk in range(CHUNKS):
                rows = slice(chunk * CR, (chunk + 1) * CR)
                for z_at in range(2):
                    for side in range(2):
                        lanes = slice(256 * z_at + 128 * side, 256 * z_at + 128 * side + 128)
                        part[chunk, side, place, 2 * pair + z_at] = both[rows, lanes]
        for chunk in range(CHUNKS):
            from_other[chunk, shift] = remote(
                part.at[chunk, 1 - c, place], core_in.at[chunk, shift],
                c_send.at[chunk, shift], c_recv.at[chunk, shift], other,
            )

    top, bottom = pl.ds(0, HALF), pl.ds(HALF, HALF)

    def join(chunk, shift, rows):
        return part[chunk, c, column(shift), :, rows].astype(F32) + core_in[chunk, shift, :, rows].astype(F32)

    x_copies = {}

    def x_first(chunk):
        from_other[chunk, 2].wait_recv()
        sums[chunk, 2] = join(chunk, 2, pl.ds(0, CR)).astype(BF16)
        x_copies[chunk, "r1"] = remote(
            sums.at[chunk, 2, :, top], first_in.at[chunk, 0], x_send.at[chunk, 0], x_recv.at[chunk, 0], right
        )
        x_copies[chunk, "l1"] = remote(
            sums.at[chunk, 2, :, bottom], first_in.at[chunk, 1], x_send.at[chunk, 1], x_recv.at[chunk, 1], left
        )

    def x_second(chunk):
        from_other[chunk, 1].wait_recv()
        sums[chunk, 1, :, bottom] = join(chunk, 1, bottom).astype(BF16)
        x_copies[chunk, "r1"].wait_recv()
        sums[chunk, 1, :, top] = (join(chunk, 1, top) + first_in[chunk, 0].astype(F32)).astype(BF16)
        x_copies[chunk, "r2"] = remote(
            sums.at[chunk, 1], second_in.at[chunk, 0], y_send.at[chunk, 0], y_recv.at[chunk, 0], right
        )
        from_other[chunk, 3].wait_recv()
        sums[chunk, 3, :, top] = join(chunk, 3, top).astype(BF16)
        x_copies[chunk, "l1"].wait_recv()
        sums[chunk, 3, :, bottom] = (join(chunk, 3, bottom) + first_in[chunk, 1].astype(F32)).astype(BF16)
        x_copies[chunk, "l2"] = remote(
            sums.at[chunk, 3], second_in.at[chunk, 1], y_send.at[chunk, 1], y_recv.at[chunk, 1], left
        )

    z_copies = {}

    def z_first(chunk):
        from_other[chunk, 0].wait_recv()
        x_copies[chunk, "r2"].wait_recv()
        x_copies[chunk, "l2"].wait_recv()
        for near in (3, 2, 1, 0):
            to = z_of[near]
            value = (
                part[chunk, c, x, to].astype(F32) + core_in[chunk, 0, to].astype(F32)
                + second_in[chunk, 0, to].astype(F32) + second_in[chunk, 1, to].astype(F32)
            )
            mixed[chunk, near] = value.astype(BF16)
            if near:
                z_copies[chunk, near] = remote(
                    mixed.at[chunk, near], z_in.at[chunk, near], z_send.at[chunk, near], z_recv.at[chunk, near],
                    to * 8 + x * 2 + c,
                )

    def z_last(chunk):
        total = mixed[chunk, 0].astype(F32)
        for near in (1, 2, 3):
            z_copies[chunk, near].wait_recv()
            total = total + z_in[chunk, near].astype(F32)
        out_ref[pl.ds(chunk * CR, CR), :] = total.astype(BF16)

    from_z(0)
    for shift in (1, 3, 2):
        for z_at in range(4):
            for copy in loads[shift, z_at]:
                copy.start(priority=1)
    factor_load.start(priority=1)
    down_load.start(priority=1)
    for z_at in range(1, 4):
        decode_piece(0, z_at)
    from_z(1)
    from_x(0)
    decode_piece(1, 0)
    decode_piece(1, 1)
    from_z(2)
    from_x(1)
    decode_piece(1, 2)
    decode_piece(1, 3)
    from_z(3)
    from_x(2)
    from_far(0)
    decode_piece(3, 0)
    decode_piece(3, 1)
    from_far(1)
    from_x(3)
    decode_piece(3, 2)
    decode_piece(3, 3)
    from_far(2)
    from_core(0)

    for group in range(4):
        total[:, both_cols[group]] = product(0, group)

    for z_at in range(4):
        decode_piece(2, z_at)
    from_core(1)
    for group in range(4):
        total[:, both_cols[group]] += product(1, group)
    from_far(3)
    from_core(3)
    for group in range(4):
        total[:, both_cols[group]] += product(3, group)
    from_core(2)
    for group in range(4):
        both = total[:, both_cols[group]] + product(2, group)
        for tile in range(2 * group, min(2 * group + 2, TILES)):
            start = 256 * (tile - 2 * group)
            gate, up = both[:, start : start + 128], both[:, start + 128 : start + 256]
            value = gate / (1.0 + jnp.exp(-gate)) * up
            hidden[:, :, pl.ds(128 * tile, 128)] = value.astype(BF16).reshape(16, 16, 128)

        scatter(group)

    factor_load.wait()
    for tile in range(TILES):
        cols = pl.ds(128 * tile, 128)
        ordered[:, cols] = jnp.dot(factor[:, cols], order, preferred_element_type=F32).astype(BF16)
    spread_scales(down_scales, down_f32, 7)
    down_load.wait()
    decode_down(0, 8)
    rotate_turn(0)
    decode_down(8, 16)
    rotate_turn(1)
    back(0)
    back(1)
    first_part = jnp.dot(
        rotated[:, :, pl.ds(0, 512)].reshape(ROWS, 512), ordered[pl.ds(0, 512), :], preferred_element_type=F32
    )
    back(2)
    back(3)
    whole = first_part + jnp.dot(
        rotated[:, :, pl.ds(512, 384)].reshape(ROWS, 384), ordered[pl.ds(512, 384), :], preferred_element_type=F32
    )
    turned[...] = (whole * math.sqrt(TP)).astype(BF16)
    down(2)
    down(1)
    for chunk in range(CHUNKS):
        x_first(chunk)
    down(3)
    down(0)
    for chunk in range(CHUNKS):
        x_second(chunk)
    for chunk in range(CHUNKS):
        z_first(chunk)
    for chunk in range(CHUNKS):
        z_last(chunk)

    for copy in waiting:
        copy.wait_send()
    for group in range(4):
        for kept in range(2):
            @pl.when((c == group % 2) if kept else (c != group % 2))
            def _():
                sent = hidden.at[pl.ds(0, 16 - kept), :, group_cols[group]]
                pltpu.make_async_copy(sent, sent, a_send.at[group]).wait()
                if kept:
                    sent = had_out.at[group // 2, pl.ds(0, TP - 1), :, pl.ds(0, group_width[group])]
                    pltpu.make_async_copy(sent, sent, b_send.at[group // 2]).wait()


def shards(tokens, gate_codes, gate_scales, up_codes, up_scales, local_factor, down_codes, down_scales):
    vmem, hbm, dma = pl.BlockSpec(memory_space=pltpu.VMEM), pl.BlockSpec(memory_space=pl.ANY), pltpu.SemaphoreType.DMA
    return pl.pallas_call(
        kernel,
        out_shape=jax.ShapeDtypeStruct((ROWS, 128), BF16),
        in_specs=[vmem] * 4 + [hbm] * 4,
        out_specs=vmem,
        scratch_shapes=[
            pltpu.VMEM((1024, UNITS), jnp.int32),
            pltpu.VMEM((1024, UNITS), jnp.int32),
            pltpu.VMEM((224, 4096), jnp.int32),
            pltpu.VMEM((UNITS, UNITS), BF16),
            pltpu.VMEM((4, ROWS, 1024), BF16),
            pltpu.VMEM((4, 1024, 2 * UNITS), BF16),
            pltpu.VMEM((4, UNITS, 1024), BF16),
            pltpu.VMEM((UNITS, UNITS), BF16),
            pltpu.VMEM((32, 8, UNITS), F32),
            pltpu.VMEM((32, 8, UNITS), F32),
            pltpu.VMEM((7, 8, 4096), F32),
            pltpu.VMEM((ROWS, 2 * UNITS), F32),
            pltpu.VMEM((16, 16, UNITS), BF16),
            pltpu.VMEM((2, TP, 16, 256), BF16),
            pltpu.VMEM((2, TP, 16, 256), BF16),
            pltpu.VMEM((16, 16, UNITS), BF16),
            pltpu.VMEM((ROWS, UNITS), BF16),
            pltpu.VMEM((CHUNKS, 2, 4, 4, CR, 128), BF16),
            pltpu.VMEM((CHUNKS, 4, 4, CR, 128), BF16),
            pltpu.VMEM((CHUNKS, 4, 4, CR, 128), BF16),
            pltpu.VMEM((CHUNKS, 2, 4, HALF, 128), BF16),
            pltpu.VMEM((CHUNKS, 2, 4, CR, 128), BF16),
            pltpu.VMEM((CHUNKS, 4, CR, 128), BF16),
            pltpu.VMEM((CHUNKS, 4, CR, 128), BF16),
            dma((34,)),
            dma((48,)),
            dma((TP, 2)),
            dma((4,)),
            dma((2,)),
            dma((2,)),
            dma((4,)),
            dma((CHUNKS, 4)),
            dma((CHUNKS, 4)),
            dma((CHUNKS, 2)),
            dma((CHUNKS, 2)),
            dma((CHUNKS, 2)),
            dma((CHUNKS, 2)),
            dma((CHUNKS, 4)),
            dma((CHUNKS, 4)),
        ],
        compiler_params=pltpu.CompilerParams(
            collective_id=0, has_side_effects=True, vmem_limit_bytes=58 * 1024 * 1024
        ),
        name="feed_forward",
    )(tokens, gate_scales, up_scales, down_scales, gate_codes, up_codes, local_factor, down_codes)


def solution(mesh):
    return jax.shard_map(
        shards,
        mesh=mesh,
        in_specs=(
            P("req", "tp"),
            P(None, "tp"),
            P(None, "tp"),
            P(None, "tp"),
            P(None, "tp"),
            P(),
            P("tp", None),
            P("tp", None),
        ),
        out_specs=P("req", "tp"),
        check_vma=False,
    )
```

```python
import functools
import math

import jax
import jax.numpy as jnp
from jax import lax
from jax.experimental import pallas as pl
from jax.experimental.pallas import tpu as pltpu
from jax.sharding import PartitionSpec as P

MESH = pl.DeviceIdType.MESH
TP = 32
ROWS = 256
UNITS = 896
TILES = 7
CHUNKS = 4
CR = ROWS // CHUNKS
HALF = CR // 2
F32 = jnp.float32
BF16 = jnp.bfloat16


def field_order():
    source = lax.broadcasted_iota(jnp.int32, (128, 128), 0)
    target = lax.broadcasted_iota(jnp.int32, (128, 128), 1)
    return jnp.where(target == (source % 4) * 32 + source // 4, 1.0, 0.0).astype(BF16)


def decode(words, scale):
    flipped = jnp.bitwise_xor(words, 0x0888)
    planes = []
    for field in range(4):
        if field == 3:
            value = jnp.right_shift(words, 12)
        else:
            value = jnp.right_shift(jnp.left_shift(flipped, 28 - 4 * field), 28)
        scaled = value.astype(F32).reshape(4, 8, 128) * scale
        planes.append(scaled.reshape(32, 128).astype(BF16))
    return planes


def kernel(
    tok_in, gate_scales, up_scales, down_scales, gate_hbm, up_hbm, factor_hbm, down_hbm, out_ref,
    gate_codes, up_codes, down_codes, factor, tok, w_both, w_down, ordered, gate_f32, up_f32, down_f32, total,
    hidden, had_in, had_out, rotated, turned, part, core_in, sums, first_in, second_in, mixed, z_in,
    load_sem, tok_send, tok_recv, a_send, a_recv, b_send, b_recv, c_send, c_recv, x_send, x_recv,
    y_send, y_recv, z_send, z_recv,
):
    me = lax.axis_index("tp")
    z, x, c = me // 8, (me // 2) % 4, me % 2
    other = me + 1 - 2 * c
    right = z * 8 + ((x + 1) % 4) * 2 + c
    left = z * 8 + ((x + 3) % 4) * 2 + c
    z_of = [z, z + 1 - 2 * (z % 2), (z + 2) % 4, 3 - z]

    barrier = pltpu.get_barrier_semaphore()

    @pl.loop(1, TP)
    def _(step):
        pl.semaphore_signal(barrier, inc=1, device_id={"tp": (me + step) % TP}, device_id_type=MESH)

    def column(shift):
        return (x + shift) % 4

    def code_rows(shift, z_at):
        return pl.ds(pl.multiple_of((z_at * 4 + column(shift)) * 64, 64), 64)

    loads = {}
    for place, shift in enumerate((0, 1, 3, 2)):
        for z_at in range(4):
            rows = code_rows(shift, z_at)
            first = (place * 4 + z_at) * 2
            loads[shift, z_at] = [
                pltpu.make_async_copy(gate_hbm.at[rows], gate_codes.at[rows], load_sem.at[first]),
                pltpu.make_async_copy(up_hbm.at[rows], up_codes.at[rows], load_sem.at[first + 1]),
            ]
            if not shift:
                for copy in loads[shift, z_at]:
                    copy.start(priority=1)
    factor_load = pltpu.make_async_copy(factor_hbm, factor, load_sem.at[32])
    down_load = pltpu.make_async_copy(down_hbm, down_codes, load_sem.at[33])

    order = field_order()

    def tokens_of(block, row, count):
        lanes = pl.ds(pl.multiple_of((block // 8) * 256 + (block % 2) * 128, 128), 128)
        return tok.at[(block // 2) % 4, pl.ds(row, count), lanes]

    tokens_of(me, 0, ROWS)[...] = jnp.dot(tok_in[...], order, preferred_element_type=F32).astype(BF16)

    def spread_scales(source, spread, groups):
        scales = source[...].astype(F32)
        for group in range(groups):
            spread[group] = jnp.broadcast_to(scales[group : group + 1], spread.shape[1:])

    def decode_piece(shift, z_at):
        for copy in loads[shift, z_at]:
            copy.wait()

        @pl.loop(0, 2)
        def _(side):
            group = (z_at * 4 + column(shift)) * 2 + side
            rows = pl.ds(pl.multiple_of(group * 32, 32), 32)
            for place, codes, scales in ((0, gate_codes, gate_f32), (128, up_codes, up_f32)):
                words = [codes[rows, pl.ds(128 * tile, 128)] for tile in range(TILES)]
                factors = [scales[group, :, pl.ds(128 * tile, 128)] for tile in range(TILES)]
                for tile in range(TILES):
                    for field, plane in enumerate(decode(words[tile], factors[tile])):
                        to = pl.ds(pl.multiple_of(z_at * 256 + side * 128 + 32 * field, 32), 32)
                        w_both[column(shift), to, pl.ds(256 * tile + place, 128)] = plane

    spread_scales(gate_scales, gate_f32, 32)
    spread_scales(up_scales, up_f32, 32)
    decode_piece(0, 0)

    pl.semaphore_wait(barrier, TP - 1)

    waiting = []

    def remote(src, dst, send, recv, device):
        copy = pltpu.make_async_remote_copy(
            src_ref=src, dst_ref=dst, send_sem=send, recv_sem=recv,
            device_id={"tp": device}, device_id_type=MESH,
        )
        copy.start()
        waiting.append(copy)
        return copy

    def pass_on(block, device, row=0, count=ROWS):
        where = tokens_of(block, row, count)
        remote(where, where, tok_send.at[len(waiting)], tok_recv.at[block, 1 if row else 0], device)

    def arrived(block, row=0, count=ROWS):
        where = tokens_of(block, row, count)
        pltpu.make_async_copy(where, where, tok_recv.at[block, 1 if row else 0]).wait()

    def at(near, shift):
        return z_of[near] * 8 + column(shift) * 2 + c

    def from_z(near):
        block = at(near, 0)
        if near:
            arrived(block)
        else:
            for peer in (1, 2, 3):
                pass_on(block, at(peer, 0))
        pass_on(block, right)
        pass_on(block, left)
        pass_on(block, other)

    def from_x(near):
        before, after = at(near, 3), at(near, 1)
        arrived(before)
        pass_on(before, right, 0, ROWS // 2)
        arrived(after)
        pass_on(after, left, ROWS // 2, ROWS // 2)
        pass_on(before, other)
        pass_on(after, other)

    def from_far(near):
        block = at(near, 2)
        arrived(block, 0, ROWS // 2)
        arrived(block, ROWS // 2, ROWS // 2)
        pass_on(block, other)

    def from_core(shift):
        for z_at in range(4):
            arrived(z_at * 8 + column(shift) * 2 + 1 - c)

    both_cols = [pl.ds(0, 512), pl.ds(512, 512), pl.ds(1024, 512), pl.ds(1536, 256)]

    def product(shift, group):
        return jnp.dot(tok[column(shift)], w_both[column(shift), :, both_cols[group]], preferred_element_type=F32)

    chip = me // 2
    wide, narrow = pl.ds(0, 256), pl.ds(0, 128)
    group_cols = [pl.ds(0, 256), pl.ds(256, 256), pl.ds(512, 256), pl.ds(768, 128)]
    group_width = [256, 256, 256, 128]

    def scatter(group):
        side, lanes = group % 2, pl.ds(0, group_width[group])

        def give(to_chip):
            pltpu.make_async_remote_copy(
                src_ref=hidden.at[to_chip, :, group_cols[group]], dst_ref=had_in.at[group // 2, me, :, lanes],
                send_sem=a_send.at[group], recv_sem=a_recv.at[group // 2],
                device_id={"tp": to_chip * 2 + side}, device_id_type=MESH,
            ).start()

        @pl.loop(1, 16)
        def _(step):
            give((chip + 1 + (step + 2) % 15) % 16)

        @pl.when(c == side)
        def _():
            pltpu.make_async_copy(
                hidden.at[chip, :, group_cols[group]], had_in.at[group // 2, me, :, lanes], a_recv.at[group // 2]
            ).start()

        @pl.when(c != side)
        def _():
            give(chip)

    def rotate(group):
        turn, lanes = group // 2, pl.ds(0, group_width[group])
        everything = had_in.at[turn, :, :, lanes]
        pltpu.make_async_copy(everything, everything, a_recv.at[turn]).wait()
        for tile in range(group_width[group] // 128):
            cols = pl.ds(128 * tile, 128)
            held = [had_in[turn, source, :, cols].astype(F32) * (1.0 / TP) for source in range(TP)]
            apart = 1
            while apart < TP:
                held = [
                    held[i - apart] - held[i] if i & apart else held[i] + held[i + apart]
                    for i in range(TP)
                ]
                apart *= 2
            for target in range(TP):
                had_out[turn, target, :, cols] = held[target].astype(BF16)

        @pl.loop(1, TP)
        def _(step):
            device = (me + 1 + (step + 6) % (TP - 1)) % TP
            pltpu.make_async_remote_copy(
                src_ref=had_out.at[turn, device, :, lanes], dst_ref=rotated.at[chip, :, group_cols[group]],
                send_sem=b_send.at[turn], recv_sem=b_recv.at[group],
                device_id={"tp": device}, device_id_type=MESH,
            ).start()

        pltpu.make_async_copy(
            had_out.at[turn, me, :, lanes], rotated.at[chip, :, group_cols[group]], b_recv.at[group]
        ).start()

    def rotate_turn(turn):
        for side in range(2):
            @pl.when(c == side)
            def _():
                rotate(2 * turn + side)

    def back(group):
        everything = rotated.at[:, :, group_cols[group]]
        pltpu.make_async_copy(everything, everything, b_recv.at[group]).wait()

    def decode_down(first, stop):
        @pl.loop(first, stop)
        def _(place):
            for side in range(2):
                cols = pl.ds(pl.multiple_of(place * 256 + 128 * side, 128), 128)
                to = pl.ds(pl.multiple_of((place // 4) * 256 + 128 * side, 128), 128)
                words = [down_codes[pl.ds(32 * group, 32), cols] for group in range(TILES)]
                factors = [down_f32[group, :, cols] for group in range(TILES)]
                for group in range(TILES):
                    for field, plane in enumerate(decode(words[group], factors[group])):
                        w_down[place % 4, pl.ds(128 * group + 32 * field, 32), to] = plane

    from_other = {}

    def down(shift):
        place = column(shift)
        for pair in range(2):
            both = jnp.dot(
                turned[...], w_down[place, :, pl.ds(512 * pair, 512)], preferred_element_type=F32
            ).astype(BF16)
            for chunk in range(CHUNKS):
                rows = slice(chunk * CR, (chunk + 1) * CR)
                for z_at in range(2):
                    for side in range(2):
                        lanes = slice(256 * z_at + 128 * side, 256 * z_at + 128 * side + 128)
                        part[chunk, side, place, 2 * pair + z_at] = both[rows, lanes]
        for chunk in range(CHUNKS):
            from_other[chunk, shift] = remote(
                part.at[chunk, 1 - c, place], core_in.at[chunk, shift],
                c_send.at[chunk, shift], c_recv.at[chunk, shift], other,
            )

    top, bottom = pl.ds(0, HALF), pl.ds(HALF, HALF)

    def join(chunk, shift, rows):
        return part[chunk, c, column(shift), :, rows].astype(F32) + core_in[chunk, shift, :, rows].astype(F32)

    x_copies = {}

    def x_first(chunk):
        from_other[chunk, 2].wait_recv()
        sums[chunk, 2] = join(chunk, 2, pl.ds(0, CR)).astype(BF16)
        x_copies[chunk, "r1"] = remote(
            sums.at[chunk, 2, :, top], first_in.at[chunk, 0], x_send.at[chunk, 0], x_recv.at[chunk, 0], right
        )
        x_copies[chunk, "l1"] = remote(
            sums.at[chunk, 2, :, bottom], first_in.at[chunk, 1], x_send.at[chunk, 1], x_recv.at[chunk, 1], left
        )

    def x_second(chunk):
        from_other[chunk, 1].wait_recv()
        sums[chunk, 1, :, bottom] = join(chunk, 1, bottom).astype(BF16)
        x_copies[chunk, "r1"].wait_recv()
        sums[chunk, 1, :, top] = (join(chunk, 1, top) + first_in[chunk, 0].astype(F32)).astype(BF16)
        x_copies[chunk, "r2"] = remote(
            sums.at[chunk, 1], second_in.at[chunk, 0], y_send.at[chunk, 0], y_recv.at[chunk, 0], right
        )
        from_other[chunk, 3].wait_recv()
        sums[chunk, 3, :, top] = join(chunk, 3, top).astype(BF16)
        x_copies[chunk, "l1"].wait_recv()
        sums[chunk, 3, :, bottom] = (join(chunk, 3, bottom) + first_in[chunk, 1].astype(F32)).astype(BF16)
        x_copies[chunk, "l2"] = remote(
            sums.at[chunk, 3], second_in.at[chunk, 1], y_send.at[chunk, 1], y_recv.at[chunk, 1], left
        )

    z_copies = {}

    def z_first(chunk):
        from_other[chunk, 0].wait_recv()
        x_copies[chunk, "r2"].wait_recv()
        x_copies[chunk, "l2"].wait_recv()
        for near in (3, 2, 1, 0):
            to = z_of[near]
            value = (
                part[chunk, c, x, to].astype(F32) + core_in[chunk, 0, to].astype(F32)
                + second_in[chunk, 0, to].astype(F32) + second_in[chunk, 1, to].astype(F32)
            )
            mixed[chunk, near] = value.astype(BF16)
            if near:
                z_copies[chunk, near] = remote(
                    mixed.at[chunk, near], z_in.at[chunk, near], z_send.at[chunk, near], z_recv.at[chunk, near],
                    to * 8 + x * 2 + c,
                )

    def z_last(chunk):
        total = mixed[chunk, 0].astype(F32)
        for near in (1, 2, 3):
            z_copies[chunk, near].wait_recv()
            total = total + z_in[chunk, near].astype(F32)
        out_ref[pl.ds(chunk * CR, CR), :] = total.astype(BF16)

    from_z(0)
    for shift in (1, 3, 2):
        for z_at in range(4):
            for copy in loads[shift, z_at]:
                copy.start(priority=1)
    factor_load.start(priority=1)
    down_load.start(priority=1)
    for z_at in range(1, 4):
        decode_piece(0, z_at)
    from_z(1)
    from_x(0)
    decode_piece(1, 0)
    decode_piece(1, 1)
    from_z(2)
    from_x(1)
    decode_piece(1, 2)
    decode_piece(1, 3)
    from_z(3)
    from_x(2)
    from_far(0)
    decode_piece(3, 0)
    decode_piece(3, 1)
    from_far(1)
    from_x(3)
    decode_piece(3, 2)
    decode_piece(3, 3)
    from_far(2)
    from_core(0)

    for group in range(4):
        total[:, both_cols[group]] = product(0, group)

    for z_at in range(4):
        decode_piece(2, z_at)
    from_core(1)
    for group in range(4):
        total[:, both_cols[group]] += product(1, group)
    from_far(3)
    from_core(3)
    for group in range(4):
        total[:, both_cols[group]] += product(3, group)
    from_core(2)
    for group in range(4):
        both = total[:, both_cols[group]] + product(2, group)
        for tile in range(2 * group, min(2 * group + 2, TILES)):
            start = 256 * (tile - 2 * group)
            gate, up = both[:, start : start + 128], both[:, start + 128 : start + 256]
            value = gate / (1.0 + jnp.exp(-gate)) * up
            hidden[:, :, pl.ds(128 * tile, 128)] = value.astype(BF16).reshape(16, 16, 128)

        scatter(group)

    factor_load.wait()
    for tile in range(TILES):
        cols = pl.ds(128 * tile, 128)
        ordered[:, cols] = jnp.dot(factor[:, cols], order, preferred_element_type=F32).astype(BF16)
    spread_scales(down_scales, down_f32, 7)
    down_load.wait()
    decode_down(0, 8)
    rotate_turn(0)
    decode_down(8, 16)
    rotate_turn(1)
    back(0)
    back(1)
    first_part = jnp.dot(
        rotated[:, :, pl.ds(0, 512)].reshape(ROWS, 512), ordered[pl.ds(0, 512), :], preferred_element_type=F32
    )
    back(2)
    back(3)
    whole = first_part + jnp.dot(
        rotated[:, :, pl.ds(512, 384)].reshape(ROWS, 384), ordered[pl.ds(512, 384), :], preferred_element_type=F32
    )
    turned[...] = (whole * math.sqrt(TP)).astype(BF16)
    down(2)
    for chunk in range(CHUNKS):
        x_first(chunk)
    down(1)
    down(3)
    down(0)
    for chunk in range(CHUNKS):
        x_second(chunk)
    for chunk in range(CHUNKS):
        z_first(chunk)
    for chunk in range(CHUNKS):
        z_last(chunk)

    for copy in waiting:
        copy.wait_send()
    for group in range(4):
        for kept in range(2):
            @pl.when((c == group % 2) if kept else (c != group % 2))
            def _():
                sent = hidden.at[pl.ds(0, 16 - kept), :, group_cols[group]]
                pltpu.make_async_copy(sent, sent, a_send.at[group]).wait()
                if kept:
                    sent = had_out.at[group // 2, pl.ds(0, TP - 1), :, pl.ds(0, group_width[group])]
                    pltpu.make_async_copy(sent, sent, b_send.at[group // 2]).wait()


def shards(tokens, gate_codes, gate_scales, up_codes, up_scales, local_factor, down_codes, down_scales):
    vmem, hbm, dma = pl.BlockSpec(memory_space=pltpu.VMEM), pl.BlockSpec(memory_space=pl.ANY), pltpu.SemaphoreType.DMA
    return pl.pallas_call(
        kernel,
        out_shape=jax.ShapeDtypeStruct((ROWS, 128), BF16),
        in_specs=[vmem] * 4 + [hbm] * 4,
        out_specs=vmem,
        scratch_shapes=[
            pltpu.VMEM((1024, UNITS), jnp.int32),
            pltpu.VMEM((1024, UNITS), jnp.int32),
            pltpu.VMEM((224, 4096), jnp.int32),
            pltpu.VMEM((UNITS, UNITS), BF16),
            pltpu.VMEM((4, ROWS, 1024), BF16),
            pltpu.VMEM((4, 1024, 2 * UNITS), BF16),
            pltpu.VMEM((4, UNITS, 1024), BF16),
            pltpu.VMEM((UNITS, UNITS), BF16),
            pltpu.VMEM((32, 8, UNITS), F32),
            pltpu.VMEM((32, 8, UNITS), F32),
            pltpu.VMEM((7, 8, 4096), F32),
            pltpu.VMEM((ROWS, 2 * UNITS), F32),
            pltpu.VMEM((16, 16, UNITS), BF16),
            pltpu.VMEM((2, TP, 16, 256), BF16),
            pltpu.VMEM((2, TP, 16, 256), BF16),
            pltpu.VMEM((16, 16, UNITS), BF16),
            pltpu.VMEM((ROWS, UNITS), BF16),
            pltpu.VMEM((CHUNKS, 2, 4, 4, CR, 128), BF16),
            pltpu.VMEM((CHUNKS, 4, 4, CR, 128), BF16),
            pltpu.VMEM((CHUNKS, 4, 4, CR, 128), BF16),
            pltpu.VMEM((CHUNKS, 2, 4, HALF, 128), BF16),
            pltpu.VMEM((CHUNKS, 2, 4, CR, 128), BF16),
            pltpu.VMEM((CHUNKS, 4, CR, 128), BF16),
            pltpu.VMEM((CHUNKS, 4, CR, 128), BF16),
            dma((34,)),
            dma((48,)),
            dma((TP, 2)),
            dma((4,)),
            dma((2,)),
            dma((2,)),
            dma((4,)),
            dma((CHUNKS, 4)),
            dma((CHUNKS, 4)),
            dma((CHUNKS, 2)),
            dma((CHUNKS, 2)),
            dma((CHUNKS, 2)),
            dma((CHUNKS, 2)),
            dma((CHUNKS, 4)),
            dma((CHUNKS, 4)),
        ],
        compiler_params=pltpu.CompilerParams(
            collective_id=0, has_side_effects=True, vmem_limit_bytes=58 * 1024 * 1024
        ),
        name="feed_forward",
    )(tokens, gate_scales, up_scales, down_scales, gate_codes, up_codes, local_factor, down_codes)


def solution(mesh):
    return jax.shard_map(
        shards,
        mesh=mesh,
        in_specs=(
            P("req", "tp"),
            P(None, "tp"),
            P(None, "tp"),
            P(None, "tp"),
            P(None, "tp"),
            P(),
            P("tp", None),
            P("tp", None),
        ),
        out_specs=P("req", "tp"),
        check_vma=False,
    )
```
